128 devices in a mesh: gx: 16 (over x, z), gy: 8 (over y, core).
Axes of the slice: x: 4, y: 4, z: 4, core: 2. Of those that a mesh axis runs over, the one named last changes fastest.
Arguments:
- particle_pos: float32 [3, 2097152], P(None, ('gx', 'gy')), may hold values from 0 to 16
- tile_dest: int32 [16384, 1], P(('gx', 'gy')), may hold values from 0 to 127; in each aligned block of 128 rows (0 to 127, 128 to 255, ...) at most 2 rows name the same one
- tile_block: int32 [16384], P(('gx', 'gy')), may hold values from 0 to 127
- fluid_flag: int32 [512, 512, 256], P('gx', 'gy'), may hold values 0 or 1
- divergence: float32 [512, 512, 256], P('gx', 'gy'), may hold values from -6 to 6
Outputs:
- level_set: float32 [512, 512, 256], P('gx', 'gy')
- pressure: float32 [512, 512, 256], P('gx', 'gy')
The draws below stay inside these ranges and needn't reach their ends.
Inputs may be any that keep to these rules, and one draw needn't show every extreme that they name: `tile_dest`: among the tiles of one device, no brick is named more than 2 times, a bound that some block reaches.
All inputs are finite; a program needn't handle non-finite values. No bound on the sum of `fluid_flag` on one device may be relied on, other than what follows from the above.
Results may differ from the reference program's by a relative error of at most 0.00002.
Values sent between devices are 32-bit elements; how exact they have to be, the bound alone decides.
No kernel may reach another device: no remote copies, remote signals or barrier semaphores. Data moves between devices by JAX's collectives and lax.ppermute only.
A program may use at most 128 MiB of HBM per device.

```python
import math
import jax
import jax.numpy as jnp
import numpy as np
from jax import lax

BLOCK = 16
TILE = 128
ITERS = 4
CX = 32
CY = 64
NZ = 256
TILES_DEV = 128
BRICKS = 128
CAP = 2
TILES = 16384
PARTICLES = 2097152
NX = 512
NY = 512
BLOCKS_DEV = 128
N_GX = 16
N_GY = 8


def touch_ends(entries, key, least, top_value):
    longest = entries.shape.index(max(entries.shape))
    spots = []
    for shift in (0, 1):
        where = [jax.random.randint(jax.random.fold_in(key, axis), (), 0, length) for axis, length in enumerate(entries.shape)]
        where[longest] = (where[longest] + shift) % entries.shape[longest]
        spots.append(tuple(where))
    return entries.at[spots[0]].set(least).at[spots[1]].set(top_value)


def block_levels(stream_key, shape, cuts, low, high):
    factor_of, own = 1.0, jax.random.fold_in(stream_key, 6)
    for axis_at, parts in cuts:
        draws = jnp.exp(jax.random.uniform(jax.random.fold_in(own, axis_at), (parts,), jnp.float32, low / len(cuts), high / len(cuts)))
        factor_of = factor_of * jnp.repeat(draws, shape[axis_at] // parts).reshape([-1 if axis == axis_at else 1 for axis in range(len(shape))])
    return factor_of


def deal_out(own_key, own, number, rows, number_of, top, reach, skew):
    sequence = jax.random.permutation(own_key, number_of)
    packed, ordinary = load_shares(number_of, rows * top, reach, skew, True), load_shares(number_of, rows * top, reach, skew, False)
    places = jnp.arange(number_of)

    def named(tallies, turn):
        used = int((tallies > 0).sum())
        fixed = max(1, used // 4)
        passed = fixed + (places - fixed + turn * (used - fixed)) % max(1, number_of - fixed)
        return jnp.zeros((number_of,), jnp.int32).at[sequence[jnp.where(places < fixed, places, passed)]].set(jnp.asarray(tallies, jnp.int32))

    tallies = jnp.where(number % 4 == 0, named(packed, number // 4), named(ordinary, number - number // 4 - 1))
    mixed = jax.random.permutation(jax.random.fold_in(own, 3), number_of)
    donor, receiver = mixed[0:number_of // 2 * 2:2], mixed[1:number_of // 2 * 2:2]
    slack = jnp.minimum(tallies[donor] - 1, reach - tallies[receiver]) // 2
    slack = jnp.where((donor == sequence[0]) | (receiver == sequence[0]) | (tallies[receiver] == 0), 0, jnp.maximum(slack, 0))
    passed = jax.random.randint(jax.random.fold_in(own, 4), (number_of // 2,), 0, 1 << 20) % (slack + 1)
    tallies = tallies.at[donor].add(-passed).at[receiver].add(passed)
    members = jnp.searchsorted(jnp.cumsum(tallies), jnp.arange(rows * top), side="right").astype(jnp.int32)
    table = members.reshape(top, rows).T
    table = table[jax.random.permutation(jax.random.fold_in(own, 1), rows)]
    turn = jax.random.randint(jax.random.fold_in(own, 2), (rows, 1), 0, top)
    return jnp.take_along_axis(table, (jnp.arange(top)[None, :] + turn) % top, axis=1)


def load_shares(number_of, total, reach, lean, full):
    weights = [(1 << 20) // math.isqrt(grade ** lean) + 1 for grade in range(1, number_of + 1)]
    largest = reach if full else min(reach, max(-(-total // number_of), total * weights[0] // sum(weights)))
    least = 1 if total - largest >= number_of - 1 else 0
    given, spare = [largest] + [least] * (number_of - 1), total - largest - least * (number_of - 1)
    while spare > 0:
        movable = [i for i in range(1, number_of) if given[i] < largest] or [i for i in range(1, number_of) if given[i] < reach]
        mass, remaining = sum([weights[i] for i in movable]), spare
        for i in movable:
            more = min(reach - given[i], max(1, remaining * weights[i] // mass), spare)
            given[i] = given[i] + more
            spare = spare - more
    return np.array(given)


def normal_values(own_key, dims, spread, bound, cuts=(), held_as=jnp.bfloat16):
    array = spread * jax.random.normal(own_key, dims, jnp.float32)
    if cuts:
        array = array * block_levels(own_key, dims, cuts, -0.22, 0.18)
    return jnp.clip(array, -bound, bound).astype(held_as)


def setup_inputs(seed: int = 0) -> dict:
    streams_of = jax.random.split(jax.random.key(seed), 6)
    particle_pos = jnp.clip(16.0 * jax.random.uniform(streams_of[0], (3, PARTICLES), jnp.float32) ** block_levels(streams_of[0], (3, PARTICLES), ((1, 128),), -0.2, 0.2), 0.0, 16.0)
    tile_dest_keys = jax.random.split(jax.random.fold_in(streams_of[1], 1), TILES // TILES_DEV)
    tile_dest_turns = jax.random.permutation(jax.random.fold_in(streams_of[1], 3), TILES // TILES_DEV)
    tile_dest = jax.vmap(lambda own, number: deal_out(jax.random.fold_in(streams_of[1], 2), own, number, TILES_DEV, BRICKS, 1, CAP, 2))(tile_dest_keys, tile_dest_turns).reshape((TILES, 1))
    tile_block = touch_ends(jax.random.randint(streams_of[2], (TILES,), 0, BLOCKS_DEV), jax.random.fold_in(streams_of[2], 1), 0, BLOCKS_DEV - 1).astype(jnp.int32)
    fluid_flag = touch_ends((jax.random.randint(streams_of[3], (NX, NY, NZ), 0, 2) < 1).astype(jnp.int32), jax.random.fold_in(streams_of[3], 1), 0, 1)
    divergence = normal_values(streams_of[4], (NX, NY, NZ), 1.0, 6.0, ((0, 16), (1, 8)), jnp.float32)
    return {"particle_pos": particle_pos, "tile_dest": tile_dest, "tile_block": tile_block, "fluid_flag": fluid_flag, "divergence": divergence}


sphere_radius = 1.2
band_limit = 3.0
theta_floor = 0.2
jacobi_weight = 2.0 / 3.0

def cell_centres(block_edge):
    flat_index = jnp.arange(block_edge ** 3, dtype=jnp.int32)
    along_x = (flat_index // (block_edge * block_edge)).astype(jnp.float32) + 0.5
    along_y = (flat_index // block_edge % block_edge).astype(jnp.float32) + 0.5
    along_z = (flat_index % block_edge).astype(jnp.float32) + 0.5
    return (along_x, along_y, along_z)

def splat_group(points, block_edge):
    along_x, along_y, along_z = cell_centres(block_edge)
    squared = (points[:, 0, :, None] - along_x) ** 2 + (points[:, 1, :, None] - along_y) ** 2
    squared = squared + (points[:, 2, :, None] - along_z) ** 2
    nearest = jnp.sqrt(lax.optimization_barrier(jnp.min(squared, axis=1))) - sphere_radius
    return jnp.minimum(nearest, band_limit)

def splat_tiles(points, block_edge, group_size):
    count = points.shape[0]
    grouped = points.reshape(count // group_size, group_size, 3, points.shape[2])
    fields = lax.map(lambda group_points: splat_group(group_points, block_edge), grouped)
    return fields.reshape(count, block_edge ** 3)

def neighbours(padded):
    return [padded[2:, 1:-1, 1:-1], padded[:-2, 1:-1, 1:-1], padded[1:-1, 2:, 1:-1], padded[1:-1, :-2, 1:-1], padded[1:-1, 1:-1, 2:], padded[1:-1, 1:-1, :-2]]

def coefficients(level_set, padded_level, padded_fluid, padded_inside):
    magnitude = jnp.abs(level_set)
    diagonal = jnp.zeros_like(level_set)
    weights = []
    for beside_level, beside_fluid, beside_inside in zip(neighbours(padded_level), neighbours(padded_fluid), neighbours(padded_inside)):
        theta_ratio = jnp.maximum(magnitude / jnp.maximum(magnitude + jnp.abs(beside_level), 1.0), theta_floor)
        air_side = beside_inside * (1.0 - beside_fluid)
        diagonal = diagonal + beside_fluid + air_side / theta_ratio
        weights.append(beside_fluid)
    return (diagonal, weights)

def sweep_once(pressure, padded_pressure, weights, diagonal, divergence, fluid_cell):
    summed = divergence
    for weight, beside in zip(weights, neighbours(padded_pressure)):
        summed = summed + weight * beside
    return fluid_cell * ((1.0 - jacobi_weight) * pressure + jacobi_weight * summed / diagonal)

def reference(particle_pos, tile_dest, tile_block, fluid_flag, divergence):
    block_edge = BLOCK
    points = particle_pos.reshape(3, TILES, TILE).transpose(1, 0, 2)
    fields = splat_tiles(points, block_edge, 4)
    owner_block = (tile_dest[:, 0] * BLOCKS_DEV + tile_block).astype(jnp.int32)
    blocks = jnp.full((BRICKS * BLOCKS_DEV, block_edge ** 3), band_limit, dtype=jnp.float32)
    blocks = blocks.at[owner_block].min(fields)
    level_set = blocks.reshape(N_GX, N_GY, CX // block_edge, CY // block_edge, NZ // block_edge, block_edge, block_edge, block_edge)
    level_set = level_set.transpose(0, 2, 5, 1, 3, 6, 4, 7).reshape(NX, NY, NZ)
    fluid_cell = fluid_flag.astype(jnp.float32)
    inside = jnp.ones_like(level_set)
    diagonal, weights = coefficients(level_set, jnp.pad(level_set, 1), jnp.pad(fluid_cell, 1), jnp.pad(inside, 1))
    pressure = jnp.zeros_like(level_set)
    for sweep_step in range(ITERS):
        pressure = sweep_once(pressure, jnp.pad(pressure, 1), weights, diagonal, divergence, fluid_cell)
    return (level_set, pressure)
```

```python
import functools

import jax
import jax.numpy as jnp
from jax import lax
from jax.experimental import pallas as pl
from jax.experimental.pallas import tpu as pltpu
from jax.sharding import PartitionSpec as P

BLOCK = 16
TILE = 128
RADIUS = 1.2
BAND = 3.0
WEIGHT = 2.0 / 3.0
FAR = 1.0e9
HALO = 4
ROWS = 8

f32 = jnp.float32


def pack_kernel(dest_ref, block_ref, pos_ref, send_ref, count_ref):
    tiles = block_ref.shape[0]

    def clear(i, carry):
        count_ref[i] = 0
        return carry

    lax.fori_loop(0, count_ref.shape[0], clear, 0)
    send_ref[...] = jnp.full(send_ref.shape, -1.0, f32)

    def place(t, carry):
        owner = dest_ref[t]
        slot = count_ref[owner]
        count_ref[owner] = slot + 1
        row = owner * 2 + slot
        send_ref[row, 0:3, :] = pos_ref[:, pl.ds(pl.multiple_of(t * TILE, TILE), TILE)]
        send_ref[row, 3:4, :] = jnp.full((1, TILE), block_ref[t].astype(f32), f32)
        return carry

    lax.fori_loop(0, tiles, place, 0)


def splat_kernel(label_ref, spread_ref, rec_ref, out_ref, list_ref, part_ref, place_ref, dx_ref, dyz_ref, acc_ref, near_ref):
    records = label_ref.shape[0]

    def pick(i, n):
        @pl.when(label_ref[i] >= 0)
        def _():
            list_ref[n] = i

        return n + (label_ref[i] >= 0).astype(jnp.int32)

    count = lax.fori_loop(0, records, pick, jnp.int32(0))
    groups = (count + 7) // 8

    def fill(i, carry):
        list_ref[i] = list_ref[count - 1]
        return carry

    lax.fori_loop(count, groups * 8, fill, 0)

    near_ref[...] = jnp.full(near_ref.shape, FAR, f32)
    part_ref[96:128, :] = jnp.zeros((32, TILE), f32)
    cell = lax.broadcasted_iota(jnp.int32, (BLOCK, 128), 0).astype(f32) + 0.5
    lane = lax.broadcasted_iota(jnp.int32, (1, 128), 1)
    depth = (lane & 15).astype(f32) + 0.5

    def group(g, carry):
        for t in range(8):
            rec = rec_ref[list_ref[g * 8 + t]]
            part_ref[t * 4 : t * 4 + 4, :] = rec
        whole = part_ref[0:32, :]
        high = whole.astype(jnp.bfloat16).astype(f32)
        rest = whole - high
        middle = rest.astype(jnp.bfloat16).astype(f32)
        part_ref[0:32, :] = high
        part_ref[32:64, :] = middle
        part_ref[64:96, :] = rest - middle
        turned = jnp.transpose(part_ref[...], (1, 0)).astype(jnp.bfloat16)
        place_ref[...] = jnp.dot(turned, spread_ref[...], preferred_element_type=f32)

        def prepare(k, inner):
            for u in range(8):
                p = k * 8 + u
                row = place_ref[pl.ds(p, 1), :]
                dx = cell - row[:, 0:128]
                dy = cell - row[:, 128:256]
                dz = depth - row[:, 256:384]
                base = pl.multiple_of(p * BLOCK, BLOCK)
                dx_ref[pl.ds(base, BLOCK), :] = dx * dx
                dyz_ref[pl.ds(base, BLOCK), :] = dy * dy + dz * dz
            return inner

        lax.fori_loop(0, TILE // 8, prepare, 0)

        for quarter in range(4):

            def step(k, accs):
                accs = list(accs)
                for u in range(8):
                    base = pl.multiple_of((k * 8 + u) * BLOCK, BLOCK)
                    dyz = dyz_ref[pl.ds(base, BLOCK), :]
                    for i in range(4):
                        dx = dx_ref[pl.ds(base + (quarter * 4 + i), 1), :]
                        accs[i] = jnp.minimum(accs[i], dyz + dx)
                return tuple(accs)

            start = tuple(jnp.full((BLOCK, 128), FAR, f32) for _ in range(4))
            accs = lax.fori_loop(0, TILE // 8, step, start)
            for i in range(4):
                acc_ref[quarter * 4 + i] = accs[i]

        def merge(t, inner):
            label = label_ref[list_ref[g * 8 + t]]
            bx = label // 64
            by = (label // 16) % 4
            bz = label % 16
            half = bz // 8
            spot = bz % 8
            shift = ((spot - t) & 7) * 16
            mask = (lane >> 4) == spot
            xs = pl.ds(pl.multiple_of(bx * 16, 16), 16)
            ys = pl.ds(pl.multiple_of(by * 16, 16), 16)
            rolled = pltpu.roll(acc_ref[...].reshape(256, 128), shift, 1)
            rolled = jnp.where(mask, rolled, FAR).reshape(16, 16, 128)
            near_ref[half, xs, ys, :] = jnp.minimum(near_ref[half, xs, ys, :], rolled)
            return inner

        lax.fori_loop(0, 8, merge, 0)
        return carry

    lax.fori_loop(0, groups, group, 0)

    def finish(x, carry):
        for half in range(2):
            out_ref[x, :, half * 128 : half * 128 + 128] = jnp.minimum(jnp.sqrt(near_ref[half, x]) - RADIUS, BAND)
        return carry

    lax.fori_loop(0, out_ref.shape[0], finish, 0)


def inverse(a):
    r = pl.reciprocal(a, approx=True)
    r = r * (2.0 - a * r)
    return r * (2.0 - a * r)


def jacobi_kernel(level_ref, kind_ref, div_ref, lxl_ref, lxh_ref, kxl_ref, kxh_ref, dxl_ref, dxh_ref,
                  lyl_ref, lyh_ref, kyl_ref, kyh_ref, dyl_ref, dyh_ref, out_ref,
                  a_ref, u_ref, d_ref, c_ref, p_ref, q_ref, sem):
    nx, ny, nz = out_ref.shape
    H = HALO
    inner = pl.ds(ROWS, ny)
    copies = []
    for n, (mid, low, high, ext) in enumerate(
        ((level_ref, lxl_ref, lxh_ref, a_ref), (kind_ref, kxl_ref, kxh_ref, u_ref), (div_ref, dxl_ref, dxh_ref, d_ref))
    ):
        copies.append(pltpu.make_async_copy(mid, ext.at[pl.ds(H, nx), inner, :], sem.at[n, 0]))
        copies.append(pltpu.make_async_copy(low, ext.at[pl.ds(0, H), inner, :], sem.at[n, 1]))
        copies.append(pltpu.make_async_copy(high, ext.at[pl.ds(nx + H, H), inner, :], sem.at[n, 2]))
    for copy in copies:
        copy.start()
    zero = jnp.zeros((nx + 2 * H, ROWS, nz), f32)
    for low, high, ext in ((lyl_ref, lyh_ref, a_ref), (kyl_ref, kyh_ref, u_ref), (dyl_ref, dyh_ref, d_ref)):
        ext[:, 0:ROWS, :] = zero
        ext[:, ROWS + ny :, :] = zero
        ext[:, ROWS - H : ROWS, :] = low[...]
        ext[:, ROWS + ny : ROWS + ny + H, :] = high[...]
    for copy in copies:
        copy.wait()

    rows = ny + 2 * ROWS
    lane = lax.broadcasted_iota(jnp.int32, (rows, nz), 1)
    first = lane == 0
    last = lane == nz - 1

    def sides(v):
        return (
            jnp.where(first, 0.0, pltpu.roll(v, 1, 1)),
            jnp.where(last, 0.0, pltpu.roll(v, nz - 1, 1)),
            pltpu.roll(v, 1, 0),
            pltpu.roll(v, rows - 1, 0),
        )

    def coefficient(x, carry):
        a = jnp.abs(a_ref[x])
        u = u_ref[x]
        r = inverse(jnp.maximum(a, 1e-30))
        diagonal = None
        near_a = sides(a) + (jnp.abs(a_ref[x - 1]), jnp.abs(a_ref[x + 1]))
        near_u = sides(u) + (u_ref[x - 1], u_ref[x + 1])
        for b, w in zip(near_a, near_u):
            term = jnp.minimum(jnp.maximum(a + b, 1.0) * r, w)
            diagonal = term if diagonal is None else diagonal + term
        c = jnp.where(u == 1.0, WEIGHT * inverse(jnp.maximum(diagonal, 1.0)), 0.0)
        c_ref[x] = c
        p_ref[x] = c * d_ref[x]
        return carry

    lax.fori_loop(1, nx + 2 * H - 1, coefficient, 0)

    def around(ref, x):
        v = ref[x]
        down, up, left, right = sides(v)
        return v, (down + up) + (left + right) + (ref[x - 1] + ref[x + 1])

    def second(x, carry):
        v, total = around(p_ref, x)
        q_ref[x] = v * (4.0 / 3.0) + c_ref[x] * total
        return carry

    lax.fori_loop(2, nx + 2 * H - 2, second, 0)

    def third(x, carry):
        v, total = around(q_ref, x)
        d_ref[x] = v * (1.0 / 3.0) + p_ref[x] + c_ref[x] * total
        return carry

    lax.fori_loop(3, nx + 2 * H - 3, third, 0)

    def fourth(x, carry):
        v, total = around(d_ref, x)
        result = v * (1.0 / 3.0) + p_ref[x] + c_ref[x] * total
        out_ref[x - H] = result[ROWS : ROWS + ny, :]
        return carry

    lax.fori_loop(H, nx + H, fourth, 0)


def spread_matrix():
    row = jnp.arange(128)
    tile, coord = row % 32 // 4, row % 4
    column = jnp.arange(384)
    hit = (row[:, None] < 96) & (coord[:, None] == column[None, :] // 128)
    hit = hit & (tile[:, None] == column[None, :] % 128 // 16)
    return hit.astype(jnp.bfloat16)


def shifts(axis):
    count = lax.axis_size(axis)
    forward = [(i, i + 1) for i in range(count - 1)]
    return forward, [(j, i) for i, j in forward]


def swap(axis, low_part, high_part):
    forward, backward = shifts(axis)
    return lax.ppermute(high_part, axis, forward), lax.ppermute(low_part, axis, backward)


def halo(block):
    H = HALO
    xl, xh = swap("gx", block[:H], block[-H:])
    low = jnp.concatenate([xl[:, :H], block[:, :H], xh[:, :H]], axis=0)
    high = jnp.concatenate([xl[:, -H:], block[:, -H:], xh[:, -H:]], axis=0)
    yl, yh = swap("gy", low, high)
    return xl, xh, yl, yh


def per_device(particle_pos, tile_dest, tile_block, fluid_flag, divergence):
    nx, ny, nz = divergence.shape
    tiles = tile_block.shape[0]
    bricks = lax.axis_size("gx") * lax.axis_size("gy")
    smem = pl.BlockSpec(memory_space=pltpu.SMEM)
    vmem = pl.BlockSpec(memory_space=pltpu.VMEM)
    hbm = pl.BlockSpec(memory_space=pl.ANY)

    kind = 5.0 - 4.0 * fluid_flag.astype(f32)
    kxl, kxh, kyl, kyh = halo(kind)
    dxl, dxh, dyl, dyh = halo(divergence)

    send = pl.pallas_call(
        pack_kernel,
        out_shape=jax.ShapeDtypeStruct((bricks * 2, 4, TILE), f32),
        in_specs=[smem, smem, vmem],
        out_specs=vmem,
        scratch_shapes=[pltpu.SMEM((bricks,), jnp.int32)],
        compiler_params=pltpu.CompilerParams(vmem_limit_bytes=16 << 20),
        name="pack",
    )(tile_dest[:, 0], tile_block, particle_pos)
    arrived = lax.all_to_all(send, ("gx", "gy"), split_axis=0, concat_axis=0, tiled=True)
    labels = arrived[:, 3, 0].astype(jnp.int32)
    level = pl.pallas_call(
        splat_kernel,
        out_shape=jax.ShapeDtypeStruct((nx, ny, nz), f32),
        in_specs=[smem, vmem, vmem],
        out_specs=vmem,
        scratch_shapes=[
            pltpu.SMEM((bricks * 2 + 8,), jnp.int32),
            pltpu.VMEM((128, TILE), f32),
            pltpu.VMEM((TILE, 384), f32),
            pltpu.VMEM((TILE * BLOCK, 128), f32),
            pltpu.VMEM((TILE * BLOCK, 128), f32),
            pltpu.VMEM((BLOCK, BLOCK, 128), f32),
            pltpu.VMEM((2, nx, ny, 128), f32),
        ],
        compiler_params=pltpu.CompilerParams(vmem_limit_bytes=32 << 20),
        name="splat",
    )(labels, spread_matrix(), arrived)
    lxl, lxh, lyl, lyh = halo(level)
    ext = (nx + 2 * HALO, ny + 2 * ROWS, nz)
    pressure = pl.pallas_call(
        jacobi_kernel,
        out_shape=jax.ShapeDtypeStruct((nx, ny, nz), f32),
        in_specs=[hbm] * 9 + [vmem] * 6,
        out_specs=vmem,
        scratch_shapes=[pltpu.VMEM(ext, f32)] * 6 + [pltpu.SemaphoreType.DMA((3, 3))],
        compiler_params=pltpu.CompilerParams(vmem_limit_bytes=48 << 20),
        name="jacobi",
    )(level, kind, divergence, lxl, lxh, kxl, kxh, dxl, dxh, lyl, lyh, kyl, kyh, dyl, dyh)
    return (level, pressure)


def solution(mesh):
    placed = (
        P(None, ("gx", "gy")),
        P(("gx", "gy"), None),
        P(("gx", "gy")),
        P("gx", "gy", None),
        P("gx", "gy", None),
    )
    return jax.shard_map(
        per_device,
        mesh=mesh,
        in_specs=placed,
        out_specs=(P("gx", "gy", None), P("gx", "gy", None)),
        check_vma=False,
    )
```

```python
import functools

import jax
import jax.numpy as jnp
from jax import lax
from jax.experimental import pallas as pl
from jax.experimental.pallas import tpu as pltpu
from jax.sharding import PartitionSpec as P

BLOCK = 16
TILE = 128
RADIUS = 1.2
BAND = 3.0
WEIGHT = 2.0 / 3.0
FAR = 1.0e9
HALO = 4
ROWS = 8
REACH = RADIUS + BAND + 1.0e-3
PAIRS = 8

f32 = jnp.float32


def ordered(keys, first, second):
    row = lax.broadcasted_iota(jnp.int32, (8, TILE), 0)
    data = [list(keys), list(first), list(second)]
    size = 2
    while size <= TILE:
        if size >= 16 and size < TILE:
            sign = jnp.where((row & (size // 16)) == 0, 1.0, -1.0).astype(f32)
        else:
            sign = None
        gap = size // 2
        while gap >= 1:
            if gap < 16:
                for v in range(16):
                    if v & gap:
                        continue
                    w = v | gap
                    a, b = data[0][v], data[0][w]
                    if sign is not None:
                        swap_now = a * sign > b * sign
                    elif size < 16 and v & size:
                        swap_now = a < b
                    else:
                        swap_now = a > b
                    for part in data:
                        a, b = part[v], part[w]
                        part[v] = jnp.where(swap_now, b, a)
                        part[w] = jnp.where(swap_now, a, b)
            else:
                e = gap // 16
                low = (row & e) == 0
                way = jnp.where(low, 1.0, -1.0).astype(f32)
                if sign is not None:
                    way = way * sign
                for v in range(16):
                    others = []
                    for part in data:
                        if e == 4:
                            others.append(pltpu.roll(part[v], 4, 0))
                        else:
                            others.append(jnp.where(low, pltpu.roll(part[v], 8 - e, 0), pltpu.roll(part[v], e, 0)))
                    take = data[0][v] * way > others[0] * way
                    for part, other in zip(data, others):
                        part[v] = jnp.where(take, other, part[v])
            gap //= 2
        size *= 2
    return data


def pack_kernel(dest_ref, block_ref, pos_ref, send_ref, count_ref, tile_ref, turn_ref):
    tiles = block_ref.shape[0]
    lane = lax.broadcasted_iota(jnp.int32, (4, TILE), 1)
    note = (lax.broadcasted_iota(jnp.int32, (4, TILE), 0) == 3) & (lane == 0)

    def clear(i, carry):
        count_ref[i] = 0
        return carry

    lax.fori_loop(0, count_ref.shape[0], clear, 0)
    empty = jnp.where(lane == 0, -1.0, jnp.where(lane <= PAIRS, float(TILE), 0.0)).astype(f32)
    send_ref[...] = jnp.broadcast_to(empty[None], send_ref.shape)

    for t in range(tiles):
        tile_ref[0:3, t, :] = pos_ref[:, t * TILE : t * TILE + TILE]
    parts = []
    for c in range(3):
        turned = jnp.transpose(tile_ref[c], (1, 0))
        parts.append([turned[v * 8 : v * 8 + 8, :] for v in range(16)])
    parts = ordered(*parts)
    turn_ref[3] = jnp.zeros((TILE, TILE), f32)
    for k in range(PAIRS):
        below = jnp.zeros((8, TILE), f32)
        upto = jnp.zeros((8, TILE), f32)
        for v in range(16):
            below = below + jnp.where(parts[0][v] < 2 * k + 0.5 - REACH, 1.0, 0.0)
            upto = upto + jnp.where(parts[0][v] < 2 * k + 1.5 + REACH, 1.0, 0.0)
        turn_ref[3, 1 + k : 2 + k, :] = jnp.sum(below, axis=0, keepdims=True)
        turn_ref[3, 1 + PAIRS + k : 2 + PAIRS + k, :] = -jnp.sum(upto, axis=0, keepdims=True)
    for c in range(3):
        for v in range(16):
            turn_ref[c, pl.ds(v, 8, stride=16), :] = parts[c][v]
    for c in range(4):
        tile_ref[c] = jnp.transpose(turn_ref[c], (1, 0))

    def place(t, carry):
        owner = dest_ref[t]
        slot = count_ref[owner]
        count_ref[owner] = slot + 1
        send_ref[owner * 2 + slot] = jnp.where(note, block_ref[t].astype(f32), tile_ref[:, t, :])
        return carry

    lax.fori_loop(0, tiles, place, 0)


def ones_where(condition):
    return jnp.where(condition, 1.0, 0.0).astype(jnp.bfloat16)


def arrange(notes, note_ref, slot_ref):
    records = notes.shape[0]
    halves = records // 128
    turned = [jnp.transpose(notes[h * 128 : h * 128 + 128, :], (1, 0))[0:1, :] for h in range(halves)]
    labels = jnp.concatenate(turned, axis=1)
    valid = labels >= 0.0
    spot = (labels.astype(jnp.int32) & 7).astype(f32)
    column = lax.broadcasted_iota(jnp.int32, (8, records), 0).astype(f32)
    member = jnp.where(valid & (column == spot), 1.0, 0.0)
    earlier = ones_where(
        lax.broadcasted_iota(jnp.int32, (records, records), 0) < lax.broadcasted_iota(jnp.int32, (records, records), 1)
    )
    before = jnp.dot(member.astype(jnp.bfloat16), earlier, preferred_element_type=f32)
    rank = jnp.sum(member * before, axis=0, keepdims=True)
    counts = jnp.sum(member, axis=1, keepdims=True)
    total = jnp.sum(counts, axis=0, keepdims=True)
    room = 8.0 * jnp.floor((total + 63.0) * (1.0 / 64.0))
    late = jnp.where(valid & (rank >= room), 1.0, 0.0)
    turn = jnp.dot(jnp.broadcast_to(late, (8, records)).astype(jnp.bfloat16), earlier, preferred_element_type=f32)[0:1]
    used = jnp.minimum(counts, room)
    free = room - used
    offsets = [jnp.zeros((1, 1), f32)]
    for t in range(7):
        offsets.append(offsets[-1] + free[t : t + 1])
    offset = jnp.concatenate(offsets, axis=0)
    chosen = (turn >= offset) & (turn < offset + free)
    moved = jnp.sum(jnp.where(chosen, (used + turn - offset) * 8.0 + column, 0.0), axis=0, keepdims=True)
    slots = jnp.where(valid, jnp.where(late > 0.0, moved, rank * 8.0 + spot), -1.0)
    for h in range(halves):
        part = jnp.broadcast_to(slots[:, h * 128 : h * 128 + 128], (128, 128))
        slot_ref[h * 128 : h * 128 + 128, :] = jnp.transpose(part, (1, 0))
    lane = lax.broadcasted_iota(jnp.int32, (records, 128), 1).astype(f32)
    raised = jnp.broadcast_to(jnp.where(valid, labels + 1.0, 0.0), (8, records)).astype(jnp.bfloat16)
    for h in range(halves):
        here = jnp.dot(raised, ones_where(slot_ref[...] == lane + 128.0 * h), preferred_element_type=f32)
        note_ref[h : h + 1, :] = (here[0:1] - 1.0).astype(jnp.int32)
    least = jnp.min(notes, axis=0, keepdims=True)
    note_ref[halves : halves + 1, :] = jnp.where(lane[0:1] == 0.0, total, least).astype(jnp.int32)


def splat_kernel(rec_ref, out_ref, low_ref, high_ref, meta_ref, sem,
                 note_ref, slot_ref, split_ref, px_ref, py_ref, pz_ref, dyz_ref, acc_ref, near_ref):
    records = rec_ref.shape[0]
    halves = records // 128
    groups = records // 8
    nx = out_ref.shape[0]

    arrange(rec_ref[:, 3, :], note_ref, slot_ref)
    copy = pltpu.make_async_copy(note_ref, meta_ref, sem)
    copy.start()
    near_ref[...] = jnp.full(near_ref.shape, FAR, f32)
    for c in range(3):
        for h in range(halves):
            whole = jnp.transpose(rec_ref[h * 128 : h * 128 + 128, c, :], (1, 0))
            high = whole.astype(jnp.bfloat16)
            rest = whole - high.astype(f32)
            middle = rest.astype(jnp.bfloat16)
            last = (rest - middle.astype(f32)).astype(jnp.bfloat16)
            for n, part in enumerate((high, middle, last)):
                at = n * records + h * 128
                split_ref[c * TILE : c * TILE + TILE, at : at + 128] = part
    copy.wait()
    batches = (meta_ref[halves, 0] + 63) // 64

    lane = lax.broadcasted_iota(jnp.int32, (8, 128), 1)
    depth = (lane & 15).astype(f32) + 0.5
    spots = lax.broadcasted_iota(jnp.int32, (1, 128), 1) >> 4
    tile_lane = (lax.broadcasted_iota(jnp.int32, (records, 128), 1) >> 4).astype(f32)

    def expand(q, carry):
        slot = slot_ref[...] - (q * 16).astype(f32)
        hit = jnp.concatenate([ones_where(slot == tile_lane), ones_where(slot == tile_lane + 8.0)], axis=1)
        place = jnp.dot(split_ref[...], jnp.concatenate([hit] * 3, axis=0), preferred_element_type=f32)
        for n in range(2):
            rows = pl.ds(q * 2 + n, TILE, stride=groups)
            lanes = slice(n * 128, n * 128 + 128)
            px_ref[rows, :] = place[0:TILE, lanes]
            py_ref[rows, :] = place[TILE : 2 * TILE, lanes]
            pz_ref[rows, :] = place[2 * TILE : 3 * TILE, lanes]
        return carry

    lax.fori_loop(0, batches * 4, expand, 0)

    def batch(g, carry):
        def prepare(k, inner):
            for u in range(2):
                p = k * 2 + u
                rows = pl.ds(pl.multiple_of(p * groups + g * 8, 8), 8)
                py = py_ref[rows, :]
                dz = depth - pz_ref[rows, :]
                dz = dz * dz
                for y in range(16):
                    dy = (y + 0.5) - py
                    dyz_ref[p * 16 + y] = dy * dy + dz
            return inner

        lax.fori_loop(0, TILE // 2, prepare, 0)

        for k in range(PAIRS):
            stop = -meta_ref[halves, 1 + PAIRS + k]
            steps = (stop - meta_ref[halves, 1 + k] + 7) // 8
            first = jnp.maximum(stop - steps * 8, 0)

            def step(i, accs):
                accs = list(accs)
                for u in range(4):
                    p = first + i * 8 + u * 2
                    away = []
                    for v in range(2):
                        px = px_ref[pl.ds(pl.multiple_of((p + v) * groups + g * 8, 8), 8), :]
                        d0 = (2 * k + 0.5) - px
                        d1 = (2 * k + 1.5) - px
                        away.append((d0 * d0, d1 * d1))
                    for y in range(16):
                        one = dyz_ref[p * 16 + y]
                        two = dyz_ref[p * 16 + 16 + y]
                        for x in range(2):
                            both = jnp.minimum(one + away[0][x], two + away[1][x])
                            accs[x * 16 + y] = jnp.minimum(accs[x * 16 + y], both)
                return tuple(accs)

            accs = lax.fori_loop(0, steps, step, tuple(jnp.full((8, 128), FAR, f32) for _ in range(32)))
            for i in range(32):
                acc_ref[(k * 32 + i) * 8 : (k * 32 + i) * 8 + 8, :] = accs[i]

        def put_down(s, t, move):
            label = meta_ref[g // 2, g % 2 * 64 + s * 8 + t]
            spot = label & 7
            wanted = (label >= 0) & ((spot == t) != move)
            mask = spots == jnp.where(wanted, spot, -1)
            label = jnp.maximum(label, 0)
            bx = label // 64
            ys = pl.ds(pl.multiple_of(label // 16 % 4 * 16, 16), 16)
            half = label // 8 % 2

            def update():
                for x in range(16):
                    tile = acc_ref[pl.ds(x * 128 + s, 16, stride=8), :]
                    if move:
                        tile = pltpu.roll(tile, ((spot - t) & 7) * 16, 1)
                    tile = jnp.where(mask, tile, FAR)
                    near_ref[half, bx * 16 + x, ys, :] = jnp.minimum(near_ref[half, bx * 16 + x, ys, :], tile)

            if move:
                pl.when(wanted)(update)
            else:
                update()

        def merge(t, inner):
            for s in range(8):
                put_down(s, t, False)
            return inner

        lax.fori_loop(0, 8, merge, 0)

        def merge_late(t, inner):
            for s in range(8):
                put_down(s, t, True)
            return inner

        lax.fori_loop(0, 8, merge_late, 0)
        return carry

    lax.fori_loop(0, batches, batch, 0)

    def finish(x, carry):
        for half in range(2):
            out_ref[x, :, half * 128 : half * 128 + 128] = jnp.minimum(jnp.sqrt(near_ref[half, x]) - RADIUS, BAND)
        return carry

    lax.fori_loop(0, nx, finish, 0)
    low_ref[...] = out_ref[0:HALO]
    high_ref[...] = out_ref[nx - HALO : nx]


def jacobi_kernel(level_ref, kind_ref, div_ref, lxl_ref, lxh_ref, ixl_ref, ixh_ref, lyl_ref, lyh_ref, iyl_ref, iyh_ref, out_ref,
                  a_ref, u_ref, d_ref, c_ref, p_ref, q_ref, sem):
    nx, ny, nz = out_ref.shape
    H = HALO
    R = ROWS
    copies = []
    for n, (mid, low, high, ext) in enumerate(
        (
            (kind_ref, ixl_ref.at[0], ixh_ref.at[0], u_ref),
            (div_ref, ixl_ref.at[1], ixh_ref.at[1], d_ref),
            (level_ref, lxl_ref, lxh_ref, a_ref),
        )
    ):
        for half in range(2):
            lanes = pl.ds(half * 128, 128)
            for m, (source, at, size) in enumerate(((mid, H, nx), (low, 0, H), (high, nx + H, H))):
                copies.append(
                    pltpu.make_async_copy(
                        source.at[:, :, lanes], ext.at[pl.ds(at, size), half, pl.ds(R, ny), :], sem.at[n, m, half]
                    )
                )
    for copy in copies:
        copy.start()
    for low, high, ext in ((lyl_ref, lyh_ref, a_ref), (iyl_ref.at[0], iyh_ref.at[0], u_ref), (iyl_ref.at[1], iyh_ref.at[1], d_ref)):
        for half in range(2):
            lanes = slice(half * 128, half * 128 + 128)
            ext[:, half, R - H : R, :] = low[:, :, lanes]
            ext[:, half, R + ny : R + ny + H, :] = high[:, :, lanes]
    for copy in copies:
        copy.wait()

    lane = lax.broadcasted_iota(jnp.int32, (8, 128), 1)

    def along(pair, rows):
        first = jnp.broadcast_to(lane[0:1] == 0, (rows, 128))
        last = jnp.broadcast_to(lane[0:1] == 127, (rows, 128))
        up = [pltpu.roll(v, 1, 1) for v in pair]
        down = [pltpu.roll(v, 127, 1) for v in pair]
        return (
            (jnp.where(first, 0.0, up[0]), jnp.where(last, down[1], down[0])),
            (jnp.where(first, up[0], up[1]), jnp.where(last, 0.0, down[1])),
        )

    def coefficient(x, carry):
        r0, rows = R - H, ny + 2 * H
        at = slice(r0, r0 + rows)
        mags = [jnp.abs(a_ref[x, h, at, :]) for h in range(2)]
        kinds = [u_ref[x, h, at, :] for h in range(2)]
        za, zu = along(mags, rows), along(kinds, rows)
        for h in range(2):
            a, u = mags[h], kinds[h]
            r = 1.0 / jnp.maximum(a, 1e-30)
            diagonal = None
            near = [(za[h][0], zu[h][0]), (za[h][1], zu[h][1])]
            for dx, dy in ((-1, 0), (1, 0), (0, -1), (0, 1)):
                beside = slice(r0 + dy, r0 + dy + rows)
                near.append((jnp.abs(a_ref[x + dx, h, beside, :]), u_ref[x + dx, h, beside, :]))
            for b, w in near:
                term = jnp.minimum(jnp.maximum(a + b, 1.0) * r, w)
                diagonal = term if diagonal is None else diagonal + term
            c = jnp.where(u == 1.0, WEIGHT / jnp.maximum(diagonal, 1.0), 0.0)
            c_ref[x, h, at, :] = c
            p_ref[x, h, at, :] = c * d_ref[x, h, at, :]
        return carry

    lax.fori_loop(1, nx + 2 * H - 1, coefficient, 0, unroll=2)

    def around(ref, x, r0, rows):
        pair = [ref[x, h, r0 : r0 + rows, :] for h in range(2)]
        z = along(pair, rows)
        totals = []
        for h in range(2):
            total = z[h][0] + z[h][1]
            total = total + (ref[x - 1, h, r0 : r0 + rows, :] + ref[x + 1, h, r0 : r0 + rows, :])
            total = total + (ref[x, h, r0 - 1 : r0 - 1 + rows, :] + ref[x, h, r0 + 1 : r0 + 1 + rows, :])
            totals.append(total)
        return pair, totals

    def second(x, carry):
        r0, rows = R - H, ny + 2 * H
        at = slice(r0, r0 + rows)
        own, total = around(p_ref, x, r0, rows)
        for h in range(2):
            q_ref[x, h, at, :] = own[h] * (4.0 / 3.0) + c_ref[x, h, at, :] * total[h]
        return carry

    lax.fori_loop(2, nx + 2 * H - 2, second, 0, unroll=8)

    def third(x, carry):
        r0, rows = R - H, ny + 2 * H
        at = slice(r0, r0 + rows)
        own, total = around(q_ref, x, r0, rows)
        for h in range(2):
            d_ref[x, h, at, :] = own[h] * (1.0 / 3.0) + p_ref[x, h, at, :] + c_ref[x, h, at, :] * total[h]
        return carry

    lax.fori_loop(3, nx + 2 * H - 3, third, 0, unroll=8)

    def fourth(x, carry):
        at = slice(R, R + ny)
        own, total = around(d_ref, x, R, ny)
        for h in range(2):
            out_ref[x - H, :, h * 128 : h * 128 + 128] = (
                own[h] * (1.0 / 3.0) + p_ref[x, h, at, :] + c_ref[x, h, at, :] * total[h]
            )
        return carry

    lax.fori_loop(H, nx + H, fourth, 0, unroll=8)


def specs():
    return pl.BlockSpec(memory_space=pltpu.SMEM), pl.BlockSpec(memory_space=pltpu.VMEM), pl.BlockSpec(memory_space=pl.ANY)


def pack(dest, block, pos, bricks):
    smem, vmem, _ = specs()
    return pl.pallas_call(
        pack_kernel,
        out_shape=jax.ShapeDtypeStruct((bricks * 2, 4, TILE), f32),
        in_specs=[smem, smem, vmem],
        out_specs=vmem,
        scratch_shapes=[
            pltpu.SMEM((bricks,), jnp.int32),
            pltpu.VMEM((4, TILE, TILE), f32),
            pltpu.VMEM((4, TILE, TILE), f32),
        ],
        compiler_params=pltpu.CompilerParams(vmem_limit_bytes=16 << 20),
        name="pack",
    )(dest, block, pos)


def splat(arrived, nx, ny, nz):
    _, vmem, _ = specs()
    records = arrived.shape[0]
    strip = jax.ShapeDtypeStruct((HALO, ny, nz), f32)
    return pl.pallas_call(
        splat_kernel,
        out_shape=(jax.ShapeDtypeStruct((nx, ny, nz), f32), strip, strip),
        in_specs=[vmem],
        out_specs=(vmem, vmem, vmem),
        scratch_shapes=[
            pltpu.SMEM((8, 128), jnp.int32),
            pltpu.SemaphoreType.DMA,
            pltpu.VMEM((8, 128), jnp.int32),
            pltpu.VMEM((records, 128), f32),
            pltpu.VMEM((3 * TILE, 3 * records), jnp.bfloat16),
            pltpu.VMEM((TILE * records // 8, 128), f32),
            pltpu.VMEM((TILE * records // 8, 128), f32),
            pltpu.VMEM((TILE * records // 8, 128), f32),
            pltpu.VMEM((TILE * BLOCK, 8, 128), f32),
            pltpu.VMEM((BLOCK * BLOCK * 8, 128), f32),
            pltpu.VMEM((2, nx, ny, 128), f32),
        ],
        compiler_params=pltpu.CompilerParams(vmem_limit_bytes=40 << 20),
        name="splat",
    )(arrived)


def jacobi(level, kind, divergence, level_halo, input_halo):
    _, vmem, hbm = specs()
    nx, ny, nz = divergence.shape
    ext = (nx + 2 * HALO, 2, ny + 2 * ROWS, 128)
    lxl, lxh, lyl, lyh = level_halo
    ixl, ixh, iyl, iyh = input_halo
    return pl.pallas_call(
        jacobi_kernel,
        out_shape=jax.ShapeDtypeStruct((nx, ny, nz), f32),
        in_specs=[hbm] * 7 + [vmem] * 4,
        out_specs=vmem,
        scratch_shapes=[pltpu.VMEM(ext, f32)] * 6 + [pltpu.SemaphoreType.DMA((3, 3, 2))],
        compiler_params=pltpu.CompilerParams(vmem_limit_bytes=48 << 20),
        name="jacobi",
    )(level, kind, divergence, lxl, lxh, ixl, ixh, lyl, lyh, iyl, iyh)


def shifts(axis):
    count = lax.axis_size(axis)
    forward = [(i, i + 1) for i in range(count - 1)]
    return forward, [(j, i) for i, j in forward]


def swap(axis, low_part, high_part):
    forward, backward = shifts(axis)
    return lax.ppermute(high_part, axis, forward), lax.ppermute(low_part, axis, backward)


def halo_y(block, xl, xh):
    H = HALO
    low = jnp.concatenate([xl[..., :H, :], block[..., :H, :], xh[..., :H, :]], axis=-3)
    high = jnp.concatenate([xl[..., -H:, :], block[..., -H:, :], xh[..., -H:, :]], axis=-3)
    return swap("gy", low, high)


def per_device(particle_pos, tile_dest, tile_block, fluid_flag, divergence):
    nx, ny, nz = divergence.shape
    bricks = lax.axis_size("gx") * lax.axis_size("gy")

    kind = 5.0 - 4.0 * fluid_flag.astype(f32)
    both = jnp.stack([kind, divergence])
    ixl, ixh = swap("gx", both[:, :HALO], both[:, -HALO:])
    iyl, iyh = halo_y(both, ixl, ixh)

    send = pack(tile_dest[:, 0], tile_block, particle_pos, bricks)
    arrived = lax.all_to_all(send, ("gx", "gy"), split_axis=0, concat_axis=0, tiled=True)
    level, low, high = splat(arrived, nx, ny, nz)
    lxl, lxh = swap("gx", low, high)
    lyl, lyh = halo_y(level, lxl, lxh)
    pressure = jacobi(level, kind, divergence, (lxl, lxh, lyl, lyh), (ixl, ixh, iyl, iyh))
    return (level, pressure)


def solution(mesh):
    placed = (
        P(None, ("gx", "gy")),
        P(("gx", "gy"), None),
        P(("gx", "gy")),
        P("gx", "gy", None),
        P("gx", "gy", None),
    )
    return jax.shard_map(
        per_device,
        mesh=mesh,
        in_specs=placed,
        out_specs=(P("gx", "gy", None), P("gx", "gy", None)),
        check_vma=False,
    )
```

```python
import functools

import jax
import jax.numpy as jnp
from jax import lax
from jax.experimental import pallas as pl
from jax.experimental.pallas import tpu as pltpu
from jax.sharding import PartitionSpec as P

BLOCK = 16
TILE = 128
RADIUS = 1.2
BAND = 3.0
WEIGHT = 2.0 / 3.0
FAR = 1.0e9
HALO = 4
ROWS = 8
REACH = RADIUS + BAND + 1.0e-3
PAIRS = 8

f32 = jnp.float32


def ordered(keys, first, second):
    row = lax.broadcasted_iota(jnp.int32, (8, TILE), 0)
    data = [list(keys), list(first), list(second)]
    size = 2
    while size <= TILE:
        if size >= 16 and size < TILE:
            sign = jnp.where((row & (size // 16)) == 0, 1.0, -1.0).astype(f32)
        else:
            sign = None
        gap = size // 2
        while gap >= 1:
            if gap < 16:
                for v in range(16):
                    if v & gap:
                        continue
                    w = v | gap
                    a, b = data[0][v], data[0][w]
                    if sign is not None:
                        swap_now = a * sign > b * sign
                    elif size < 16 and v & size:
                        swap_now = a < b
                    else:
                        swap_now = a > b
                    for part in data:
                        a, b = part[v], part[w]
                        part[v] = jnp.where(swap_now, b, a)
                        part[w] = jnp.where(swap_now, a, b)
            else:
                e = gap // 16
                low = (row & e) == 0
                way = jnp.where(low, 1.0, -1.0).astype(f32)
                if sign is not None:
                    way = way * sign
                for v in range(16):
                    others = []
                    for part in data:
                        if e == 4:
                            others.append(pltpu.roll(part[v], 4, 0))
                        else:
                            others.append(jnp.where(low, pltpu.roll(part[v], 8 - e, 0), pltpu.roll(part[v], e, 0)))
                    take = data[0][v] * way > others[0] * way
                    for part, other in zip(data, others):
                        part[v] = jnp.where(take, other, part[v])
            gap //= 2
        size *= 2
    return data


def pack_kernel(dest_in, block_in, pos_in, send_ref, dest_ref, block_ref, pos_ref, count_ref, tile_ref, turn_ref, sem):
    tiles = block_ref.shape[0]
    copies = [
        pltpu.make_async_copy(a, b, sem.at[n])
        for n, (a, b) in enumerate(((pos_in, pos_ref), (dest_in, dest_ref), (block_in, block_ref)))
    ]
    for copy in copies:
        copy.start()
    lane = lax.broadcasted_iota(jnp.int32, (4, TILE), 1)
    note = (lax.broadcasted_iota(jnp.int32, (4, TILE), 0) == 3) & (lane == 0)

    def clear(i, carry):
        count_ref[i] = 0
        return carry

    lax.fori_loop(0, count_ref.shape[0], clear, 0)
    empty = jnp.where(lane == 0, -1.0, 0.0).astype(f32)
    send_ref[...] = jnp.broadcast_to(empty[None], send_ref.shape)

    copies[0].wait()
    for t in range(tiles):
        tile_ref[0:3, t, :] = pos_ref[:, t * TILE : t * TILE + TILE]
    parts = []
    for c in range(3):
        turned = jnp.transpose(tile_ref[c], (1, 0))
        parts.append([turned[v * 8 : v * 8 + 8, :] for v in range(16)])
    parts = ordered(*parts)
    turn_ref[3] = jnp.zeros((TILE, TILE), f32)
    for k in range(PAIRS):
        below = jnp.zeros((8, TILE), f32)
        upto = jnp.zeros((8, TILE), f32)
        for v in range(16):
            below = below + jnp.where(parts[0][v] < 2 * k + 0.5 - REACH, 1.0, 0.0)
            upto = upto + jnp.where(parts[0][v] < 2 * k + 1.5 + REACH, 1.0, 0.0)
        turn_ref[3, 1 + k : 2 + k, :] = jnp.sum(below, axis=0, keepdims=True) - TILE
        turn_ref[3, 1 + PAIRS + k : 2 + PAIRS + k, :] = -jnp.sum(upto, axis=0, keepdims=True)
    for c in range(3):
        for v in range(16):
            turn_ref[c, pl.ds(v, 8, stride=16), :] = parts[c][v]
    for c in range(4):
        tile_ref[c] = jnp.transpose(turn_ref[c], (1, 0))

    copies[1].wait()
    copies[2].wait()

    def place(t, carry):
        owner = dest_ref[t]
        slot = count_ref[owner]
        count_ref[owner] = slot + 1
        send_ref[owner * 2 + slot] = jnp.where(note, block_ref[t].astype(f32), tile_ref[:, t, :])
        return carry

    lax.fori_loop(0, tiles, place, 0)


def ones_where(condition):
    return jnp.where(condition, 1.0, 0.0).astype(jnp.bfloat16)


def row_to_column(row):
    return jnp.concatenate(
        [
            jnp.transpose(jnp.broadcast_to(row[:, h : h + 128], (128, 128)), (1, 0))
            for h in range(0, row.shape[1], 128)
        ],
        axis=0,
    )


def arrange(notes, note_ref, slot_ref):
    records = notes.shape[0]
    halves = records // 128
    turned = [jnp.transpose(notes[h * 128 : h * 128 + 128, :], (1, 0)) for h in range(halves)]
    labels = jnp.concatenate([v[0:1, :] for v in turned], axis=1)
    keys = jnp.concatenate([jnp.sum(v[1 : 1 + 2 * PAIRS], axis=0, keepdims=True) for v in turned], axis=1)
    valid = labels >= 0.0
    spot = (labels.astype(jnp.int32) & 7).astype(f32)
    column = lax.broadcasted_iota(jnp.int32, (8, records), 0).astype(f32)
    member = jnp.where(valid & (column == spot), 1.0, 0.0)
    from_index = lax.broadcasted_iota(jnp.int32, (records, records), 0)
    to_index = lax.broadcasted_iota(jnp.int32, (records, records), 1)
    earlier = ones_where(from_index < to_index)
    own = row_to_column(keys)
    own = jnp.concatenate([own] * halves, axis=1)
    smaller = (own < keys) | ((own == keys) & (from_index < to_index))
    before = jnp.dot(member.astype(jnp.bfloat16), ones_where(smaller), preferred_element_type=f32)
    rank = jnp.sum(member * before, axis=0, keepdims=True)
    counts = jnp.sum(member, axis=1, keepdims=True)
    total = jnp.sum(counts, axis=0, keepdims=True)
    room = 8.0 * jnp.floor((total + 63.0) * (1.0 / 64.0))
    late = jnp.where(valid & (rank >= room), 1.0, 0.0)
    turn = jnp.dot(jnp.broadcast_to(late, (8, records)).astype(jnp.bfloat16), earlier, preferred_element_type=f32)[0:1]
    used = jnp.minimum(counts, room)
    free = room - used
    offsets = [jnp.zeros((1, 1), f32)]
    for t in range(7):
        offsets.append(offsets[-1] + free[t : t + 1])
    offset = jnp.concatenate(offsets, axis=0)
    chosen = (turn >= offset) & (turn < offset + free)
    moved = jnp.sum(jnp.where(chosen, (used + turn - offset) * 8.0 + column, 0.0), axis=0, keepdims=True)
    slots = jnp.where(valid, jnp.where(late > 0.0, moved, rank * 8.0 + spot), -1.0)
    slot_ref[...] = slots
    lane = lax.broadcasted_iota(jnp.int32, (records, 128), 1).astype(f32)
    raised = jnp.broadcast_to(jnp.where(valid, labels + 1.0, 0.0), (8, records)).astype(jnp.bfloat16)
    late_slots = jnp.broadcast_to(jnp.where(late > 0.0, slots + 1.0, 0.0), (8, records)).astype(jnp.bfloat16)
    to_slot = row_to_column(slots)
    to_turn = row_to_column(jnp.where(late > 0.0, turn, -1.0))
    for h in range(halves):
        here = jnp.dot(raised, ones_where(to_slot == lane + 128.0 * h), preferred_element_type=f32)
        note_ref[h : h + 1, :] = (here[0:1] - 1.0).astype(jnp.int32)
        here = jnp.dot(late_slots, ones_where(to_turn == lane + 128.0 * h), preferred_element_type=f32)
        note_ref[halves + h : halves + h + 1, :] = here[0:1].astype(jnp.int32)
    sums = jnp.where(lane[0:1] == 0.0, total, jnp.sum(late, axis=1, keepdims=True))
    note_ref[2 * halves : 2 * halves + 1, :] = sums.astype(jnp.int32)


def splat_kernel(spread_ref, rec_ref, out_ref, low_ref, high_ref, meta_ref, sem,
                 note_ref, slot_ref, piece_ref, turn_ref, px_ref, py_ref, pz_ref, dyz_ref, acc_ref, near_ref):
    records = rec_ref.shape[0]
    halves = records // 128
    nx, ny = out_ref.shape[0:2]

    notes = rec_ref[:, 3, :]
    arrange(notes, note_ref, slot_ref)
    index = lax.broadcasted_iota(jnp.int32, (records, records), 0).astype(f32)
    to_slot = ones_where(index == slot_ref[...])
    pieces = [[], [], []]
    for c in range(3):
        whole = rec_ref[:, c, :]
        high = whole.astype(jnp.bfloat16)
        rest = whole - high.astype(f32)
        middle = rest.astype(jnp.bfloat16)
        pieces[0].append(high)
        pieces[1].append(middle)
        pieces[2].append((rest - middle.astype(f32)).astype(jnp.bfloat16))
    for n in range(3):
        for c in range(3):
            piece_ref[n * 3 + c] = jnp.dot(to_slot, pieces[n][c], preferred_element_type=f32)
    placed = jnp.dot(to_slot, notes.astype(jnp.bfloat16), preferred_element_type=f32)
    for b in range(records // 64):
        least = jnp.min(placed[b * 64 : b * 64 + 64, :], axis=0, keepdims=True)
        note_ref[2 * halves + 1 + b : 2 * halves + 2 + b, :] = least.astype(jnp.int32)
    copy = pltpu.make_async_copy(note_ref, meta_ref, sem)
    copy.start()
    near_ref[...] = jnp.full(near_ref.shape, FAR, f32)
    turn_ref[...] = jnp.zeros(turn_ref.shape, f32)
    copy.wait()
    batches = (meta_ref[2 * halves, 0] + 63) // 64
    late = meta_ref[2 * halves, 1]

    lane = lax.broadcasted_iota(jnp.int32, (8, 128), 1)
    depth = (lane & 15).astype(f32) + 0.5
    spots = lax.broadcasted_iota(jnp.int32, (1, 128), 1) >> 4

    def batch(g, carry):
        for s in range(8):
            for n in range(9):
                turn_ref[s, n * 8 : n * 8 + 8, :] = piece_ref[n, pl.ds(pl.multiple_of(g * 64 + s * 8, 8), 8), :]
            turned = jnp.transpose(turn_ref[s], (1, 0)).astype(jnp.bfloat16)
            place = jnp.dot(turned, spread_ref[...], preferred_element_type=f32)
            px_ref[pl.ds(s, TILE, stride=8), :] = place[:, 0:128]
            py_ref[pl.ds(s, TILE, stride=8), :] = place[:, 128:256]
            pz_ref[pl.ds(s, TILE, stride=8), :] = place[:, 256:384]

        def prepare(k, inner):
            for u in range(8):
                p = k * 8 + u
                rows = pl.ds(pl.multiple_of(p * 8, 8), 8)
                py = py_ref[rows, :]
                dz = depth - pz_ref[rows, :]
                dz = dz * dz
                for y in range(16):
                    dy = (y + 0.5) - py
                    dyz_ref[p * 16 + y] = dy * dy + dz
            return inner

        lax.fori_loop(0, TILE // 8, prepare, 0)

        for k in range(PAIRS):
            stop = -meta_ref[2 * halves + 1 + g, 1 + PAIRS + k]
            steps = (stop - (meta_ref[2 * halves + 1 + g, 1 + k] + TILE) + 7) // 8
            first = jnp.maximum(stop - steps * 8, 0)

            def step(i, accs):
                accs = list(accs)
                for u in range(4):
                    p = first + i * 8 + u * 2
                    away = []
                    for v in range(2):
                        px = px_ref[pl.ds(pl.multiple_of((p + v) * 8, 8), 8), :]
                        d0 = (2 * k + 0.5) - px
                        d1 = (2 * k + 1.5) - px
                        away.append((d0 * d0, d1 * d1))
                    for y in range(16):
                        one = dyz_ref[p * 16 + y]
                        two = dyz_ref[p * 16 + 16 + y]
                        for x in range(2):
                            both = jnp.minimum(one + away[0][x], two + away[1][x])
                            accs[x * 16 + y] = jnp.minimum(accs[x * 16 + y], both)
                return tuple(accs)

            accs = lax.fori_loop(0, steps, step, tuple(jnp.full((8, 128), FAR, f32) for _ in range(32)))
            for i in range(32):
                acc_ref[(k * 32 + i) * 8 : (k * 32 + i) * 8 + 8, :] = accs[i]

        def put_down(s, t, label, mask, move):
            bx = label // 64
            base = (label // 8 % 2) * (nx * ny) + bx * (16 * ny) + label // 16 % 4 * 16
            for x in range(16):
                tile = acc_ref[pl.ds(x * 128 + s, 16, stride=8), :]
                if move is not None:
                    tile = pltpu.roll(tile, move, 1)
                rows = pl.ds(pl.multiple_of(base + x * ny, 16), 16)
                near_ref[rows, :] = jnp.minimum(near_ref[rows, :], jnp.where(mask, tile, FAR))

        def merge(t, inner):
            for s in range(8):
                label = meta_ref[g // 2, g % 2 * 64 + s * 8 + t]
                wanted = (label >= 0) & ((label & 7) == t)
                put_down(s, t, jnp.maximum(label, 0), spots == jnp.where(wanted, t, -1), None)
            return inner

        lax.fori_loop(0, 8, merge, 0)

        def merge_late(i, inner):
            j = meta_ref[halves + i // 128, i % 128] - 1

            @pl.when(j // 64 == g)
            def _():
                t = j % 8
                label = meta_ref[j // 128, j % 128]
                spot = label & 7
                put_down(j // 8 % 8, t, label, spots == spot, ((spot - t) & 7) * 16)

            return inner

        lax.fori_loop(0, late, merge_late, 0)
        return carry

    lax.fori_loop(0, batches, batch, 0)

    def finish(x, carry):
        for half in range(2):
            out_ref[x, :, half * 128 : half * 128 + 128] = jnp.minimum(jnp.sqrt(near_ref[pl.ds(pl.multiple_of(half * nx * ny + x * ny, ny), ny), :]) - RADIUS, BAND)
        return carry

    lax.fori_loop(0, nx, finish, 0)
    low_ref[...] = out_ref[0:HALO]
    high_ref[...] = out_ref[nx - HALO : nx]


def jacobi_kernel(level_ref, kind_ref, div_ref, lxl_ref, lxh_ref, ixl_ref, ixh_ref, lyl_ref, lyh_ref, iyl_ref, iyh_ref, out_ref,
                  a_ref, u_ref, d_ref, c_ref, p_ref, q_ref, sem):
    nx, ny, nz = out_ref.shape
    H = HALO
    R = ROWS
    copies = []
    for n, (mid, low, high, ext) in enumerate(
        (
            (kind_ref, ixl_ref.at[0], ixh_ref.at[0], u_ref),
            (div_ref, ixl_ref.at[1], ixh_ref.at[1], d_ref),
            (level_ref, lxl_ref, lxh_ref, a_ref),
        )
    ):
        for half in range(2):
            lanes = pl.ds(half * 128, 128)
            for m, (source, at, size) in enumerate(((mid, H, nx), (low, 0, H), (high, nx + H, H))):
                copies.append(
                    pltpu.make_async_copy(
                        source.at[:, :, lanes], ext.at[pl.ds(at, size), half, pl.ds(R, ny), :], sem.at[n, m, half]
                    )
                )
    for copy in copies:
        copy.start()
    for low, high, ext in ((lyl_ref, lyh_ref, a_ref), (iyl_ref.at[0], iyh_ref.at[0], u_ref), (iyl_ref.at[1], iyh_ref.at[1], d_ref)):
        for half in range(2):
            lanes = slice(half * 128, half * 128 + 128)
            ext[:, half, R - H : R, :] = low[:, :, lanes]
            ext[:, half, R + ny : R + ny + H, :] = high[:, :, lanes]
    for copy in copies:
        copy.wait()

    lane = lax.broadcasted_iota(jnp.int32, (8, 128), 1)

    def along(pair, rows):
        first = jnp.broadcast_to(lane[0:1] == 0, (rows, 128))
        last = jnp.broadcast_to(lane[0:1] == 127, (rows, 128))
        up = [pltpu.roll(v, 1, 1) for v in pair]
        down = [pltpu.roll(v, 127, 1) for v in pair]
        return (
            (jnp.where(first, 0.0, up[0]), jnp.where(last, down[1], down[0])),
            (jnp.where(first, up[0], up[1]), jnp.where(last, 0.0, down[1])),
        )

    def coefficient(x, carry):
        r0, rows = R - H, ny + 2 * H
        at = slice(r0, r0 + rows)
        mags = [jnp.abs(a_ref[x, h, at, :]) for h in range(2)]
        kinds = [u_ref[x, h, at, :] for h in range(2)]
        za, zu = along(mags, rows), along(kinds, rows)
        for h in range(2):
            a, u = mags[h], kinds[h]
            r = 1.0 / jnp.maximum(a, 1e-30)
            diagonal = None
            near = [(za[h][0], zu[h][0]), (za[h][1], zu[h][1])]
            for dx, dy in ((-1, 0), (1, 0), (0, -1), (0, 1)):
                beside = slice(r0 + dy, r0 + dy + rows)
                near.append((jnp.abs(a_ref[x + dx, h, beside, :]), u_ref[x + dx, h, beside, :]))
            for b, w in near:
                term = jnp.minimum(jnp.maximum(a + b, 1.0) * r, w)
                diagonal = term if diagonal is None else diagonal + term
            c = jnp.where(u == 1.0, WEIGHT / jnp.maximum(diagonal, 1.0), 0.0)
            c_ref[x, h, at, :] = c
            p_ref[x, h, at, :] = c * d_ref[x, h, at, :]
        return carry

    lax.fori_loop(1, nx + 2 * H - 1, coefficient, 0, unroll=2)

    def around(ref, x, r0, rows):
        pair = [ref[x, h, r0 : r0 + rows, :] for h in range(2)]
        z = along(pair, rows)
        totals = []
        for h in range(2):
            total = z[h][0] + z[h][1]
            total = total + (ref[x - 1, h, r0 : r0 + rows, :] + ref[x + 1, h, r0 : r0 + rows, :])
            total = total + (ref[x, h, r0 - 1 : r0 - 1 + rows, :] + ref[x, h, r0 + 1 : r0 + 1 + rows, :])
            totals.append(total)
        return pair, totals

    def second(x, carry):
        r0, rows = R - H, ny + 2 * H
        at = slice(r0, r0 + rows)
        own, total = around(p_ref, x, r0, rows)
        for h in range(2):
            q_ref[x, h, at, :] = own[h] * (4.0 / 3.0) + c_ref[x, h, at, :] * total[h]
        return carry

    lax.fori_loop(2, nx + 2 * H - 2, second, 0, unroll=8)

    def third(x, carry):
        r0, rows = R - H, ny + 2 * H
        at = slice(r0, r0 + rows)
        own, total = around(q_ref, x, r0, rows)
        for h in range(2):
            d_ref[x, h, at, :] = own[h] * (1.0 / 3.0) + p_ref[x, h, at, :] + c_ref[x, h, at, :] * total[h]
        return carry

    lax.fori_loop(3, nx + 2 * H - 3, third, 0, unroll=8)

    def fourth(x, carry):
        at = slice(R, R + ny)
        own, total = around(d_ref, x, R, ny)
        for h in range(2):
            out_ref[x - H, :, h * 128 : h * 128 + 128] = (
                own[h] * (1.0 / 3.0) + p_ref[x, h, at, :] + c_ref[x, h, at, :] * total[h]
            )
        return carry

    lax.fori_loop(H, nx + H, fourth, 0, unroll=8)


def specs():
    return tuple(pl.BlockSpec(memory_space=space) for space in (pltpu.VMEM, pl.ANY, pltpu.HBM))


def pack(dest, block, pos, bricks):
    vmem, _, hbm = specs()
    return pl.pallas_call(
        pack_kernel,
        out_shape=jax.ShapeDtypeStruct((bricks * 2, 4, TILE), f32),
        in_specs=[hbm] * 3,
        out_specs=vmem,
        scratch_shapes=[
            pltpu.SMEM(dest.shape, jnp.int32),
            pltpu.SMEM(block.shape, jnp.int32),
            pltpu.VMEM(pos.shape, f32),
            pltpu.SMEM((bricks,), jnp.int32),
            pltpu.VMEM((4, TILE, TILE), f32),
            pltpu.VMEM((4, TILE, TILE), f32),
            pltpu.SemaphoreType.DMA((3,)),
        ],
        compiler_params=pltpu.CompilerParams(vmem_limit_bytes=16 << 20),
        name="pack",
    )(dest, block, pos)


def splat(arrived, nx, ny, nz):
    vmem, _, _ = specs()
    records = arrived.shape[0]
    strip = jax.ShapeDtypeStruct((HALO, ny, nz), f32)
    return pl.pallas_call(
        splat_kernel,
        out_shape=(jax.ShapeDtypeStruct((nx, ny, nz), f32), strip, strip),
        in_specs=[vmem, vmem],
        out_specs=(vmem, vmem, vmem),
        scratch_shapes=[
            pltpu.SMEM((16, 128), jnp.int32),
            pltpu.SemaphoreType.DMA,
            pltpu.VMEM((16, 128), jnp.int32),
            pltpu.VMEM((1, records), f32),
            pltpu.VMEM((9, records, TILE), f32),
            pltpu.VMEM((8, 128, TILE), f32),
            pltpu.VMEM((TILE * 8, 128), f32),
            pltpu.VMEM((TILE * 8, 128), f32),
            pltpu.VMEM((TILE * 8, 128), f32),
            pltpu.VMEM((TILE * BLOCK, 8, 128), f32),
            pltpu.VMEM((BLOCK * BLOCK * 8, 128), f32),
            pltpu.VMEM((2 * nx * ny, 128), f32),
        ],
        compiler_params=pltpu.CompilerParams(vmem_limit_bytes=40 << 20),
        name="splat",
    )(spread_matrix(), arrived)


def jacobi(level, kind, divergence, level_halo, input_halo):
    vmem, hbm, _ = specs()
    nx, ny, nz = divergence.shape
    ext = (nx + 2 * HALO, 2, ny + 2 * ROWS, 128)
    lxl, lxh, lyl, lyh = level_halo
    ixl, ixh, iyl, iyh = input_halo
    return pl.pallas_call(
        jacobi_kernel,
        out_shape=jax.ShapeDtypeStruct((nx, ny, nz), f32),
        in_specs=[hbm] * 7 + [vmem] * 4,
        out_specs=vmem,
        scratch_shapes=[pltpu.VMEM(ext, f32)] * 6 + [pltpu.SemaphoreType.DMA((3, 3, 2))],
        compiler_params=pltpu.CompilerParams(vmem_limit_bytes=48 << 20),
        name="jacobi",
    )(level, kind, divergence, lxl, lxh, ixl, ixh, lyl, lyh, iyl, iyh)


def spread_matrix():
    row = jnp.arange(128)
    coord, tile = row // 8 % 3, row % 8
    column = jnp.arange(384)
    hit = (row[:, None] < 72) & (coord[:, None] == column[None, :] // 128)
    hit = hit & (tile[:, None] == column[None, :] % 128 // 16)
    return hit.astype(jnp.bfloat16)


def shifts(axis):
    count = lax.axis_size(axis)
    forward = [(i, i + 1) for i in range(count - 1)]
    return forward, [(j, i) for i, j in forward]


def swap(axis, low_part, high_part):
    forward, backward = shifts(axis)
    return lax.ppermute(high_part, axis, forward), lax.ppermute(low_part, axis, backward)


def halo_y(block, xl, xh):
    H = HALO
    low = jnp.concatenate([xl[..., :H, :], block[..., :H, :], xh[..., :H, :]], axis=-3)
    high = jnp.concatenate([xl[..., -H:, :], block[..., -H:, :], xh[..., -H:, :]], axis=-3)
    return swap("gy", low, high)


def per_device(particle_pos, tile_dest, tile_block, fluid_flag, divergence):
    nx, ny, nz = divergence.shape
    bricks = lax.axis_size("gx") * lax.axis_size("gy")

    kind = 5.0 - 4.0 * fluid_flag.astype(f32)
    pair = (kind, divergence)
    ixl, ixh = swap("gx", jnp.stack([v[:HALO] for v in pair]), jnp.stack([v[-HALO:] for v in pair]))
    edge = jnp.stack([jnp.concatenate([v[:, :HALO], v[:, -HALO:]], axis=1) for v in pair])
    iyl, iyh = halo_y(edge, ixl, ixh)

    send = pack(tile_dest[:, 0], tile_block, particle_pos, bricks)
    arrived = lax.all_to_all(send, ("gx", "gy"), split_axis=0, concat_axis=0, tiled=True)
    arrived, iyl, iyh = lax.optimization_barrier((arrived, iyl, iyh))
    level, low, high = splat(arrived, nx, ny, nz)
    lxl, lxh = swap("gx", low, high)
    lyl, lyh = halo_y(level, lxl, lxh)
    pressure = jacobi(level, kind, divergence, (lxl, lxh, lyl, lyh), (ixl, ixh, iyl, iyh))
    return (level, pressure)


def solution(mesh):
    placed = (
        P(None, ("gx", "gy")),
        P(("gx", "gy"), None),
        P(("gx", "gy")),
        P("gx", "gy", None),
        P("gx", "gy", None),
    )
    return jax.shard_map(
        per_device,
        mesh=mesh,
        in_specs=placed,
        out_specs=(P("gx", "gy", None), P("gx", "gy", None)),
        check_vma=False,
    )
```

```python
import functools

import jax
import jax.numpy as jnp
from jax import lax
from jax.experimental import pallas as pl
from jax.experimental.pallas import tpu as pltpu
from jax.sharding import PartitionSpec as P

BLOCK = 16
TILE = 128
RADIUS = 1.2
BAND = 3.0
WEIGHT = 2.0 / 3.0
FAR = 1.0e9
HALO = 4
ROWS = 8
REACH = RADIUS + BAND + 1.0e-3
PAIRS = 8

f32 = jnp.float32


def ordered(keys, first, second):
    row = lax.broadcasted_iota(jnp.int32, (8, TILE), 0)
    data = [list(keys), list(first), list(second)]
    size = 2
    while size <= TILE:
        if size >= 16 and size < TILE:
            sign = jnp.where((row & (size // 16)) == 0, 1.0, -1.0).astype(f32)
        else:
            sign = None
        gap = size // 2
        while gap >= 1:
            if gap < 16:
                for v in range(16):
                    if v & gap:
                        continue
                    w = v | gap
                    a, b = data[0][v], data[0][w]
                    if sign is not None:
                        swap_now = a * sign > b * sign
                    elif size < 16 and v & size:
                        swap_now = a < b
                    else:
                        swap_now = a > b
                    for part in data:
                        a, b = part[v], part[w]
                        part[v] = jnp.where(swap_now, b, a)
                        part[w] = jnp.where(swap_now, a, b)
            else:
                e = gap // 16
                low = (row & e) == 0
                way = jnp.where(low, 1.0, -1.0).astype(f32)
                if sign is not None:
                    way = way * sign
                for v in range(16):
                    others = []
                    for part in data:
                        if e == 4:
                            others.append(pltpu.roll(part[v], 4, 0))
                        else:
                            others.append(jnp.where(low, pltpu.roll(part[v], 8 - e, 0), pltpu.roll(part[v], e, 0)))
                    take = data[0][v] * way > others[0] * way
                    for part, other in zip(data, others):
                        part[v] = jnp.where(take, other, part[v])
            gap //= 2
        size *= 2
    return data


def pack_kernel(dest_in, block_in, pos_in, send_ref, dest_ref, block_ref, pos_ref, count_ref, tile_ref, turn_ref, sem):
    tiles = block_ref.shape[0]
    copies = [
        pltpu.make_async_copy(a, b, sem.at[n])
        for n, (a, b) in enumerate(((pos_in, pos_ref), (dest_in, dest_ref), (block_in, block_ref)))
    ]
    for copy in copies:
        copy.start()
    lane = lax.broadcasted_iota(jnp.int32, (4, TILE), 1)
    note = (lax.broadcasted_iota(jnp.int32, (4, TILE), 0) == 3) & (lane == 0)

    def clear(i, carry):
        count_ref[i] = 0
        return carry

    lax.fori_loop(0, count_ref.shape[0], clear, 0)
    empty = jnp.where(lane == 0, -1.0, 0.0).astype(f32)
    send_ref[...] = jnp.broadcast_to(empty[None], send_ref.shape)

    copies[0].wait()
    for t in range(tiles):
        tile_ref[0:3, t, :] = pos_ref[:, t * TILE : t * TILE + TILE]
    parts = []
    for c in range(3):
        turned = jnp.transpose(tile_ref[c], (1, 0))
        parts.append([turned[v * 8 : v * 8 + 8, :] for v in range(16)])
    parts = ordered(*parts)
    turn_ref[3] = jnp.zeros((TILE, TILE), f32)
    for k in range(PAIRS):
        below = jnp.zeros((8, TILE), f32)
        upto = jnp.zeros((8, TILE), f32)
        for v in range(16):
            below = below + jnp.where(parts[0][v] < 2 * k + 0.5 - REACH, 1.0, 0.0)
            upto = upto + jnp.where(parts[0][v] < 2 * k + 1.5 + REACH, 1.0, 0.0)
        turn_ref[3, 1 + k : 2 + k, :] = jnp.sum(below, axis=0, keepdims=True) - TILE
        turn_ref[3, 1 + PAIRS + k : 2 + PAIRS + k, :] = -jnp.sum(upto, axis=0, keepdims=True)
    for c in range(3):
        for v in range(16):
            turn_ref[c, pl.ds(v, 8, stride=16), :] = parts[c][v]
    for c in range(4):
        tile_ref[c] = jnp.transpose(turn_ref[c], (1, 0))

    copies[1].wait()
    copies[2].wait()

    def place(t, carry):
        owner = dest_ref[t]
        slot = count_ref[owner]
        count_ref[owner] = slot + 1
        send_ref[owner * 2 + slot] = jnp.where(note, block_ref[t].astype(f32), tile_ref[:, t, :])
        return carry

    lax.fori_loop(0, tiles, place, 0)


def ones_where(condition):
    return jnp.where(condition, 1.0, 0.0).astype(jnp.bfloat16)


def row_to_column(row):
    return jnp.concatenate(
        [
            jnp.transpose(jnp.broadcast_to(row[:, h : h + 128], (128, 128)), (1, 0))
            for h in range(0, row.shape[1], 128)
        ],
        axis=0,
    )


def arrange(notes, note_ref, slot_ref):
    records = notes.shape[0]
    halves = records // 128
    turned = [jnp.transpose(notes[h * 128 : h * 128 + 128, :], (1, 0)) for h in range(halves)]
    labels = jnp.concatenate([v[0:1, :] for v in turned], axis=1)
    shift = [v[1 : 1 + PAIRS] - v[1 + PAIRS : 1 + 2 * PAIRS] for v in turned]
    keys = jnp.concatenate([jnp.sum(v, axis=0, keepdims=True) for v in shift], axis=1)
    valid = labels >= 0.0
    spot = (labels.astype(jnp.int32) & 7).astype(f32)
    column = lax.broadcasted_iota(jnp.int32, (8, records), 0).astype(f32)
    member = jnp.where(valid & (column == spot), 1.0, 0.0)
    from_index = lax.broadcasted_iota(jnp.int32, (records, records), 0)
    to_index = lax.broadcasted_iota(jnp.int32, (records, records), 1)
    earlier = ones_where(from_index < to_index)
    own = row_to_column(keys)
    own = jnp.concatenate([own] * halves, axis=1)
    smaller = (own < keys) | ((own == keys) & (from_index < to_index))
    before = jnp.dot(member.astype(jnp.bfloat16), ones_where(smaller), preferred_element_type=f32)
    rank = jnp.sum(member * before, axis=0, keepdims=True)
    counts = jnp.sum(member, axis=1, keepdims=True)
    total = jnp.sum(counts, axis=0, keepdims=True)
    room = 8.0 * jnp.floor((total + 63.0) * (1.0 / 64.0))
    late = jnp.where(valid & (rank >= room), 1.0, 0.0)
    turn = jnp.dot(jnp.broadcast_to(late, (8, records)).astype(jnp.bfloat16), earlier, preferred_element_type=f32)[0:1]
    used = jnp.minimum(counts, room)
    free = room - used
    offsets = [jnp.zeros((1, 1), f32)]
    for t in range(7):
        offsets.append(offsets[-1] + free[t : t + 1])
    offset = jnp.concatenate(offsets, axis=0)
    chosen = (turn >= offset) & (turn < offset + free)
    moved = jnp.sum(jnp.where(chosen, (used + turn - offset) * 8.0 + column, 0.0), axis=0, keepdims=True)
    slots = jnp.where(valid, jnp.where(late > 0.0, moved, rank * 8.0 + spot), -1.0)
    slot_ref[...] = slots
    lane = lax.broadcasted_iota(jnp.int32, (records, 128), 1).astype(f32)
    raised = jnp.broadcast_to(jnp.where(valid, labels + 1.0, 0.0), (8, records)).astype(jnp.bfloat16)
    late_slots = jnp.broadcast_to(jnp.where(late > 0.0, slots + 1.0, 0.0), (8, records)).astype(jnp.bfloat16)
    to_slot = row_to_column(slots)
    to_turn = row_to_column(jnp.where(late > 0.0, turn, -1.0))
    for h in range(halves):
        here = jnp.dot(raised, ones_where(to_slot == lane + 128.0 * h), preferred_element_type=f32)
        note_ref[h : h + 1, :] = (here[0:1] - 1.0).astype(jnp.int32)
        here = jnp.dot(late_slots, ones_where(to_turn == lane + 128.0 * h), preferred_element_type=f32)
        note_ref[halves + h : halves + h + 1, :] = here[0:1].astype(jnp.int32)
    sums = jnp.where(lane[0:1] == 0.0, total, jnp.sum(late, axis=1, keepdims=True))
    for b in range(records // 64):
        here = jnp.where((slots >= 64.0 * b) & (slots < 64.0 * b + 64.0), late, 0.0)
        sums = jnp.where(lane[0:1] == 2.0 + b, jnp.sum(here, axis=1, keepdims=True), sums)
    note_ref[2 * halves : 2 * halves + 1, :] = sums.astype(jnp.int32)


def strips_kernel(side_ref, kind_in, div_in, first_ref, second_ref, face1_ref, face2_ref, kx_ref, ky_ref, dy_ref, sem):
    nx, ny, nz = kind_in.shape
    copies = []
    side = side_ref[0]
    for n, (at, out) in enumerate((((1 - side) * (nx - HALO), first_ref), (side * (nx - HALO), second_ref))):
        planes = pl.ds(at, HALO)
        copies.append(pltpu.make_async_copy(kind_in.at[planes], kx_ref.at[n], sem.at[n]))
        copies.append(pltpu.make_async_copy(div_in.at[planes], out.at[1], sem.at[2 + n]))
    for n, at in enumerate((0, ny - 8)):
        rows = pl.ds(at, 8)
        copies.append(pltpu.make_async_copy(kind_in.at[:, rows, :], ky_ref.at[n], sem.at[4 + n]))
        copies.append(pltpu.make_async_copy(div_in.at[:, rows, :], dy_ref.at[n], sem.at[6 + n]))
    for copy in copies:
        copy.start()
    for copy in copies:
        copy.wait()
    first_ref[0] = kind_of(kx_ref[0])
    second_ref[0] = kind_of(kx_ref[1])
    low = slice(0, HALO)
    high = slice(8 - HALO, 8)
    even = side_ref[1] == 0
    for turn, out in ((True, face1_ref), (False, face2_ref)):
        up = even if turn else jnp.logical_not(even)
        out[0] = jnp.where(up, kind_of(ky_ref[1, :, high, :]), kind_of(ky_ref[0, :, low, :]))
        out[1] = jnp.where(up, dy_ref[1, :, high, :], dy_ref[0, :, low, :])


def strips(side, flag, divergence):
    vmem, hbm, _ = specs()
    nx, ny, nz = divergence.shape
    strip = jax.ShapeDtypeStruct((2, HALO, ny, nz), f32)
    edge = jax.ShapeDtypeStruct((2, nx, HALO, nz), f32)
    return pl.pallas_call(
        strips_kernel,
        out_shape=(strip, strip, edge, edge),
        in_specs=[scalars(), hbm, hbm],
        out_specs=(vmem,) * 4,
        scratch_shapes=[
            pltpu.VMEM((2, HALO, ny, nz), jnp.int32),
            pltpu.VMEM((2, nx, 8, nz), jnp.int32),
            pltpu.VMEM((2, nx, 8, nz), f32),
            pltpu.SemaphoreType.DMA((8,)),
        ],
        compiler_params=pltpu.CompilerParams(vmem_limit_bytes=60 << 20),
        name="strips",
    )(side, flag, divergence)


def kind_of(flag):
    return 5.0 - 4.0 * flag.astype(f32)


def splat_kernel(side_ref, spread_ref, rec_ref, out_ref, halves_ref, first_ref, second_ref, left_ref, right_ref, meta_ref, sem,
                 note_ref, slot_ref, piece_ref, turn_ref, px_ref, py_ref, pz_ref, dyz_ref, acc_ref, near_ref):
    records = rec_ref.shape[0]
    halves = records // 128
    nx, ny = out_ref.shape[0:2]

    notes = rec_ref[:, 3, :]
    arrange(notes, note_ref, slot_ref)
    index = lax.broadcasted_iota(jnp.int32, (records, records), 0).astype(f32)
    to_slot = ones_where(index == slot_ref[...])
    pieces = [[], [], []]
    for c in range(3):
        whole = rec_ref[:, c, :]
        high = whole.astype(jnp.bfloat16)
        rest = whole - high.astype(f32)
        middle = rest.astype(jnp.bfloat16)
        pieces[0].append(high)
        pieces[1].append(middle)
        pieces[2].append((rest - middle.astype(f32)).astype(jnp.bfloat16))
    for n in range(3):
        for c in range(3):
            piece_ref[n * 3 + c] = jnp.dot(to_slot, pieces[n][c], preferred_element_type=f32)
    placed = jnp.dot(to_slot, notes.astype(jnp.bfloat16), preferred_element_type=f32)
    for b in range(records // 64):
        least = jnp.min(placed[b * 64 : b * 64 + 64, :], axis=0, keepdims=True)
        note_ref[2 * halves + 1 + b : 2 * halves + 2 + b, :] = least.astype(jnp.int32)
    copy = pltpu.make_async_copy(note_ref, meta_ref, sem)
    copy.start()
    near_ref[...] = jnp.full(near_ref.shape, FAR, f32)
    turn_ref[...] = jnp.zeros(turn_ref.shape, f32)
    copy.wait()
    batches = (meta_ref[2 * halves, 0] + 63) // 64
    late = meta_ref[2 * halves, 1]

    lane = lax.broadcasted_iota(jnp.int32, (8, 128), 1)
    depth = (lane & 15).astype(f32) + 0.5
    spots = lax.broadcasted_iota(jnp.int32, (1, 128), 1) >> 4

    def batch(g, carry):
        for s in range(8):
            for n in range(9):
                turn_ref[s, n * 8 : n * 8 + 8, :] = piece_ref[n, pl.ds(pl.multiple_of(g * 64 + s * 8, 8), 8), :]
            turned = jnp.transpose(turn_ref[s], (1, 0)).astype(jnp.bfloat16)
            place = jnp.dot(turned, spread_ref[...], preferred_element_type=f32)
            px_ref[pl.ds(s, TILE, stride=8), :] = place[:, 0:128]
            py_ref[pl.ds(s, TILE, stride=8), :] = place[:, 128:256]
            pz_ref[pl.ds(s, TILE, stride=8), :] = place[:, 256:384]

        def prepare(k, inner):
            for u in range(8):
                p = k * 8 + u
                rows = pl.ds(pl.multiple_of(p * 8, 8), 8)
                py = py_ref[rows, :]
                dz = depth - pz_ref[rows, :]
                dz = dz * dz
                for y in range(16):
                    dy = (y + 0.5) - py
                    dyz_ref[p * 16 + y] = dy * dy + dz
            return inner

        lax.fori_loop(0, TILE // 8, prepare, 0)

        for k in range(PAIRS):
            stop = -meta_ref[2 * halves + 1 + g, 1 + PAIRS + k]
            steps = (stop - (meta_ref[2 * halves + 1 + g, 1 + k] + TILE) + 7) // 8
            first = jnp.maximum(stop - steps * 8, 0)

            def step(i, accs):
                accs = list(accs)
                for u in range(4):
                    p = first + i * 8 + u * 2
                    away = []
                    for v in range(2):
                        px = px_ref[pl.ds(pl.multiple_of((p + v) * 8, 8), 8), :]
                        d0 = (2 * k + 0.5) - px
                        d1 = (2 * k + 1.5) - px
                        away.append((d0 * d0, d1 * d1))
                    for y in range(16):
                        one = dyz_ref[p * 16 + y]
                        two = dyz_ref[p * 16 + 16 + y]
                        for x in range(2):
                            both = jnp.minimum(one + away[0][x], two + away[1][x])
                            accs[x * 16 + y] = jnp.minimum(accs[x * 16 + y], both)
                return tuple(accs)

            accs = lax.fori_loop(0, steps, step, tuple(jnp.full((8, 128), FAR, f32) for _ in range(32)))
            for i in range(32):
                acc_ref[(k * 32 + i) * 8 : (k * 32 + i) * 8 + 8, :] = accs[i]

        def put_down(s, t, label, mask, move):
            bx = label // 64
            base = (label // 8 % 2) * (nx * ny) + bx * (16 * ny) + label // 16 % 4 * 16
            for x in range(16):
                tile = acc_ref[pl.ds(x * 128 + s, 16, stride=8), :]
                if move is not None:
                    tile = pltpu.roll(tile, move, 1)
                rows = pl.ds(pl.multiple_of(base + x * ny, 16), 16)
                near_ref[rows, :] = jnp.minimum(near_ref[rows, :], jnp.where(mask, tile, FAR))

        def merge(t, inner):
            for s in range(8):
                label = meta_ref[g // 2, g % 2 * 64 + s * 8 + t]
                wanted = (label >= 0) & ((label & 7) == t)
                put_down(s, t, jnp.maximum(label, 0), spots == jnp.where(wanted, t, -1), None)
            return inner

        lax.fori_loop(0, 8, merge, 0)

        def merge_late(i, inner):
            j = meta_ref[halves + i // 128, i % 128] - 1

            @pl.when(j // 64 == g)
            def _():
                t = j % 8
                label = meta_ref[j // 128, j % 128]
                spot = label & 7
                put_down(j // 8 % 8, t, label, spots == spot, ((spot - t) & 7) * 16)

            return inner

        lax.fori_loop(0, jnp.where(meta_ref[2 * halves, 2 + g] > 0, late, 0), merge_late, 0)
        return carry

    lax.fori_loop(0, batches, batch, 0)

    def finish(x, carry):
        for half in range(2):
            lanes = slice(half * 128, half * 128 + 128)
            rows = pl.ds(pl.multiple_of(half * nx * ny + x * ny, ny), ny)
            level = jnp.minimum(jnp.sqrt(near_ref[rows, :]) - RADIUS, BAND)
            out_ref[x, :, lanes] = level
            size = jnp.abs(level)
            halves_ref[x, half] = size
            left_ref[x, :, lanes] = size[0:HALO, :]
            right_ref[x, :, lanes] = size[ny - HALO : ny, :]
        return carry

    lax.fori_loop(0, nx, finish, 0)
    side = side_ref[0]
    first_ref[...] = jnp.abs(out_ref[pl.ds((1 - side) * (nx - HALO), HALO)])
    second_ref[...] = jnp.abs(out_ref[pl.ds(side * (nx - HALO), HALO)])


def jacobi_kernel(side_ref, level_ref, flag_ref, div_ref, lx1_ref, lx2_ref, ix1_ref, ix2_ref, ly1_ref, ly2_ref, iy1_ref, iy2_ref, out_ref,
                  a_ref, u_ref, d_ref, c_ref, p_ref, q_ref, f_ref, sem):
    nx, ny, nz = out_ref.shape
    H = HALO
    R = ROWS
    copies = []
    inner = pl.ds(R, ny)
    side = side_ref[0]
    mid_x = pl.ds(H, nx)
    first_x, second_x = pl.ds((1 - side) * (nx + H), H), pl.ds(side * (nx + H), H)
    for half in range(2):
        lanes = pl.ds(half * 128, 128)
        for n, (source, target) in enumerate(
            (
                (flag_ref, f_ref.at[:, half]),
                (ix1_ref.at[0], u_ref.at[first_x, half, inner]),
                (ix2_ref.at[0], u_ref.at[second_x, half, inner]),
                (div_ref, d_ref.at[mid_x, half, inner]),
                (ix1_ref.at[1], d_ref.at[first_x, half, inner]),
                (ix2_ref.at[1], d_ref.at[second_x, half, inner]),
                (lx1_ref, a_ref.at[first_x, half, inner]),
                (lx2_ref, a_ref.at[second_x, half, inner]),
            )
        ):
            copies.append(pltpu.make_async_copy(source.at[:, :, lanes], target, sem.at[n, half]))
    copies.append(pltpu.make_async_copy(level_ref, a_ref.at[mid_x, :, inner], sem.at[8, 0]))
    for copy in copies:
        copy.start()
    for half in range(2):
        lanes = slice(half * 128, half * 128 + 128)
        for turn, rows in ((1, slice(R - H, R)), (0, slice(R + ny, R + ny + H))):
            first = side_ref[1] == turn
            a_ref[:, half, rows, :] = jnp.where(first, ly1_ref[0 : nx + 2 * H, :, lanes], ly2_ref[0 : nx + 2 * H, :, lanes])
            for n, ext in enumerate((u_ref, d_ref)):
                at = nx + 2 * H + n * 2 * H
                corner = jnp.where(first, ly1_ref[at : at + 2 * H, :, lanes], ly2_ref[at : at + 2 * H, :, lanes])
                ext[0:H, half, rows, :] = corner[0:H]
                ext[nx + H : nx + 2 * H, half, rows, :] = corner[H : 2 * H]
                ext[H : nx + H, half, rows, :] = jnp.where(first, iy1_ref[n, :, :, lanes], iy2_ref[n, :, :, lanes])
    copies[0].wait()
    copies[8].wait()

    def convert(x, carry):
        for h in range(2):
            u_ref[x + H, h, R : R + ny, :] = kind_of(f_ref[x, h])
        return carry

    lax.fori_loop(0, nx, convert, 0, unroll=2)
    for copy in copies[1:8] + copies[9:]:
        copy.wait()

    lane = lax.broadcasted_iota(jnp.int32, (8, 128), 1)

    def along(pair, rows):
        first = jnp.broadcast_to(lane[0:1] == 0, (rows, 128))
        last = jnp.broadcast_to(lane[0:1] == 127, (rows, 128))
        up = [pltpu.roll(v, 1, 1) for v in pair]
        down = [pltpu.roll(v, 127, 1) for v in pair]
        return (
            (jnp.where(first, 0.0, up[0]), jnp.where(last, down[1], down[0])),
            (jnp.where(first, up[0], up[1]), jnp.where(last, 0.0, down[1])),
        )

    def coefficient(x, carry):
        r0, rows = R - H, ny + 2 * H
        at = slice(r0, r0 + rows)
        mags = [a_ref[x, h, at, :] for h in range(2)]
        kinds = [u_ref[x, h, at, :] for h in range(2)]
        za, zu = along(mags, rows), along(kinds, rows)
        for h in range(2):
            a, u = mags[h], kinds[h]
            r = 1.0 / jnp.maximum(a, 1e-30)
            diagonal = None
            near = [(za[h][0], zu[h][0]), (za[h][1], zu[h][1])]
            for dx, dy in ((-1, 0), (1, 0), (0, -1), (0, 1)):
                beside = slice(r0 + dy, r0 + dy + rows)
                near.append((a_ref[x + dx, h, beside, :], u_ref[x + dx, h, beside, :]))
            for b, w in near:
                term = jnp.minimum(jnp.maximum(a + b, 1.0) * r, w)
                diagonal = term if diagonal is None else diagonal + term
            c = jnp.where(u == 1.0, WEIGHT / jnp.maximum(diagonal, 1.0), 0.0)
            c_ref[x, h, at, :] = c
            p_ref[x, h, at, :] = c * d_ref[x, h, at, :]
        return carry

    lax.fori_loop(1, nx + 2 * H - 1, coefficient, 0, unroll=2)

    def around(ref, x, r0, rows):
        pair = [ref[x, h, r0 : r0 + rows, :] for h in range(2)]
        z = along(pair, rows)
        totals = []
        for h in range(2):
            total = z[h][0] + z[h][1]
            total = total + (ref[x - 1, h, r0 : r0 + rows, :] + ref[x + 1, h, r0 : r0 + rows, :])
            total = total + (ref[x, h, r0 - 1 : r0 - 1 + rows, :] + ref[x, h, r0 + 1 : r0 + 1 + rows, :])
            totals.append(total)
        return pair, totals

    def second(x, carry):
        r0, rows = R - H, ny + 2 * H
        at = slice(r0, r0 + rows)
        own, total = around(p_ref, x, r0, rows)
        for h in range(2):
            q_ref[x, h, at, :] = own[h] * (4.0 / 3.0) + c_ref[x, h, at, :] * total[h]
        return carry

    lax.fori_loop(2, nx + 2 * H - 2, second, 0, unroll=8)

    def third(x, carry):
        r0, rows = R - H, ny + 2 * H
        at = slice(r0, r0 + rows)
        own, total = around(q_ref, x, r0, rows)
        for h in range(2):
            d_ref[x, h, at, :] = own[h] * (1.0 / 3.0) + p_ref[x, h, at, :] + c_ref[x, h, at, :] * total[h]
        return carry

    lax.fori_loop(3, nx + 2 * H - 3, third, 0, unroll=8)

    def fourth(x, carry):
        at = slice(R, R + ny)
        own, total = around(d_ref, x, R, ny)
        for h in range(2):
            out_ref[x - H, :, h * 128 : h * 128 + 128] = (
                own[h] * (1.0 / 3.0) + p_ref[x, h, at, :] + c_ref[x, h, at, :] * total[h]
            )
        return carry

    lax.fori_loop(H, nx + H, fourth, 0, unroll=8)


def specs():
    return tuple(pl.BlockSpec(memory_space=space) for space in (pltpu.VMEM, pl.ANY, pltpu.HBM))


def scalars():
    return pl.BlockSpec(memory_space=pltpu.SMEM)


def pack(dest, block, pos, bricks):
    vmem, _, hbm = specs()
    return pl.pallas_call(
        pack_kernel,
        out_shape=jax.ShapeDtypeStruct((bricks * 2, 4, TILE), f32),
        in_specs=[hbm] * 3,
        out_specs=vmem,
        scratch_shapes=[
            pltpu.SMEM(dest.shape, jnp.int32),
            pltpu.SMEM(block.shape, jnp.int32),
            pltpu.VMEM(pos.shape, f32),
            pltpu.SMEM((bricks,), jnp.int32),
            pltpu.VMEM((4, TILE, TILE), f32),
            pltpu.VMEM((4, TILE, TILE), f32),
            pltpu.SemaphoreType.DMA((3,)),
        ],
        compiler_params=pltpu.CompilerParams(vmem_limit_bytes=60 << 20),
        name="pack",
    )(dest, block, pos)


def splat(side, arrived, nx, ny, nz):
    vmem, _, _ = specs()
    records = arrived.shape[0]
    strip = jax.ShapeDtypeStruct((HALO, ny, nz), f32)
    edge = jax.ShapeDtypeStruct((nx, HALO, nz), f32)
    return pl.pallas_call(
        splat_kernel,
        out_shape=(
            jax.ShapeDtypeStruct((nx, ny, nz), f32),
            jax.ShapeDtypeStruct((nx, 2, ny, 128), f32),
            strip,
            strip,
            edge,
            edge,
        ),
        in_specs=[scalars(), vmem, vmem],
        out_specs=(vmem,) * 6,
        scratch_shapes=[
            pltpu.SMEM((16, 128), jnp.int32),
            pltpu.SemaphoreType.DMA,
            pltpu.VMEM((16, 128), jnp.int32),
            pltpu.VMEM((1, records), f32),
            pltpu.VMEM((9, records, TILE), f32),
            pltpu.VMEM((8, 128, TILE), f32),
            pltpu.VMEM((TILE * 8, 128), f32),
            pltpu.VMEM((TILE * 8, 128), f32),
            pltpu.VMEM((TILE * 8, 128), f32),
            pltpu.VMEM((TILE * BLOCK, 8, 128), f32),
            pltpu.VMEM((BLOCK * BLOCK * 8, 128), f32),
            pltpu.VMEM((2 * nx * ny, 128), f32),
        ],
        compiler_params=pltpu.CompilerParams(vmem_limit_bytes=40 << 20),
        name="splat",
    )(side, spread_matrix(), arrived)


def edges_kernel(side_ref, left_ref, right_ref, lx1_ref, lx2_ref, ix1_ref, ix2_ref, out1_ref, out2_ref):
    nx, H = left_ref.shape[0:2]
    ny = lx1_ref.shape[1]
    side = side_ref[0]
    even = side_ref[1] == 0
    ext = nx + 2 * H
    low = slice(0, H)
    high = slice(ny - H, ny)
    for turn, out in ((True, out1_ref), (False, out2_ref)):
        up = even if turn else jnp.logical_not(even)
        out[H : nx + H] = jnp.where(up, right_ref[...], left_ref[...])
        for at, step, one, two in (
            (0, nx + H, lx1_ref, lx2_ref),
            (ext, H, ix1_ref.at[0], ix2_ref.at[0]),
            (ext + 2 * H, H, ix1_ref.at[1], ix2_ref.at[1]),
        ):
            out[pl.ds(at + (1 - side) * step, H)] = jnp.where(up, one[:, high, :], one[:, low, :])
            out[pl.ds(at + side * step, H)] = jnp.where(up, two[:, high, :], two[:, low, :])


def edges(side, left, right, lx1, lx2, ix1, ix2):
    vmem, _, _ = specs()
    nx, H, nz = left.shape
    out = jax.ShapeDtypeStruct((nx + 6 * H, H, nz), f32)
    return pl.pallas_call(
        edges_kernel,
        out_shape=(out, out),
        in_specs=[scalars()] + [vmem] * 6,
        out_specs=(vmem, vmem),
        compiler_params=pltpu.CompilerParams(vmem_limit_bytes=16 << 20),
        name="edges",
    )(side, left, right, lx1, lx2, ix1, ix2)


def jacobi(side, level, flag, divergence, halo):
    vmem, hbm, _ = specs()
    nx, ny, nz = divergence.shape
    ext = (nx + 2 * HALO, 2, ny + 2 * ROWS, 128)
    return pl.pallas_call(
        jacobi_kernel,
        out_shape=jax.ShapeDtypeStruct((nx, ny, nz), f32),
        in_specs=[scalars()] + [hbm] * 7 + [vmem] * (len(halo) - 4),
        out_specs=vmem,
        scratch_shapes=[pltpu.VMEM(ext, f32)] * 6
        + [pltpu.VMEM((nx, 2, ny, 128), jnp.int32), pltpu.SemaphoreType.DMA((9, 2))],
        compiler_params=pltpu.CompilerParams(vmem_limit_bytes=48 << 20),
        name="jacobi",
    )(side, level, flag, divergence, *halo)


def spread_matrix():
    row = jnp.arange(128)
    coord, tile = row // 8 % 3, row % 8
    column = jnp.arange(384)
    hit = (row[:, None] < 72) & (coord[:, None] == column[None, :] // 128)
    hit = hit & (tile[:, None] == column[None, :] % 128 // 16)
    return hit.astype(jnp.bfloat16)


def swap(axis, first, second):
    count = lax.axis_size(axis)
    arrived = []
    for part, start in ((first, 0), (second, 1)):
        pairs = []
        for i in range(start, count - 1, 2):
            pairs += [(i, i + 1), (i + 1, i)]
        arrived.append(lax.ppermute(part, axis, pairs))
    return arrived


def per_device(particle_pos, tile_dest, tile_block, fluid_flag, divergence):
    nx, ny, nz = divergence.shape
    bricks = lax.axis_size("gx") * lax.axis_size("gy")
    side = jnp.stack([lax.axis_index("gx") % 2, lax.axis_index("gy") % 2]).astype(jnp.int32)

    send = pack(tile_dest[:, 0], tile_block, particle_pos, bricks)
    send, flag, div = lax.optimization_barrier((send, fluid_flag, divergence))
    arrived = lax.all_to_all(send, ("gx", "gy"), split_axis=0, concat_axis=0, tiled=True)
    first, second, face1, face2 = strips(side, flag, div)
    ix1, ix2 = swap("gx", first, second)
    iy1, iy2 = swap("gy", face1, face2)
    arrived, iy1, iy2 = lax.optimization_barrier((arrived, iy1, iy2))
    level, sizes, first, second, left, right = splat(side, arrived, nx, ny, nz)
    lx1, lx2 = swap("gx", first, second)
    ly1, ly2 = swap("gy", *edges(side, left, right, lx1, lx2, ix1, ix2))
    pressure = jacobi(side, sizes, flag, div, (lx1, lx2, ix1, ix2, ly1, ly2, iy1, iy2))
    return (level, pressure)


def solution(mesh):
    placed = (
        P(None, ("gx", "gy")),
        P(("gx", "gy"), None),
        P(("gx", "gy")),
        P("gx", "gy", None),
        P("gx", "gy", None),
    )
    return jax.shard_map(
        per_device,
        mesh=mesh,
        in_specs=placed,
        out_specs=(P("gx", "gy", None), P("gx", "gy", None)),
        check_vma=False,
    )
```

```python
import functools

import jax
import jax.numpy as jnp
from jax import lax
from jax.experimental import pallas as pl
from jax.experimental.pallas import tpu as pltpu
from jax.sharding import PartitionSpec as P

BLOCK = 16
TILE = 128
RADIUS = 1.2
BAND = 3.0
WEIGHT = 2.0 / 3.0
FAR = 1.0e9
HALO = 4
ROWS = 8
REACH = RADIUS + BAND + 1.0e-3
PAIRS = 8

f32 = jnp.float32


def ordered(keys, first, second):
    row = lax.broadcasted_iota(jnp.int32, (8, TILE), 0)
    data = [list(keys), list(first), list(second)]
    size = 2
    while size <= TILE:
        if size >= 16 and size < TILE:
            sign = jnp.where((row & (size // 16)) == 0, 1.0, -1.0).astype(f32)
        else:
            sign = None
        gap = size // 2
        while gap >= 1:
            if gap < 16:
                for v in range(16):
                    if v & gap:
                        continue
                    w = v | gap
                    a, b = data[0][v], data[0][w]
                    if sign is not None:
                        swap_now = a * sign > b * sign
                    elif size < 16 and v & size:
                        swap_now = a < b
                    else:
                        swap_now = a > b
                    for part in data:
                        a, b = part[v], part[w]
                        part[v] = jnp.where(swap_now, b, a)
                        part[w] = jnp.where(swap_now, a, b)
            else:
                e = gap // 16
                low = (row & e) == 0
                way = jnp.where(low, 1.0, -1.0).astype(f32)
                if sign is not None:
                    way = way * sign
                for v in range(16):
                    others = []
                    for part in data:
                        if e == 4:
                            others.append(pltpu.roll(part[v], 4, 0))
                        else:
                            others.append(jnp.where(low, pltpu.roll(part[v], 8 - e, 0), pltpu.roll(part[v], e, 0)))
                    take = data[0][v] * way > others[0] * way
                    for part, other in zip(data, others):
                        part[v] = jnp.where(take, other, part[v])
            gap //= 2
        size *= 2
    return data


def pack_kernel(dest_in, block_in, pos_in, send_ref, dest_ref, block_ref, pos_ref, count_ref, tile_ref, turn_ref, sem):
    tiles = block_ref.shape[0]
    copies = [
        pltpu.make_async_copy(a, b, sem.at[n])
        for n, (a, b) in enumerate(((pos_in, pos_ref), (dest_in, dest_ref), (block_in, block_ref)))
    ]
    for copy in copies:
        copy.start()
    lane = lax.broadcasted_iota(jnp.int32, (4, TILE), 1)
    note = (lax.broadcasted_iota(jnp.int32, (4, TILE), 0) == 3) & (lane == 0)

    def clear(i, carry):
        count_ref[i] = 0
        return carry

    lax.fori_loop(0, count_ref.shape[0], clear, 0)
    empty = jnp.where(lane == 0, -1.0, 0.0).astype(f32)
    send_ref[...] = jnp.broadcast_to(empty[None], send_ref.shape)

    copies[0].wait()
    for t in range(tiles):
        tile_ref[0:3, t, :] = pos_ref[:, t * TILE : t * TILE + TILE]
    parts = []
    for c in range(3):
        turned = jnp.transpose(tile_ref[c], (1, 0))
        parts.append([turned[v * 8 : v * 8 + 8, :] for v in range(16)])
    parts = ordered(*parts)
    turn_ref[3] = jnp.zeros((TILE, TILE), f32)
    for k in range(PAIRS):
        below = jnp.zeros((8, TILE), f32)
        upto = jnp.zeros((8, TILE), f32)
        for v in range(16):
            below = below + jnp.where(parts[0][v] < 2 * k + 0.5 - REACH, 1.0, 0.0)
            upto = upto + jnp.where(parts[0][v] < 2 * k + 1.5 + REACH, 1.0, 0.0)
        turn_ref[3, 1 + k : 2 + k, :] = jnp.sum(below, axis=0, keepdims=True) - TILE
        turn_ref[3, 1 + PAIRS + k : 2 + PAIRS + k, :] = -jnp.sum(upto, axis=0, keepdims=True)
    for c in range(3):
        for v in range(16):
            turn_ref[c, pl.ds(v, 8, stride=16), :] = parts[c][v]
    for c in range(4):
        tile_ref[c] = jnp.transpose(turn_ref[c], (1, 0))

    copies[1].wait()
    copies[2].wait()

    def place(t, carry):
        owner = dest_ref[t]
        slot = count_ref[owner]
        count_ref[owner] = slot + 1
        send_ref[owner * 2 + slot] = jnp.where(note, block_ref[t].astype(f32), tile_ref[:, t, :])
        return carry

    lax.fori_loop(0, tiles, place, 0)


def ones_where(condition):
    return jnp.where(condition, 1.0, 0.0).astype(jnp.bfloat16)


def row_to_column(row):
    return jnp.concatenate(
        [
            jnp.transpose(jnp.broadcast_to(row[:, h : h + 128], (128, 128)), (1, 0))
            for h in range(0, row.shape[1], 128)
        ],
        axis=0,
    )


def arrange(notes, note_ref, slot_ref):
    records = notes.shape[0]
    halves = records // 128
    turned = [jnp.transpose(notes[h * 128 : h * 128 + 128, :], (1, 0)) for h in range(halves)]
    labels = jnp.concatenate([v[0:1, :] for v in turned], axis=1)
    shift = [v[1 : 1 + PAIRS] - v[1 + PAIRS : 1 + 2 * PAIRS] for v in turned]
    keys = jnp.concatenate([jnp.sum(v, axis=0, keepdims=True) for v in shift], axis=1)
    valid = labels >= 0.0
    spot = (labels.astype(jnp.int32) & 7).astype(f32)
    column = lax.broadcasted_iota(jnp.int32, (8, records), 0).astype(f32)
    member = jnp.where(valid & (column == spot), 1.0, 0.0)
    from_index = lax.broadcasted_iota(jnp.int32, (records, records), 0)
    to_index = lax.broadcasted_iota(jnp.int32, (records, records), 1)
    earlier = ones_where(from_index < to_index)
    own = row_to_column(keys)
    own = jnp.concatenate([own] * halves, axis=1)
    smaller = (own < keys) | ((own == keys) & (from_index < to_index))
    before = jnp.dot(member.astype(jnp.bfloat16), ones_where(smaller), preferred_element_type=f32)
    rank = jnp.sum(member * before, axis=0, keepdims=True)
    counts = jnp.sum(member, axis=1, keepdims=True)
    total = jnp.sum(counts, axis=0, keepdims=True)
    room = 8.0 * jnp.floor((total + 63.0) * (1.0 / 64.0))
    late = jnp.where(valid & (rank >= room), 1.0, 0.0)
    turn = jnp.dot(jnp.broadcast_to(late, (8, records)).astype(jnp.bfloat16), earlier, preferred_element_type=f32)[0:1]
    used = jnp.minimum(counts, room)
    free = room - used
    offsets = [jnp.zeros((1, 1), f32)]
    for t in range(7):
        offsets.append(offsets[-1] + free[t : t + 1])
    offset = jnp.concatenate(offsets, axis=0)
    chosen = (turn >= offset) & (turn < offset + free)
    moved = jnp.sum(jnp.where(chosen, (used + turn - offset) * 8.0 + column, 0.0), axis=0, keepdims=True)
    slots = jnp.where(valid, jnp.where(late > 0.0, moved, rank * 8.0 + spot), -1.0)
    slot_ref[...] = slots
    lane = lax.broadcasted_iota(jnp.int32, (records, 128), 1).astype(f32)
    raised = jnp.broadcast_to(jnp.where(valid, labels + 1.0, 0.0), (8, records)).astype(jnp.bfloat16)
    late_slots = jnp.broadcast_to(jnp.where(late > 0.0, slots + 1.0, 0.0), (8, records)).astype(jnp.bfloat16)
    to_slot = row_to_column(slots)
    to_turn = row_to_column(jnp.where(late > 0.0, turn, -1.0))
    for h in range(halves):
        here = jnp.dot(raised, ones_where(to_slot == lane + 128.0 * h), preferred_element_type=f32)
        note_ref[h : h + 1, :] = (here[0:1] - 1.0).astype(jnp.int32)
        here = jnp.dot(late_slots, ones_where(to_turn == lane + 128.0 * h), preferred_element_type=f32)
        note_ref[halves + h : halves + h + 1, :] = here[0:1].astype(jnp.int32)
    sums = jnp.where(lane[0:1] == 0.0, total, jnp.sum(late, axis=1, keepdims=True))
    for b in range(records // 64):
        here = jnp.where((slots >= 64.0 * b) & (slots < 64.0 * b + 64.0), late, 0.0)
        sums = jnp.where(lane[0:1] == 2.0 + b, jnp.sum(here, axis=1, keepdims=True), sums)
    note_ref[2 * halves : 2 * halves + 1, :] = sums.astype(jnp.int32)


def strips_kernel(kind_in, div_in, first_ref, second_ref, face1_ref, face2_ref, kx_ref, ky_ref, dy_ref, sem):
    nx, ny, nz = kind_in.shape
    copies = []
    side = lax.axis_index("gx") % 2
    for n, (at, out) in enumerate((((1 - side) * (nx - HALO), first_ref), (side * (nx - HALO), second_ref))):
        planes = pl.ds(at, HALO)
        copies.append(pltpu.make_async_copy(kind_in.at[planes], kx_ref.at[n], sem.at[n]))
        copies.append(pltpu.make_async_copy(div_in.at[planes], out.at[1], sem.at[2 + n]))
    for n, at in enumerate((0, ny - 8)):
        rows = pl.ds(at, 8)
        copies.append(pltpu.make_async_copy(kind_in.at[:, rows, :], ky_ref.at[n], sem.at[4 + n]))
        copies.append(pltpu.make_async_copy(div_in.at[:, rows, :], dy_ref.at[n], sem.at[6 + n]))
    for copy in copies:
        copy.start()
    for copy in copies:
        copy.wait()
    first_ref[0] = kind_of(kx_ref[0])
    second_ref[0] = kind_of(kx_ref[1])
    low = slice(0, HALO)
    high = slice(8 - HALO, 8)
    even = lax.axis_index("gy") % 2 == 0
    for turn, out in ((True, face1_ref), (False, face2_ref)):
        up = even if turn else jnp.logical_not(even)
        out[0] = jnp.where(up, kind_of(ky_ref[1, :, high, :]), kind_of(ky_ref[0, :, low, :]))
        out[1] = jnp.where(up, dy_ref[1, :, high, :], dy_ref[0, :, low, :])


def strips(flag, divergence):
    vmem, hbm, _ = specs()
    nx, ny, nz = divergence.shape
    strip = jax.ShapeDtypeStruct((2, HALO, ny, nz), f32)
    edge = jax.ShapeDtypeStruct((2, nx, HALO, nz), f32)
    return pl.pallas_call(
        strips_kernel,
        out_shape=(strip, strip, edge, edge),
        in_specs=[hbm, hbm],
        out_specs=(vmem,) * 4,
        scratch_shapes=[
            pltpu.VMEM((2, HALO, ny, nz), jnp.int32),
            pltpu.VMEM((2, nx, 8, nz), jnp.int32),
            pltpu.VMEM((2, nx, 8, nz), f32),
            pltpu.SemaphoreType.DMA((8,)),
        ],
        compiler_params=pltpu.CompilerParams(vmem_limit_bytes=60 << 20),
        name="strips",
    )(flag, divergence)


def kind_of(flag):
    return 5.0 - 4.0 * flag.astype(f32)


def splat_kernel(spread_ref, rec_ref, near_ref, first_ref, second_ref, left_ref, right_ref, meta_ref, sem,
                 note_ref, slot_ref, piece_ref, turn_ref, px_ref, py_ref, pz_ref, dyz_ref, acc_ref):
    records = rec_ref.shape[0]
    halves = records // 128
    nx, ny = left_ref.shape[0], first_ref.shape[1]

    notes = rec_ref[:, 3, :]
    arrange(notes, note_ref, slot_ref)
    index = lax.broadcasted_iota(jnp.int32, (records, records), 0).astype(f32)
    to_slot = ones_where(index == slot_ref[...])
    pieces = [[], [], []]
    for c in range(3):
        whole = rec_ref[:, c, :]
        high = whole.astype(jnp.bfloat16)
        rest = whole - high.astype(f32)
        middle = rest.astype(jnp.bfloat16)
        pieces[0].append(high)
        pieces[1].append(middle)
        pieces[2].append((rest - middle.astype(f32)).astype(jnp.bfloat16))
    for n in range(3):
        for c in range(3):
            piece_ref[n * 3 + c] = jnp.dot(to_slot, pieces[n][c], preferred_element_type=f32)
    placed = jnp.dot(to_slot, notes.astype(jnp.bfloat16), preferred_element_type=f32)
    for b in range(records // 64):
        least = jnp.min(placed[b * 64 : b * 64 + 64, :], axis=0, keepdims=True)
        note_ref[2 * halves + 1 + b : 2 * halves + 2 + b, :] = least.astype(jnp.int32)
    copy = pltpu.make_async_copy(note_ref, meta_ref, sem)
    copy.start()
    near_ref[...] = jnp.full(near_ref.shape, FAR, f32)
    turn_ref[...] = jnp.zeros(turn_ref.shape, f32)
    copy.wait()
    batches = (meta_ref[2 * halves, 0] + 63) // 64
    late = meta_ref[2 * halves, 1]

    lane = lax.broadcasted_iota(jnp.int32, (8, 128), 1)
    depth = (lane & 15).astype(f32) + 0.5
    spots = lax.broadcasted_iota(jnp.int32, (1, 128), 1) >> 4

    def batch(g, carry):
        for s in range(8):
            for n in range(9):
                turn_ref[s, n * 8 : n * 8 + 8, :] = piece_ref[n, pl.ds(pl.multiple_of(g * 64 + s * 8, 8), 8), :]
            turned = jnp.transpose(turn_ref[s], (1, 0)).astype(jnp.bfloat16)
            place = jnp.dot(turned, spread_ref[...], preferred_element_type=f32)
            px_ref[pl.ds(s, TILE, stride=8), :] = place[:, 0:128]
            py_ref[pl.ds(s, TILE, stride=8), :] = place[:, 128:256]
            pz_ref[pl.ds(s, TILE, stride=8), :] = place[:, 256:384]

        def prepare(k, inner):
            for u in range(8):
                p = k * 8 + u
                rows = pl.ds(pl.multiple_of(p * 8, 8), 8)
                py = py_ref[rows, :]
                dz = depth - pz_ref[rows, :]
                dz = dz * dz
                for y in range(16):
                    dy = (y + 0.5) - py
                    dyz_ref[p * 16 + y] = dy * dy + dz
            return inner

        lax.fori_loop(0, TILE // 8, prepare, 0)

        for k in range(PAIRS):
            stop = -meta_ref[2 * halves + 1 + g, 1 + PAIRS + k]
            steps = (stop - (meta_ref[2 * halves + 1 + g, 1 + k] + TILE) + 7) // 8
            first = jnp.maximum(stop - steps * 8, 0)

            def step(i, accs):
                accs = list(accs)
                for u in range(4):
                    p = first + i * 8 + u * 2
                    away = []
                    for v in range(2):
                        px = px_ref[pl.ds(pl.multiple_of((p + v) * 8, 8), 8), :]
                        d0 = (2 * k + 0.5) - px
                        d1 = (2 * k + 1.5) - px
                        away.append((d0 * d0, d1 * d1))
                    for y in range(16):
                        one = dyz_ref[p * 16 + y]
                        two = dyz_ref[p * 16 + 16 + y]
                        for x in range(2):
                            both = jnp.minimum(one + away[0][x], two + away[1][x])
                            accs[x * 16 + y] = jnp.minimum(accs[x * 16 + y], both)
                return tuple(accs)

            accs = lax.fori_loop(0, steps, step, tuple(jnp.full((8, 128), FAR, f32) for _ in range(32)))
            for i in range(32):
                acc_ref[(k * 32 + i) * 8 : (k * 32 + i) * 8 + 8, :] = accs[i]

        def put_down(s, t, label, mask, move):
            bx = label // 64
            base = (label // 8 % 2) * ny + bx * (32 * ny) + label // 16 % 4 * 16
            for x in range(16):
                tile = acc_ref[pl.ds(x * 128 + s, 16, stride=8), :]
                tile = pltpu.roll(tile, move, 1)
                rows = pl.ds(pl.multiple_of(base + x * (2 * ny), 16), 16)
                near_ref[rows, :] = jnp.minimum(near_ref[rows, :], jnp.where(mask, tile, FAR))

        def merge(s, inner):
            labels = [meta_ref[g // 2, g % 2 * 64 + s * 8 + t] for t in range(8)]
            wanted = [(label >= 0) & ((label & 7) == t) for t, label in enumerate(labels)]
            masks = [spots == jnp.where(want, t, -1) for t, want in enumerate(wanted)]
            labels = [jnp.maximum(label, 0) for label in labels]
            bases = [v // 8 % 2 * ny + v // 64 * (32 * ny) + v // 16 % 4 * 16 for v in labels]
            for start in range(0, 16, 8):
                tiles = [acc_ref[pl.ds(x * 128 + s, 16, stride=8), :] for x in range(start, start + 8)]
                for mask, base in zip(masks, bases):
                    for x, tile in enumerate(tiles):
                        rows = pl.ds(pl.multiple_of(base + (start + x) * (2 * ny), 16), 16)
                        near_ref[rows, :] = jnp.minimum(near_ref[rows, :], jnp.where(mask, tile, FAR))
            return inner

        lax.fori_loop(0, 8, merge, 0)

        def merge_late(i, inner):
            j = meta_ref[halves + i // 128, i % 128] - 1

            @pl.when(j // 64 == g)
            def _():
                t = j % 8
                label = meta_ref[j // 128, j % 128]
                spot = label & 7
                put_down(j // 8 % 8, t, label, spots == spot, ((spot - t) & 7) * 16)

            return inner

        lax.fori_loop(0, jnp.where(meta_ref[2 * halves, 2 + g] > 0, late, 0), merge_late, 0)
        return carry

    lax.fori_loop(0, batches, batch, 0)

    def size_at(row, rows):
        return jnp.abs(level_of(near_ref[pl.ds(row, rows), :]))

    side = lax.axis_index("gx") % 2
    for at, out in (((1 - side) * (nx - HALO), first_ref), (side * (nx - HALO), second_ref)):
        for i in range(HALO):
            for half in range(2):
                row = pl.multiple_of((at + i) * (2 * ny) + half * ny, ny)
                out[i, :, half * 128 : half * 128 + 128] = size_at(row, ny)
    for x in range(nx):
        for half in range(2):
            lanes = slice(half * 128, half * 128 + 128)
            row = (x * 2 + half) * ny
            left_ref[x, :, lanes] = size_at(row, HALO)
            right_ref[x, :, lanes] = size_at(row + ny - HALO, HALO)


def level_of(near):
    return jnp.minimum(jnp.sqrt(near) - RADIUS, BAND)


def along(pair):
    rows = pair[0].shape[0]
    lane = lax.broadcasted_iota(jnp.int32, (rows, 128), 1)
    first = lane == 0
    last = lane == 127
    up = [pltpu.roll(v, 1, 1) for v in pair]
    down = [pltpu.roll(v, 127, 1) for v in pair]
    return (
        (jnp.where(first, 0.0, up[0]), jnp.where(last, down[1], down[0])),
        (jnp.where(first, up[0], up[1]), jnp.where(last, 0.0, down[1])),
    )


def coefficients(a_ref, u_ref, x, r0, rows):
    at = slice(r0, r0 + rows)
    mags = [a_ref[x, h, at, :] for h in range(2)]
    kinds = [u_ref[x, h, at, :] for h in range(2)]
    za, zu = along(mags), along(kinds)
    result = []
    for h in range(2):
        a, u = mags[h], kinds[h]
        r = 1.0 / jnp.maximum(a, 1e-30)
        diagonal = None
        near = [(za[h][0], zu[h][0]), (za[h][1], zu[h][1])]
        for dx, dy in ((-1, 0), (1, 0), (0, -1), (0, 1)):
            beside = slice(r0 + dy, r0 + dy + rows)
            near.append((a_ref[x + dx, h, beside, :], u_ref[x + dx, h, beside, :]))
        for b, w in near:
            term = jnp.minimum(jnp.maximum(a + b, 1.0) * r, w)
            diagonal = term if diagonal is None else diagonal + term
        result.append(jnp.where(u == 1.0, WEIGHT / jnp.maximum(diagonal, 1.0), 0.0))
    return result


def interior_kernel(near_ref, flag_in, div_in, out_ref, size_ref, kind_ref, c_ref, p_ref, a_ref, u_ref, d_ref, f_ref, sem):
    nx, _, ny, _ = near_ref.shape
    R = ROWS
    copies = []
    for half in range(2):
        lanes = pl.ds(half * 128, 128)
        copies.append(pltpu.make_async_copy(flag_in.at[:, :, lanes], f_ref.at[:, half], sem.at[0, half]))
        copies.append(pltpu.make_async_copy(div_in.at[:, :, lanes], d_ref.at[:, half], sem.at[1, half]))
    for copy in copies:
        copy.start()

    def levels(x, carry):
        for half in range(2):
            level = level_of(near_ref[x, half])
            out_ref[x, :, half * 128 : half * 128 + 128] = level
            size = jnp.abs(level)
            size_ref[x, half] = size
            a_ref[x, half, R : R + ny, :] = size
        return carry

    lax.fori_loop(0, nx, levels, 0, unroll=2)
    for copy in copies:
        copy.wait()

    def convert(x, carry):
        for half in range(2):
            kind = kind_of(f_ref[x, half])
            kind_ref[x, half] = kind
            u_ref[x, half, R : R + ny, :] = kind
        return carry

    lax.fori_loop(0, nx, convert, 0, unroll=2)

    def weigh(x, carry):
        for half, c in enumerate(coefficients(a_ref, u_ref, x, R, ny)):
            c_ref[x, half] = c
            p_ref[x, half, R : R + ny, :] = c * d_ref[x, half]
        return carry

    lax.fori_loop(1, nx - 1, weigh, 0, unroll=2)


def interior(near, flag, divergence):
    vmem, hbm, _ = specs()
    nx, ny, nz = divergence.shape
    whole = jax.ShapeDtypeStruct((nx, 2, ny, 128), f32)
    padded = (nx, 2, ny + 2 * ROWS, 128)
    return pl.pallas_call(
        interior_kernel,
        out_shape=(jax.ShapeDtypeStruct((nx, ny, nz), f32),) + (whole,) * 3 + (jax.ShapeDtypeStruct(padded, f32),),
        in_specs=[vmem, hbm, hbm],
        out_specs=(vmem,) * 5,
        scratch_shapes=[
            pltpu.VMEM(padded, f32),
            pltpu.VMEM(padded, f32),
            pltpu.VMEM(whole.shape, f32),
            pltpu.VMEM(whole.shape, jnp.int32),
            pltpu.SemaphoreType.DMA((2, 2)),
        ],
        compiler_params=pltpu.CompilerParams(vmem_limit_bytes=36 << 20),
        name="interior",
    )(near.reshape(whole.shape), flag, divergence)


def specs():
    return tuple(pl.BlockSpec(memory_space=space) for space in (pltpu.VMEM, pl.ANY, pltpu.HBM))


def pack(dest, block, pos, bricks):
    vmem, _, hbm = specs()
    return pl.pallas_call(
        pack_kernel,
        out_shape=jax.ShapeDtypeStruct((bricks * 2, 4, TILE), f32),
        in_specs=[hbm] * 3,
        out_specs=vmem,
        scratch_shapes=[
            pltpu.SMEM(dest.shape, jnp.int32),
            pltpu.SMEM(block.shape, jnp.int32),
            pltpu.VMEM(pos.shape, f32),
            pltpu.SMEM((bricks,), jnp.int32),
            pltpu.VMEM((4, TILE, TILE), f32),
            pltpu.VMEM((4, TILE, TILE), f32),
            pltpu.SemaphoreType.DMA((3,)),
        ],
        compiler_params=pltpu.CompilerParams(vmem_limit_bytes=60 << 20),
        name="pack",
    )(dest, block, pos)


def splat(arrived, nx, ny, nz):
    vmem, _, _ = specs()
    records = arrived.shape[0]
    strip = jax.ShapeDtypeStruct((HALO, ny, nz), f32)
    edge = jax.ShapeDtypeStruct((nx, HALO, nz), f32)
    return pl.pallas_call(
        splat_kernel,
        out_shape=(
            jax.ShapeDtypeStruct((nx * 2 * ny, 128), f32),
            strip,
            strip,
            edge,
            edge,
        ),
        in_specs=[vmem, vmem],
        out_specs=(vmem,) * 5,
        scratch_shapes=[
            pltpu.SMEM((16, 128), jnp.int32),
            pltpu.SemaphoreType.DMA,
            pltpu.VMEM((16, 128), jnp.int32),
            pltpu.VMEM((1, records), f32),
            pltpu.VMEM((9, records, TILE), f32),
            pltpu.VMEM((8, 128, TILE), f32),
            pltpu.VMEM((TILE * 8, 128), f32),
            pltpu.VMEM((TILE * 8, 128), f32),
            pltpu.VMEM((TILE * 8, 128), f32),
            pltpu.VMEM((TILE * BLOCK, 8, 128), f32),
            pltpu.VMEM((BLOCK * BLOCK * 8, 128), f32),
        ],
        compiler_params=pltpu.CompilerParams(vmem_limit_bytes=28 << 20),
        name="splat",
    )(spread_matrix(), arrived)


def edges_kernel(left_ref, right_ref, lx1_ref, lx2_ref, ix1_ref, ix2_ref, out1_ref, out2_ref):
    nx, H = left_ref.shape[0:2]
    ny = lx1_ref.shape[1]
    side = lax.axis_index("gx") % 2
    even = lax.axis_index("gy") % 2 == 0
    ext = nx + 2 * H
    low = slice(0, H)
    high = slice(ny - H, ny)
    for turn, out in ((True, out1_ref), (False, out2_ref)):
        up = even if turn else jnp.logical_not(even)
        out[H : nx + H] = jnp.where(up, right_ref[...], left_ref[...])
        for at, step, one, two in (
            (0, nx + H, lx1_ref, lx2_ref),
            (ext, H, ix1_ref.at[0], ix2_ref.at[0]),
            (ext + 2 * H, H, ix1_ref.at[1], ix2_ref.at[1]),
        ):
            out[pl.ds(at + (1 - side) * step, H)] = jnp.where(up, one[:, high, :], one[:, low, :])
            out[pl.ds(at + side * step, H)] = jnp.where(up, two[:, high, :], two[:, low, :])


def edges(left, right, lx1, lx2, ix1, ix2):
    vmem, _, _ = specs()
    nx, H, nz = left.shape
    out = jax.ShapeDtypeStruct((nx + 6 * H, H, nz), f32)
    return pl.pallas_call(
        edges_kernel,
        out_shape=(out, out),
        in_specs=[vmem] * 6,
        out_specs=(vmem, vmem),
        compiler_params=pltpu.CompilerParams(vmem_limit_bytes=16 << 20),
        name="edges",
    )(left, right, lx1, lx2, ix1, ix2)


def around(ref, x, r0, rows):
    at = slice(r0, r0 + rows)
    pair = [ref[x, h, at, :] for h in range(2)]
    z = along(pair)
    totals = []
    for h in range(2):
        total = z[h][0] + z[h][1]
        total = total + (ref[x - 1, h, at, :] + ref[x + 1, h, at, :])
        total = total + (ref[x, h, r0 - 1 : r0 - 1 + rows, :] + ref[x, h, r0 + 1 : r0 + 1 + rows, :])
        totals.append(total)
    return pair, totals


def second_sweep(p_ref, c, x, r0, rows):
    own, total = around(p_ref, x, r0, rows)
    return [own[h] * (4.0 / 3.0) + c[h] * total[h] for h in range(2)]


def later_sweep(ref, p, c, x, r0, rows):
    own, total = around(ref, x, r0, rows)
    return [own[h] * (1.0 / 3.0) + p[h] + c[h] * total[h] for h in range(2)]


def middle_kernel(c_ref, p_ref, out_ref, q_ref, r_ref):
    nx, _, ny, _ = c_ref.shape
    R = ROWS
    at = slice(R, R + ny)

    def both(ref, x, rows=slice(None)):
        return [ref[x, h, rows, :] for h in range(2)]

    def second(x, carry):
        for h, v in enumerate(second_sweep(p_ref, both(c_ref, x), x, R, ny)):
            q_ref[x, h, at, :] = v
        return carry

    lax.fori_loop(2, nx - 2, second, 0, unroll=7)

    def third(x, carry):
        for h, v in enumerate(later_sweep(q_ref, both(p_ref, x, at), both(c_ref, x), x, R, ny)):
            r_ref[x, h, at, :] = v
        return carry

    lax.fori_loop(3, nx - 3, third, 0, unroll=13)

    def fourth(x, carry):
        for h, v in enumerate(later_sweep(r_ref, both(p_ref, x, at), both(c_ref, x), x, R, ny)):
            out_ref[x, :, h * 128 : h * 128 + 128] = v
        return carry

    lax.fori_loop(4, nx - 4, fourth, 0, unroll=8)


def middle(c, p):
    vmem, _, _ = specs()
    nx, _, ny, lanes = c.shape
    padded = jax.ShapeDtypeStruct(p.shape, f32)
    return pl.pallas_call(
        middle_kernel,
        out_shape=(jax.ShapeDtypeStruct((nx, ny, 2 * lanes), f32), padded, padded),
        in_specs=[vmem, vmem],
        out_specs=(vmem,) * 3,
        compiler_params=pltpu.CompilerParams(vmem_limit_bytes=24 << 20),
        name="middle",
    )(c, p)


def jacobi_kernel(result_in, size_ref, kind_ref, div_ref, c_in, p_in, q_in, r_in, lx1_ref, lx2_ref, ix1_ref, ix2_ref,
                  ly1_ref, ly2_ref, iy1_ref, iy2_ref, out_ref,
                  a_ref, u_ref, d_ref, c_ref, p_ref, q_ref, r_ref, slab_ref, tile_ref, sem, out_sem):
    nx, _, ny, _ = size_ref.shape
    H = HALO
    R = ROWS
    S = H + 1
    side = lax.axis_index("gx") % 2
    inner = pl.ds(R, ny)
    first_x, second_x = pl.ds((1 - side) * (nx + H), H), pl.ds(side * (nx + H), H)
    copies = []

    def copy(source, target, n, half):
        copies.append(pltpu.make_async_copy(source, target, sem.at[n, half]))
        copies[-1].start()

    shell = ((0, S, 0, ny), (nx - S, S, 0, ny), (S, nx - 2 * S, 0, 8), (S, nx - 2 * S, ny - 8, 8))
    for n, (x, planes, y, rows) in enumerate(shell):
        xs, ys, padded = pl.ds(x, planes), pl.ds(y, rows), pl.ds(y + R, rows)
        at = pl.ds(x + H, planes)
        copy(size_ref.at[xs, :, ys], a_ref.at[at, :, padded], n, 0)
        copy(kind_ref.at[xs, :, ys], u_ref.at[at, :, padded], n, 1)
        for half in range(2):
            copy(div_ref.at[xs, ys, pl.ds(half * 128, 128)], d_ref.at[at, half, padded], 4 + n, half)
        copy(c_in.at[xs, :, ys], c_ref.at[at, :, padded], 8 + n, 0)
        copy(p_in.at[xs, :, padded], p_ref.at[at, :, padded], 8 + n, 1)
    for half in range(2):
        lanes = pl.ds(half * 128, 128)
        for n, (source, target) in enumerate(
            (
                (ix1_ref.at[0], u_ref.at[first_x, half, inner]),
                (ix2_ref.at[0], u_ref.at[second_x, half, inner]),
                (ix1_ref.at[1], d_ref.at[first_x, half, inner]),
                (ix2_ref.at[1], d_ref.at[second_x, half, inner]),
                (lx1_ref, a_ref.at[first_x, half, inner]),
                (lx2_ref, a_ref.at[second_x, half, inner]),
            )
        ):
            copy(source.at[:, :, lanes], target, 16 + n, half)
    ready = len(copies)
    for m, (source, target) in enumerate(((q_in, q_ref), (r_in, r_ref))):
        for n, (x, planes, y, rows) in enumerate(shell):
            xs, padded, at = pl.ds(x, planes), pl.ds(y + R, rows), pl.ds(x + H, planes)
            copy(source.at[xs, :, padded], target.at[at, :, padded], 12 + n, m)
    mid = pl.ds(H, nx - 2 * H)
    copy(result_in.at[mid, pl.ds(0, 8)], tile_ref.at[0], 22, 0)
    copy(result_in.at[mid, pl.ds(ny - 8, 8)], tile_ref.at[1], 22, 1)
    for half in range(2):
        lanes = slice(half * 128, half * 128 + 128)
        for turn, rows in ((1, slice(R - H, R)), (0, slice(R + ny, R + ny + H))):
            first = lax.axis_index("gy") % 2 == turn
            a_ref[:, half, rows, :] = jnp.where(first, ly1_ref[0 : nx + 2 * H, :, lanes], ly2_ref[0 : nx + 2 * H, :, lanes])
            for n, ext in enumerate((u_ref, d_ref)):
                at = nx + 2 * H + n * 2 * H
                corner = jnp.where(first, ly1_ref[at : at + 2 * H, :, lanes], ly2_ref[at : at + 2 * H, :, lanes])
                ext[0:H, half, rows, :] = corner[0:H]
                ext[nx + H : nx + 2 * H, half, rows, :] = corner[H : 2 * H]
                ext[H : nx + H, half, rows, :] = jnp.where(first, iy1_ref[n, :, :, lanes], iy2_ref[n, :, :, lanes])
    for one in copies[:ready]:
        one.wait()

    def over_shell(first, body):
        last = nx + 2 * H - first - H

        def planes(i, carry):
            body(first + i, R - H, ny + 2 * H)
            body(last + i, R - H, ny + 2 * H)
            return carry

        def sides(x, carry):
            body(x, R - H, 8)
            body(x, R + ny - H, 8)
            return carry

        lax.fori_loop(0, H, planes, 0, unroll=2)
        lax.fori_loop(first + H, last, sides, 0, unroll=4)

    def both(ref, x, r0, rows):
        return [ref[x, h, r0 : r0 + rows, :] for h in range(2)]

    def weigh(x, r0, rows):
        at = slice(r0, r0 + rows)
        for half, c in enumerate(coefficients(a_ref, u_ref, x, r0, rows)):
            c_ref[x, half, at, :] = c
            p_ref[x, half, at, :] = c * d_ref[x, half, at, :]

    def second(x, r0, rows):
        for h, v in enumerate(second_sweep(p_ref, both(c_ref, x, r0, rows), x, r0, rows)):
            q_ref[x, h, r0 : r0 + rows, :] = v

    def third(x, r0, rows):
        for h, v in enumerate(later_sweep(q_ref, both(p_ref, x, r0, rows), both(c_ref, x, r0, rows), x, r0, rows)):
            r_ref[x, h, r0 : r0 + rows, :] = v

    over_shell(1, weigh)
    for one in copies[ready:]:
        one.wait()
    over_shell(2, second)
    over_shell(3, third)

    def last(x, r0, rows):
        return later_sweep(r_ref, both(p_ref, x, r0, rows), both(c_ref, x, r0, rows), x, r0, rows)

    def planes(i, carry):
        for n, x in enumerate((H + i, nx + i)):
            for h, v in enumerate(last(x, R, ny)):
                slab_ref[n, i, :, h * 128 : h * 128 + 128] = v
        return carry

    lax.fori_loop(0, H, planes, 0, unroll=2)
    outs = [
        pltpu.make_async_copy(slab_ref.at[n], out_ref.at[pl.ds(x, H)], out_sem.at[n]) for n, x in enumerate((0, nx - H))
    ]
    for one in outs:
        one.start()

    def sides(x, carry):
        for h, v in enumerate(last(x, R - H, 8)):
            tile_ref[0, x - 2 * H, 0:H, h * 128 : h * 128 + 128] = v[H:8]
        for h, v in enumerate(last(x, R + ny - H, 8)):
            tile_ref[1, x - 2 * H, 8 - H : 8, h * 128 : h * 128 + 128] = v[0:H]
        return carry

    lax.fori_loop(2 * H, nx, sides, 0, unroll=4)
    for n, y in enumerate((0, ny - 8)):
        outs.append(pltpu.make_async_copy(tile_ref.at[n], out_ref.at[mid, pl.ds(y, 8)], out_sem.at[2 + n]))
        outs[-1].start()
    for one in outs:
        one.wait()


def jacobi(result, parts, halo):
    vmem, hbm, _ = specs()
    nx, ny, nz = result.shape
    ext = (nx + 2 * HALO, 2, ny + 2 * ROWS, 128)
    return pl.pallas_call(
        jacobi_kernel,
        out_shape=jax.ShapeDtypeStruct((nx, ny, nz), f32),
        in_specs=[hbm] * 12 + [vmem] * 4,
        out_specs=hbm,
        input_output_aliases={0: 0},
        scratch_shapes=[pltpu.VMEM(ext, f32)] * 7
        + [
            pltpu.VMEM((2, HALO, ny, nz), f32),
            pltpu.VMEM((2, nx - 2 * HALO, 8, nz), f32),
            pltpu.SemaphoreType.DMA((23, 2)),
            pltpu.SemaphoreType.DMA((4,)),
        ],
        compiler_params=pltpu.CompilerParams(vmem_limit_bytes=32 << 20),
        name="jacobi",
    )(result, *parts, *halo)


def spread_matrix():
    row = jnp.arange(128)
    coord, tile = row // 8 % 3, row % 8
    column = jnp.arange(384)
    hit = (row[:, None] < 72) & (coord[:, None] == column[None, :] // 128)
    hit = hit & (tile[:, None] == column[None, :] % 128 // 16)
    return hit.astype(jnp.bfloat16)


def swap(axis, first, second):
    count = lax.axis_size(axis)
    arrived = []
    for part, start in ((first, 0), (second, 1)):
        pairs = []
        for i in range(start, count - 1, 2):
            pairs += [(i, i + 1), (i + 1, i)]
        arrived.append(lax.ppermute(part, axis, pairs))
    return arrived


def per_device(particle_pos, tile_dest, tile_block, fluid_flag, divergence):
    nx, ny, nz = divergence.shape
    bricks = lax.axis_size("gx") * lax.axis_size("gy")
    send = pack(tile_dest[:, 0], tile_block, particle_pos, bricks)
    send, flag, div = lax.optimization_barrier((send, fluid_flag, divergence))
    arrived = lax.all_to_all(send, ("gx", "gy"), split_axis=0, concat_axis=0, tiled=True)
    first, second, face1, face2 = strips(flag, div)
    ix1, ix2 = swap("gx", first, second)
    iy1, iy2 = swap("gy", face1, face2)
    arrived, iy1, iy2 = lax.optimization_barrier((arrived, iy1, iy2))
    near, first, second, left, right = splat(arrived, nx, ny, nz)
    lx1, lx2 = swap("gx", first, second)
    level, sizes, kinds, c, p = interior(near, flag, div)
    lx1, lx2, c = lax.optimization_barrier((lx1, lx2, c))
    ly1, ly2 = swap("gy", *edges(left, right, lx1, lx2, ix1, ix2))
    result, q, r = middle(c, p)
    pressure = jacobi(result, (sizes, kinds, div, c, p, q, r), (lx1, lx2, ix1, ix2, ly1, ly2, iy1, iy2))
    return (level, pressure)


def solution(mesh):
    placed = (
        P(None, ("gx", "gy")),
        P(("gx", "gy"), None),
        P(("gx", "gy")),
        P("gx", "gy", None),
        P("gx", "gy", None),
    )
    return jax.shard_map(
        per_device,
        mesh=mesh,
        in_specs=placed,
        out_specs=(P("gx", "gy", None), P("gx", "gy", None)),
        check_vma=False,
    )
```

```python
import functools

import jax
import jax.numpy as jnp
from jax import lax
from jax.experimental import pallas as pl
from jax.experimental.pallas import tpu as pltpu
from jax.sharding import PartitionSpec as P

BLOCK = 16
TILE = 128
RADIUS = 1.2
BAND = 3.0
WEIGHT = 2.0 / 3.0
FAR = 1.0e9
HALO = 4
ROWS = 8
REACH = RADIUS + BAND + 1.0e-3
PAIRS = 8

f32 = jnp.float32


def ordered(keys, first, second):
    row = lax.broadcasted_iota(jnp.int32, (8, TILE), 0)
    data = [list(keys), list(first), list(second)]
    size = 2
    while size <= TILE:
        if size >= 16 and size < TILE:
            sign = jnp.where((row & (size // 16)) == 0, 1.0, -1.0).astype(f32)
        else:
            sign = None
        gap = size // 2
        while gap >= 1:
            if gap < 16:
                for v in range(16):
                    if v & gap:
                        continue
                    w = v | gap
                    a, b = data[0][v], data[0][w]
                    if sign is not None:
                        swap_now = a * sign > b * sign
                    elif size < 16 and v & size:
                        swap_now = a < b
                    else:
                        swap_now = a > b
                    for part in data:
                        a, b = part[v], part[w]
                        part[v] = jnp.where(swap_now, b, a)
                        part[w] = jnp.where(swap_now, a, b)
            else:
                e = gap // 16
                low = (row & e) == 0
                way = jnp.where(low, 1.0, -1.0).astype(f32)
                if sign is not None:
                    way = way * sign
                for v in range(16):
                    others = []
                    for part in data:
                        if e == 4:
                            others.append(pltpu.roll(part[v], 4, 0))
                        else:
                            others.append(jnp.where(low, pltpu.roll(part[v], 8 - e, 0), pltpu.roll(part[v], e, 0)))
                    take = data[0][v] * way > others[0] * way
                    for part, other in zip(data, others):
                        part[v] = jnp.where(take, other, part[v])
            gap //= 2
        size *= 2
    return data


def strip_copies(kind_in, div_in, first_ref, second_ref, kx_ref, ky_ref, dy_ref, sem):
    nx, ny, nz = kind_in.shape
    copies = []
    side = lax.axis_index("gx") % 2
    for n, (at, out) in enumerate((((1 - side) * (nx - HALO), first_ref), (side * (nx - HALO), second_ref))):
        planes = pl.ds(at, HALO)
        copies.append(pltpu.make_async_copy(kind_in.at[planes], kx_ref.at[n], sem.at[n]))
        copies.append(pltpu.make_async_copy(div_in.at[planes], out.at[1], sem.at[2 + n]))
    for n, at in enumerate((0, ny - 8)):
        rows = pl.ds(at, 8)
        copies.append(pltpu.make_async_copy(kind_in.at[:, rows, :], ky_ref.at[n], sem.at[4 + n]))
        copies.append(pltpu.make_async_copy(div_in.at[:, rows, :], dy_ref.at[n], sem.at[6 + n]))
    return copies


def cut_strips(first_ref, second_ref, face1_ref, face2_ref, kx_ref, ky_ref, dy_ref):
    first_ref[0] = kind_of(kx_ref[0])
    second_ref[0] = kind_of(kx_ref[1])
    low = slice(0, HALO)
    high = slice(8 - HALO, 8)
    even = lax.axis_index("gy") % 2 == 0
    for turn, out in ((True, face1_ref), (False, face2_ref)):
        up = even if turn else jnp.logical_not(even)
        out[0] = jnp.where(up, kind_of(ky_ref[1, :, high, :]), kind_of(ky_ref[0, :, low, :]))
        out[1] = jnp.where(up, dy_ref[1, :, high, :], dy_ref[0, :, low, :])


def pack_kernel(dest_in, block_in, pos_in, kind_in, div_in, send_ref, first_ref, second_ref, face1_ref, face2_ref,
                dest_ref, block_ref, pos_ref, count_ref, tile_ref, turn_ref, kx_ref, ky_ref, dy_ref, sem, strip_sem):
    tiles = block_ref.shape[0]
    copies = [
        pltpu.make_async_copy(a, b, sem.at[n])
        for n, (a, b) in enumerate(((pos_in, pos_ref), (dest_in, dest_ref), (block_in, block_ref)))
    ]
    strips = strip_copies(kind_in, div_in, first_ref, second_ref, kx_ref, ky_ref, dy_ref, strip_sem)
    for copy in copies + strips:
        copy.start()
    lane = lax.broadcasted_iota(jnp.int32, (4, TILE), 1)
    note = (lax.broadcasted_iota(jnp.int32, (4, TILE), 0) == 3) & (lane == 0)

    def clear(i, carry):
        count_ref[i] = 0
        return carry

    lax.fori_loop(0, count_ref.shape[0], clear, 0, unroll=16)
    empty = jnp.where(lane == 0, -1.0, 0.0).astype(f32)
    send_ref[...] = jnp.broadcast_to(empty[None], send_ref.shape)

    copies[0].wait()
    for t in range(tiles):
        tile_ref[0:3, t, :] = pos_ref[:, t * TILE : t * TILE + TILE]
    parts = []
    for c in range(3):
        turned = jnp.transpose(tile_ref[c], (1, 0))
        parts.append([turned[v * 8 : v * 8 + 8, :] for v in range(16)])
    parts = ordered(*parts)
    turn_ref[3] = jnp.zeros((TILE, TILE), f32)
    for k in range(PAIRS):
        below = jnp.zeros((8, TILE), f32)
        upto = jnp.zeros((8, TILE), f32)
        for v in range(16):
            below = below + jnp.where(parts[0][v] < 2 * k + 0.5 - REACH, 1.0, 0.0)
            upto = upto + jnp.where(parts[0][v] < 2 * k + 1.5 + REACH, 1.0, 0.0)
        turn_ref[3, 1 + k : 2 + k, :] = jnp.sum(below, axis=0, keepdims=True) - TILE
        turn_ref[3, 1 + PAIRS + k : 2 + PAIRS + k, :] = -jnp.sum(upto, axis=0, keepdims=True)
    for c in range(3):
        for v in range(16):
            turn_ref[c, pl.ds(v, 8, stride=16), :] = parts[c][v]
    for c in range(4):
        tile_ref[c] = jnp.transpose(turn_ref[c], (1, 0))

    for copy in copies[1:] + strips:
        copy.wait()
    cut_strips(first_ref, second_ref, face1_ref, face2_ref, kx_ref, ky_ref, dy_ref)

    def place(t, carry):
        owner = dest_ref[t]
        slot = count_ref[owner]
        count_ref[owner] = slot + 1
        send_ref[owner * 2 + slot] = jnp.where(note, block_ref[t].astype(f32), tile_ref[:, t, :])
        return carry

    lax.fori_loop(0, tiles, place, 0, unroll=16)


def ones_where(condition):
    return jnp.where(condition, 1.0, 0.0).astype(jnp.bfloat16)


def row_to_column(row):
    return jnp.concatenate(
        [
            jnp.transpose(jnp.broadcast_to(row[:, h : h + 128], (128, 128)), (1, 0))
            for h in range(0, row.shape[1], 128)
        ],
        axis=0,
    )


def arrange(notes, note_ref, slot_ref):
    records = notes.shape[0]
    halves = records // 128
    turned = [jnp.transpose(notes[h * 128 : h * 128 + 128, :], (1, 0)) for h in range(halves)]
    labels = jnp.concatenate([v[0:1, :] for v in turned], axis=1)
    shift = [v[1 : 1 + PAIRS] - v[1 + PAIRS : 1 + 2 * PAIRS] for v in turned]
    keys = jnp.concatenate([jnp.sum(v, axis=0, keepdims=True) for v in shift], axis=1)
    valid = labels >= 0.0
    spot = (labels.astype(jnp.int32) & 7).astype(f32)
    column = lax.broadcasted_iota(jnp.int32, (8, records), 0).astype(f32)
    member = jnp.where(valid & (column == spot), 1.0, 0.0)
    from_index = lax.broadcasted_iota(jnp.int32, (records, records), 0)
    to_index = lax.broadcasted_iota(jnp.int32, (records, records), 1)
    earlier = ones_where(from_index < to_index)
    own = row_to_column(keys)
    own = jnp.concatenate([own] * halves, axis=1)
    smaller = (own < keys) | ((own == keys) & (from_index < to_index))
    before = jnp.dot(member.astype(jnp.bfloat16), ones_where(smaller), preferred_element_type=f32)
    rank = jnp.sum(member * before, axis=0, keepdims=True)
    counts = jnp.sum(member, axis=1, keepdims=True)
    total = jnp.sum(counts, axis=0, keepdims=True)
    room = 8.0 * jnp.floor((total + 63.0) * (1.0 / 64.0))
    late = jnp.where(valid & (rank >= room), 1.0, 0.0)
    turn = jnp.dot(jnp.broadcast_to(late, (8, records)).astype(jnp.bfloat16), earlier, preferred_element_type=f32)[0:1]
    used = jnp.minimum(counts, room)
    free = room - used
    offsets = [jnp.zeros((1, 1), f32)]
    for t in range(7):
        offsets.append(offsets[-1] + free[t : t + 1])
    offset = jnp.concatenate(offsets, axis=0)
    chosen = (turn >= offset) & (turn < offset + free)
    moved = jnp.sum(jnp.where(chosen, (used + turn - offset) * 8.0 + column, 0.0), axis=0, keepdims=True)
    slots = jnp.where(valid, jnp.where(late > 0.0, moved, rank * 8.0 + spot), -1.0)
    slot_ref[...] = slots
    lane = lax.broadcasted_iota(jnp.int32, (records, 128), 1).astype(f32)
    raised = jnp.broadcast_to(jnp.where(valid, labels + 1.0, 0.0), (8, records)).astype(jnp.bfloat16)
    late_slots = jnp.broadcast_to(jnp.where(late > 0.0, slots + 1.0, 0.0), (8, records)).astype(jnp.bfloat16)
    to_slot = row_to_column(slots)
    to_turn = row_to_column(jnp.where(late > 0.0, turn, -1.0))
    for h in range(halves):
        here = jnp.dot(raised, ones_where(to_slot == lane + 128.0 * h), preferred_element_type=f32)
        note_ref[h : h + 1, :] = (here[0:1] - 1.0).astype(jnp.int32)
        here = jnp.dot(late_slots, ones_where(to_turn == lane + 128.0 * h), preferred_element_type=f32)
        note_ref[halves + h : halves + h + 1, :] = here[0:1].astype(jnp.int32)
    sums = jnp.where(lane[0:1] == 0.0, total, jnp.sum(late, axis=1, keepdims=True))
    for b in range(records // 64):
        here = jnp.where((slots >= 64.0 * b) & (slots < 64.0 * b + 64.0), late, 0.0)
        sums = jnp.where(lane[0:1] == 2.0 + b, jnp.sum(here, axis=1, keepdims=True), sums)
    note_ref[2 * halves : 2 * halves + 1, :] = sums.astype(jnp.int32)


def kind_of(flag):
    return 5.0 - 4.0 * flag.astype(f32)


def splat_kernel(spread_ref, rec_ref, near_ref, first_ref, second_ref, left_ref, right_ref, meta_ref, sem,
                 note_ref, slot_ref, piece_ref, turn_ref, px_ref, py_ref, pz_ref, dyz_ref, acc_ref):
    records = rec_ref.shape[0]
    halves = records // 128
    nx, ny = left_ref.shape[0], first_ref.shape[1]

    notes = rec_ref[:, 3, :]
    arrange(notes, note_ref, slot_ref)
    index = lax.broadcasted_iota(jnp.int32, (records, records), 0).astype(f32)
    to_slot = ones_where(index == slot_ref[...])
    pieces = [[], [], []]
    for c in range(3):
        whole = rec_ref[:, c, :]
        high = whole.astype(jnp.bfloat16)
        rest = whole - high.astype(f32)
        middle = rest.astype(jnp.bfloat16)
        pieces[0].append(high)
        pieces[1].append(middle)
        pieces[2].append((rest - middle.astype(f32)).astype(jnp.bfloat16))
    for n in range(3):
        for c in range(3):
            piece_ref[n * 3 + c] = jnp.dot(to_slot, pieces[n][c], preferred_element_type=f32)
    placed = jnp.dot(to_slot, notes.astype(jnp.bfloat16), preferred_element_type=f32)
    for b in range(records // 64):
        least = jnp.min(placed[b * 64 : b * 64 + 64, :], axis=0, keepdims=True)
        note_ref[2 * halves + 1 + b : 2 * halves + 2 + b, :] = least.astype(jnp.int32)
    copy = pltpu.make_async_copy(note_ref, meta_ref, sem)
    copy.start()
    near_ref[...] = jnp.full(near_ref.shape, FAR, f32)
    turn_ref[...] = jnp.zeros(turn_ref.shape, f32)
    copy.wait()
    batches = (meta_ref[2 * halves, 0] + 63) // 64
    late = meta_ref[2 * halves, 1]

    lane = lax.broadcasted_iota(jnp.int32, (8, 128), 1)
    depth = (lane & 15).astype(f32) + 0.5
    spots = lax.broadcasted_iota(jnp.int32, (1, 128), 1) >> 4

    def batch(g, carry):
        turns = []
        for s in range(8):
            for n in range(9):
                turn_ref[s, n * 8 : n * 8 + 8, :] = piece_ref[n, pl.ds(pl.multiple_of(g * 64 + s * 8, 8), 8), :]
            turns.append(jnp.transpose(turn_ref[s], (1, 0)).astype(jnp.bfloat16))
        place = jnp.dot(jnp.concatenate(turns, axis=0), spread_ref[...], preferred_element_type=f32)
        for s in range(8):
            at = slice(s * TILE, s * TILE + TILE)
            px_ref[pl.ds(s, TILE, stride=8), :] = place[at, 0:128]
            py_ref[pl.ds(s, TILE, stride=8), :] = place[at, 128:256]
            pz_ref[pl.ds(s, TILE, stride=8), :] = place[at, 256:384]

        def prepare(k, inner):
            for u in range(16):
                p = k * 16 + u
                rows = pl.ds(pl.multiple_of(p * 8, 8), 8)
                py = py_ref[rows, :]
                dz = depth - pz_ref[rows, :]
                dz = dz * dz
                for y in range(16):
                    dy = (y + 0.5) - py
                    dyz_ref[p * 16 + y] = dy * dy + dz
            return inner

        lax.fori_loop(0, TILE // 16, prepare, 0)

        for k in range(PAIRS):
            stop = -meta_ref[2 * halves + 1 + g, 1 + PAIRS + k]
            steps = (stop - (meta_ref[2 * halves + 1 + g, 1 + k] + TILE) + 7) // 8
            first = jnp.maximum(stop - steps * 8, 0)

            def step(i, accs):
                accs = list(accs)
                for u in range(4):
                    p = first + i * 8 + u * 2
                    away = []
                    for v in range(2):
                        px = px_ref[pl.ds(pl.multiple_of((p + v) * 8, 8), 8), :]
                        d0 = (2 * k + 0.5) - px
                        d1 = (2 * k + 1.5) - px
                        away.append((d0 * d0, d1 * d1))
                    for y in range(16):
                        one = dyz_ref[p * 16 + y]
                        two = dyz_ref[p * 16 + 16 + y]
                        for x in range(2):
                            both = jnp.minimum(one + away[0][x], two + away[1][x])
                            accs[x * 16 + y] = jnp.minimum(accs[x * 16 + y], both)
                return tuple(accs)

            accs = lax.fori_loop(0, steps, step, tuple(jnp.full((8, 128), FAR, f32) for _ in range(32)))
            for i in range(32):
                acc_ref[(k * 32 + i) * 8 : (k * 32 + i) * 8 + 8, :] = accs[i]

        def put_down(s, t, label, mask, move):
            bx = label // 64
            base = (label // 8 % 2) * ny + bx * (32 * ny) + label // 16 % 4 * 16
            for x in range(16):
                tile = acc_ref[pl.ds(x * 128 + s, 16, stride=8), :]
                tile = pltpu.roll(tile, move, 1)
                rows = pl.ds(pl.multiple_of(base + x * (2 * ny), 16), 16)
                near_ref[rows, :] = jnp.minimum(near_ref[rows, :], jnp.where(mask, tile, FAR))

        def merge(s, inner):
            labels = [meta_ref[g // 2, g % 2 * 64 + s * 8 + t] for t in range(8)]
            wanted = [(label >= 0) & ((label & 7) == t) for t, label in enumerate(labels)]
            masks = [spots == jnp.where(want, t, -1) for t, want in enumerate(wanted)]
            labels = [jnp.maximum(label, 0) for label in labels]
            bases = [v // 8 % 2 * ny + v // 64 * (32 * ny) + v // 16 % 4 * 16 for v in labels]
            for start in range(0, 16, 8):
                tiles = [acc_ref[pl.ds(x * 128 + s, 16, stride=8), :] for x in range(start, start + 8)]
                for mask, base in zip(masks, bases):
                    for x, tile in enumerate(tiles):
                        rows = pl.ds(pl.multiple_of(base + (start + x) * (2 * ny), 16), 16)
                        near_ref[rows, :] = jnp.minimum(near_ref[rows, :], jnp.where(mask, tile, FAR))
            return inner

        lax.fori_loop(0, 8, merge, 0)

        def merge_late(i, inner):
            j = meta_ref[halves + i // 128, i % 128] - 1
            here = j // 64 == g
            j = jnp.maximum(j, 0)
            t = j % 8
            label = jnp.maximum(meta_ref[j // 128, j % 128], 0)
            spot = label & 7
            put_down(j // 8 % 8, t, label, spots == jnp.where(here, spot, -1), ((spot - t) & 7) * 16)
            return inner

        steps = jnp.where(meta_ref[2 * halves, 2 + g] > 0, (late + 3) // 4, 0)

        def merge_late_four(i, inner):
            for n in range(4):
                merge_late(i * 4 + n, inner)
            return inner

        lax.fori_loop(0, steps, merge_late_four, 0)
        return carry

    lax.fori_loop(0, batches, batch, 0)

    def size_at(row, rows):
        return jnp.abs(level_of(near_ref[pl.ds(row, rows), :]))

    side = lax.axis_index("gx") % 2
    for at, out in (((1 - side) * (nx - HALO), first_ref), (side * (nx - HALO), second_ref)):
        for i in range(HALO):
            for half in range(2):
                row = pl.multiple_of((at + i) * (2 * ny) + half * ny, ny)
                out[i, :, half * 128 : half * 128 + 128] = size_at(row, ny)
    for x in range(nx):
        for half in range(2):
            lanes = slice(half * 128, half * 128 + 128)
            row = (x * 2 + half) * ny
            left_ref[x, :, lanes] = size_at(row, HALO)
            right_ref[x, :, lanes] = size_at(row + ny - HALO, HALO)


def level_of(near):
    return jnp.minimum(jnp.sqrt(near) - RADIUS, BAND)


def along(pair):
    rows = pair[0].shape[0]
    lane = lax.broadcasted_iota(jnp.int32, (rows, 128), 1)
    first = lane == 0
    last = lane == 127
    up = [pltpu.roll(v, 1, 1) for v in pair]
    down = [pltpu.roll(v, 127, 1) for v in pair]
    return (
        (jnp.where(first, 0.0, up[0]), jnp.where(last, down[1], down[0])),
        (jnp.where(first, up[0], up[1]), jnp.where(last, 0.0, down[1])),
    )


def coefficients(a_ref, u_ref, x, r0, rows):
    at = slice(r0, r0 + rows)
    mags = [a_ref[x, h, at, :] for h in range(2)]
    kinds = [u_ref[x, h, at, :] for h in range(2)]
    za, zu = along(mags), along(kinds)
    result = []
    for h in range(2):
        a, u = mags[h], kinds[h]
        r = 1.0 / jnp.maximum(a, 1e-30)
        diagonal = None
        near = [(za[h][0], zu[h][0]), (za[h][1], zu[h][1])]
        for dx, dy in ((-1, 0), (1, 0), (0, -1), (0, 1)):
            beside = slice(r0 + dy, r0 + dy + rows)
            near.append((a_ref[x + dx, h, beside, :], u_ref[x + dx, h, beside, :]))
        for b, w in near:
            term = jnp.minimum(jnp.maximum(a + b, 1.0) * r, w)
            diagonal = term if diagonal is None else diagonal + term
        result.append(jnp.where(u == 1.0, WEIGHT / jnp.maximum(diagonal, 1.0), 0.0))
    return result


def interior_kernel(near_ref, flag_in, div_in, out_ref, size_ref, kind_ref, c_ref, p_ref, a_ref, u_ref, d_ref, f_ref, sem):
    nx, _, ny, _ = near_ref.shape
    R = ROWS
    copies = []
    for half in range(2):
        lanes = pl.ds(half * 128, 128)
        copies.append(pltpu.make_async_copy(flag_in.at[:, :, lanes], f_ref.at[:, half], sem.at[0, half]))
        copies.append(pltpu.make_async_copy(div_in.at[:, :, lanes], d_ref.at[:, half], sem.at[1, half]))
    for copy in copies:
        copy.start()

    def levels(x, carry):
        for half in range(2):
            level = level_of(near_ref[x, half])
            out_ref[x, :, half * 128 : half * 128 + 128] = level
            size = jnp.abs(level)
            size_ref[x, half] = size
            a_ref[x, half, R : R + ny, :] = size
        return carry

    lax.fori_loop(0, nx, levels, 0, unroll=2)
    for copy in copies:
        copy.wait()

    def convert(x, carry):
        for half in range(2):
            kind = kind_of(f_ref[x, half])
            kind_ref[x, half] = kind
            u_ref[x, half, R : R + ny, :] = kind
        return carry

    lax.fori_loop(0, nx, convert, 0, unroll=2)

    def weigh(x, carry):
        for half, c in enumerate(coefficients(a_ref, u_ref, x, R, ny)):
            c_ref[x, half] = c
            p_ref[x, half, R : R + ny, :] = c * d_ref[x, half]
        return carry

    lax.fori_loop(1, nx - 1, weigh, 0, unroll=2)


def interior(near, flag, divergence):
    vmem, hbm, _ = specs()
    nx, ny, nz = divergence.shape
    whole = jax.ShapeDtypeStruct((nx, 2, ny, 128), f32)
    padded = (nx, 2, ny + 2 * ROWS, 128)
    return pl.pallas_call(
        interior_kernel,
        out_shape=(jax.ShapeDtypeStruct((nx, ny, nz), f32),) + (whole,) * 3 + (jax.ShapeDtypeStruct(padded, f32),),
        in_specs=[vmem, hbm, hbm],
        out_specs=(vmem,) * 5,
        scratch_shapes=[
            pltpu.VMEM(padded, f32),
            pltpu.VMEM(padded, f32),
            pltpu.VMEM(whole.shape, f32),
            pltpu.VMEM(whole.shape, jnp.int32),
            pltpu.SemaphoreType.DMA((2, 2)),
        ],
        compiler_params=pltpu.CompilerParams(vmem_limit_bytes=36 << 20),
        name="interior",
    )(near.reshape(whole.shape), flag, divergence)


def specs():
    return tuple(pl.BlockSpec(memory_space=space) for space in (pltpu.VMEM, pl.ANY, pltpu.HBM))


def pack(dest, block, pos, flag, divergence, bricks):
    vmem, _, hbm = specs()
    nx, ny, nz = divergence.shape
    strip = jax.ShapeDtypeStruct((2, HALO, ny, nz), f32)
    edge = jax.ShapeDtypeStruct((2, nx, HALO, nz), f32)
    return pl.pallas_call(
        pack_kernel,
        out_shape=(jax.ShapeDtypeStruct((bricks * 2, 4, TILE), f32), strip, strip, edge, edge),
        in_specs=[hbm] * 5,
        out_specs=(vmem,) * 5,
        scratch_shapes=[
            pltpu.SMEM(dest.shape, jnp.int32),
            pltpu.SMEM(block.shape, jnp.int32),
            pltpu.VMEM(pos.shape, f32),
            pltpu.SMEM((bricks,), jnp.int32),
            pltpu.VMEM((4, TILE, TILE), f32),
            pltpu.VMEM((4, TILE, TILE), f32),
            pltpu.VMEM((2, HALO, ny, nz), jnp.int32),
            pltpu.VMEM((2, nx, 8, nz), jnp.int32),
            pltpu.VMEM((2, nx, 8, nz), f32),
            pltpu.SemaphoreType.DMA((3,)),
            pltpu.SemaphoreType.DMA((8,)),
        ],
        compiler_params=pltpu.CompilerParams(vmem_limit_bytes=60 << 20),
        name="pack",
    )(dest, block, pos, flag, divergence)


def splat(arrived, nx, ny, nz):
    vmem, _, _ = specs()
    records = arrived.shape[0]
    strip = jax.ShapeDtypeStruct((HALO, ny, nz), f32)
    edge = jax.ShapeDtypeStruct((nx, HALO, nz), f32)
    return pl.pallas_call(
        splat_kernel,
        out_shape=(
            jax.ShapeDtypeStruct((nx * 2 * ny, 128), f32),
            strip,
            strip,
            edge,
            edge,
        ),
        in_specs=[vmem, vmem],
        out_specs=(vmem,) * 5,
        scratch_shapes=[
            pltpu.SMEM((16, 128), jnp.int32),
            pltpu.SemaphoreType.DMA,
            pltpu.VMEM((16, 128), jnp.int32),
            pltpu.VMEM((1, records), f32),
            pltpu.VMEM((9, records, TILE), f32),
            pltpu.VMEM((8, 128, TILE), f32),
            pltpu.VMEM((TILE * 8, 128), f32),
            pltpu.VMEM((TILE * 8, 128), f32),
            pltpu.VMEM((TILE * 8, 128), f32),
            pltpu.VMEM((TILE * BLOCK, 8, 128), f32),
            pltpu.VMEM((BLOCK * BLOCK * 8, 128), f32),
        ],
        compiler_params=pltpu.CompilerParams(vmem_limit_bytes=28 << 20),
        name="splat",
    )(spread_matrix(), arrived)


def edges_kernel(left_ref, right_ref, lx1_ref, lx2_ref, ix1_ref, ix2_ref, out1_ref, out2_ref):
    nx, H = left_ref.shape[0:2]
    ny = lx1_ref.shape[1]
    side = lax.axis_index("gx") % 2
    even = lax.axis_index("gy") % 2 == 0
    ext = nx + 2 * H
    low = slice(0, H)
    high = slice(ny - H, ny)
    for turn, out in ((True, out1_ref), (False, out2_ref)):
        up = even if turn else jnp.logical_not(even)
        out[H : nx + H] = jnp.where(up, right_ref[...], left_ref[...])
        for at, step, one, two in (
            (0, nx + H, lx1_ref, lx2_ref),
            (ext, H, ix1_ref.at[0], ix2_ref.at[0]),
            (ext + 2 * H, H, ix1_ref.at[1], ix2_ref.at[1]),
        ):
            out[pl.ds(at + (1 - side) * step, H)] = jnp.where(up, one[:, high, :], one[:, low, :])
            out[pl.ds(at + side * step, H)] = jnp.where(up, two[:, high, :], two[:, low, :])


def edges(left, right, lx1, lx2, ix1, ix2):
    vmem, _, _ = specs()
    nx, H, nz = left.shape
    out = jax.ShapeDtypeStruct((nx + 6 * H, H, nz), f32)
    return pl.pallas_call(
        edges_kernel,
        out_shape=(out, out),
        in_specs=[vmem] * 6,
        out_specs=(vmem, vmem),
        compiler_params=pltpu.CompilerParams(vmem_limit_bytes=16 << 20),
        name="edges",
    )(left, right, lx1, lx2, ix1, ix2)


def around(ref, x, r0, rows):
    at = slice(r0, r0 + rows)
    pair = [ref[x, h, at, :] for h in range(2)]
    z = along(pair)
    totals = []
    for h in range(2):
        total = z[h][0] + z[h][1]
        total = total + (ref[x - 1, h, at, :] + ref[x + 1, h, at, :])
        total = total + (ref[x, h, r0 - 1 : r0 - 1 + rows, :] + ref[x, h, r0 + 1 : r0 + 1 + rows, :])
        totals.append(total)
    return pair, totals


def second_sweep(p_ref, c, x, r0, rows):
    own, total = around(p_ref, x, r0, rows)
    return [own[h] * (4.0 / 3.0) + c[h] * total[h] for h in range(2)]


def later_sweep(ref, p, c, x, r0, rows):
    own, total = around(ref, x, r0, rows)
    return [own[h] * (1.0 / 3.0) + p[h] + c[h] * total[h] for h in range(2)]


def middle_kernel(c_ref, p_ref, out_ref, q_ref, r_ref):
    nx, _, ny, _ = c_ref.shape
    R = ROWS
    at = slice(R, R + ny)

    def both(ref, x, rows=slice(None)):
        return [ref[x, h, rows, :] for h in range(2)]

    def second(x, carry):
        for h, v in enumerate(second_sweep(p_ref, both(c_ref, x), x, R, ny)):
            q_ref[x, h, at, :] = v
        return carry

    lax.fori_loop(2, nx - 2, second, 0, unroll=7)

    def third(x, carry):
        for h, v in enumerate(later_sweep(q_ref, both(p_ref, x, at), both(c_ref, x), x, R, ny)):
            r_ref[x, h, at, :] = v
        return carry

    lax.fori_loop(3, nx - 3, third, 0, unroll=13)

    def fourth(x, carry):
        for h, v in enumerate(later_sweep(r_ref, both(p_ref, x, at), both(c_ref, x), x, R, ny)):
            out_ref[x, :, h * 128 : h * 128 + 128] = v
        return carry

    lax.fori_loop(4, nx - 4, fourth, 0, unroll=8)


def middle(c, p):
    vmem, _, _ = specs()
    nx, _, ny, lanes = c.shape
    padded = jax.ShapeDtypeStruct(p.shape, f32)
    return pl.pallas_call(
        middle_kernel,
        out_shape=(jax.ShapeDtypeStruct((nx, ny, 2 * lanes), f32), padded, padded),
        in_specs=[vmem, vmem],
        out_specs=(vmem,) * 3,
        compiler_params=pltpu.CompilerParams(vmem_limit_bytes=24 << 20),
        name="middle",
    )(c, p)


def jacobi_kernel(result_in, size_ref, kind_ref, div_ref, c_in, p_in, q_in, r_in, lx1_ref, lx2_ref, ix1_ref, ix2_ref,
                  ly1_ref, ly2_ref, iy1_ref, iy2_ref, out_ref,
                  a_ref, u_ref, d_ref, c_ref, p_ref, q_ref, r_ref, slab_ref, tile_ref, sem, out_sem):
    nx, _, ny, _ = size_ref.shape
    H = HALO
    R = ROWS
    S = H + 1
    side = lax.axis_index("gx") % 2
    inner = pl.ds(R, ny)
    first_x, second_x = pl.ds((1 - side) * (nx + H), H), pl.ds(side * (nx + H), H)
    copies = []

    def copy(source, target, n, half):
        copies.append(pltpu.make_async_copy(source, target, sem.at[n, half]))
        copies[-1].start()

    shell = ((0, S, 0, ny), (nx - S, S, 0, ny), (S, nx - 2 * S, 0, 8), (S, nx - 2 * S, ny - 8, 8))
    for n, (x, planes, y, rows) in enumerate(shell):
        xs, ys, padded = pl.ds(x, planes), pl.ds(y, rows), pl.ds(y + R, rows)
        at = pl.ds(x + H, planes)
        copy(size_ref.at[xs, :, ys], a_ref.at[at, :, padded], n, 0)
        copy(kind_ref.at[xs, :, ys], u_ref.at[at, :, padded], n, 1)
        for half in range(2):
            copy(div_ref.at[xs, ys, pl.ds(half * 128, 128)], d_ref.at[at, half, padded], 4 + n, half)
        copy(c_in.at[xs, :, ys], c_ref.at[at, :, padded], 8 + n, 0)
        copy(p_in.at[xs, :, padded], p_ref.at[at, :, padded], 8 + n, 1)
    for half in range(2):
        lanes = pl.ds(half * 128, 128)
        for n, (source, target) in enumerate(
            (
                (ix1_ref.at[0], u_ref.at[first_x, half, inner]),
                (ix2_ref.at[0], u_ref.at[second_x, half, inner]),
                (ix1_ref.at[1], d_ref.at[first_x, half, inner]),
                (ix2_ref.at[1], d_ref.at[second_x, half, inner]),
                (lx1_ref, a_ref.at[first_x, half, inner]),
                (lx2_ref, a_ref.at[second_x, half, inner]),
            )
        ):
            copy(source.at[:, :, lanes], target, 16 + n, half)
    ready = len(copies)
    for m, (source, target) in enumerate(((q_in, q_ref), (r_in, r_ref))):
        for n, (x, planes, y, rows) in enumerate(shell):
            xs, padded, at = pl.ds(x, planes), pl.ds(y + R, rows), pl.ds(x + H, planes)
            copy(source.at[xs, :, padded], target.at[at, :, padded], 12 + n, m)
    mid = pl.ds(H, nx - 2 * H)
    copy(result_in.at[mid, pl.ds(0, 8)], tile_ref.at[0], 22, 0)
    copy(result_in.at[mid, pl.ds(ny - 8, 8)], tile_ref.at[1], 22, 1)
    for half in range(2):
        lanes = slice(half * 128, half * 128 + 128)
        for turn, rows in ((1, slice(R - H, R)), (0, slice(R + ny, R + ny + H))):
            first = lax.axis_index("gy") % 2 == turn
            a_ref[:, half, rows, :] = jnp.where(first, ly1_ref[0 : nx + 2 * H, :, lanes], ly2_ref[0 : nx + 2 * H, :, lanes])
            for n, ext in enumerate((u_ref, d_ref)):
                at = nx + 2 * H + n * 2 * H
                corner = jnp.where(first, ly1_ref[at : at + 2 * H, :, lanes], ly2_ref[at : at + 2 * H, :, lanes])
                ext[0:H, half, rows, :] = corner[0:H]
                ext[nx + H : nx + 2 * H, half, rows, :] = corner[H : 2 * H]
                ext[H : nx + H, half, rows, :] = jnp.where(first, iy1_ref[n, :, :, lanes], iy2_ref[n, :, :, lanes])
    for one in copies[:ready]:
        one.wait()

    def over_shell(first, body):
        last = nx + 2 * H - first - H

        def planes(i, carry):
            body(first + i, R - H, ny + 2 * H)
            body(last + i, R - H, ny + 2 * H)
            return carry

        def sides(x, carry):
            body(x, R - H, 8)
            body(x, R + ny - H, 8)
            return carry

        lax.fori_loop(0, H, planes, 0, unroll=4)
        lax.fori_loop(first + H, last, sides, 0, unroll=8)

    def both(ref, x, r0, rows):
        return [ref[x, h, r0 : r0 + rows, :] for h in range(2)]

    def weigh(x, r0, rows):
        at = slice(r0, r0 + rows)
        for half, c in enumerate(coefficients(a_ref, u_ref, x, r0, rows)):
            c_ref[x, half, at, :] = c
            p_ref[x, half, at, :] = c * d_ref[x, half, at, :]

    def second(x, r0, rows):
        for h, v in enumerate(second_sweep(p_ref, both(c_ref, x, r0, rows), x, r0, rows)):
            q_ref[x, h, r0 : r0 + rows, :] = v

    def third(x, r0, rows):
        for h, v in enumerate(later_sweep(q_ref, both(p_ref, x, r0, rows), both(c_ref, x, r0, rows), x, r0, rows)):
            r_ref[x, h, r0 : r0 + rows, :] = v

    over_shell(1, weigh)
    for one in copies[ready:]:
        one.wait()
    over_shell(2, second)
    over_shell(3, third)

    def last(x, r0, rows):
        return later_sweep(r_ref, both(p_ref, x, r0, rows), both(c_ref, x, r0, rows), x, r0, rows)

    def planes(i, carry):
        for n, x in enumerate((H + i, nx + i)):
            for h, v in enumerate(last(x, R, ny)):
                slab_ref[n, i, :, h * 128 : h * 128 + 128] = v
        return carry

    lax.fori_loop(0, H, planes, 0, unroll=4)
    outs = [
        pltpu.make_async_copy(slab_ref.at[n], out_ref.at[pl.ds(x, H)], out_sem.at[n]) for n, x in enumerate((0, nx - H))
    ]
    for one in outs:
        one.start()

    def sides(x, carry):
        for h, v in enumerate(last(x, R - H, 8)):
            tile_ref[0, x - 2 * H, 0:H, h * 128 : h * 128 + 128] = v[H:8]
        for h, v in enumerate(last(x, R + ny - H, 8)):
            tile_ref[1, x - 2 * H, 8 - H : 8, h * 128 : h * 128 + 128] = v[0:H]
        return carry

    lax.fori_loop(2 * H, nx, sides, 0, unroll=8)
    for n, y in enumerate((0, ny - 8)):
        outs.append(pltpu.make_async_copy(tile_ref.at[n], out_ref.at[mid, pl.ds(y, 8)], out_sem.at[2 + n]))
        outs[-1].start()
    for one in outs:
        one.wait()


def jacobi(result, parts, halo):
    vmem, hbm, _ = specs()
    nx, ny, nz = result.shape
    ext = (nx + 2 * HALO, 2, ny + 2 * ROWS, 128)
    return pl.pallas_call(
        jacobi_kernel,
        out_shape=jax.ShapeDtypeStruct((nx, ny, nz), f32),
        in_specs=[hbm] * 12 + [vmem] * 4,
        out_specs=hbm,
        input_output_aliases={0: 0},
        scratch_shapes=[pltpu.VMEM(ext, f32)] * 7
        + [
            pltpu.VMEM((2, HALO, ny, nz), f32),
            pltpu.VMEM((2, nx - 2 * HALO, 8, nz), f32),
            pltpu.SemaphoreType.DMA((23, 2)),
            pltpu.SemaphoreType.DMA((4,)),
        ],
        compiler_params=pltpu.CompilerParams(vmem_limit_bytes=32 << 20),
        name="jacobi",
    )(result, *parts, *halo)


def spread_matrix():
    row = jnp.arange(128)
    coord, tile = row // 8 % 3, row % 8
    column = jnp.arange(384)
    hit = (row[:, None] < 72) & (coord[:, None] == column[None, :] // 128)
    hit = hit & (tile[:, None] == column[None, :] % 128 // 16)
    return hit.astype(jnp.bfloat16)


def swap(axis, first, second):
    count = lax.axis_size(axis)
    arrived = []
    for part, start in ((first, 0), (second, 1)):
        pairs = []
        for i in range(start, count - 1, 2):
            pairs += [(i, i + 1), (i + 1, i)]
        arrived.append(lax.ppermute(part, axis, pairs))
    return arrived


def per_device(particle_pos, tile_dest, tile_block, fluid_flag, divergence):
    nx, ny, nz = divergence.shape
    bricks = lax.axis_size("gx") * lax.axis_size("gy")
    flag, div = fluid_flag, divergence
    send, first, second, face1, face2 = pack(tile_dest[:, 0], tile_block, particle_pos, flag, div, bricks)
    arrived = lax.all_to_all(send, ("gx", "gy"), split_axis=0, concat_axis=0, tiled=True)
    ix1, ix2 = swap("gx", first, second)
    iy1, iy2 = swap("gy", face1, face2)
    arrived, iy1, iy2 = lax.optimization_barrier((arrived, iy1, iy2))
    near, first, second, left, right = splat(arrived, nx, ny, nz)
    lx1, lx2 = swap("gx", first, second)
    level, sizes, kinds, c, p = interior(near, flag, div)
    lx1, lx2, c = lax.optimization_barrier((lx1, lx2, c))
    ly1, ly2 = swap("gy", *edges(left, right, lx1, lx2, ix1, ix2))
    result, q, r = middle(c, p)
    pressure = jacobi(result, (sizes, kinds, div, c, p, q, r), (lx1, lx2, ix1, ix2, ly1, ly2, iy1, iy2))
    return (level, pressure)


def solution(mesh):
    placed = (
        P(None, ("gx", "gy")),
        P(("gx", "gy"), None),
        P(("gx", "gy")),
        P("gx", "gy", None),
        P("gx", "gy", None),
    )
    return jax.shard_map(
        per_device,
        mesh=mesh,
        in_specs=placed,
        out_specs=(P("gx", "gy", None), P("gx", "gy", None)),
        check_vma=False,
    )
```

```python
import functools

import jax
import jax.numpy as jnp
from jax import lax
from jax.experimental import pallas as pl
from jax.experimental.pallas import tpu as pltpu
from jax.sharding import PartitionSpec as P

BLOCK = 16
TILE = 128
RADIUS = 1.2
BAND = 3.0
WEIGHT = 2.0 / 3.0
FAR = 1.0e9
HALO = 4
ROWS = 8
REACH = RADIUS + BAND + 1.0e-3
PAIRS = 8

f32 = jnp.float32


def ordered(keys, first, second):
    row = lax.broadcasted_iota(jnp.int32, (8, TILE), 0)
    data = [list(keys), list(first), list(second)]
    size = 2
    while size <= TILE:
        if size >= 16 and size < TILE:
            sign = jnp.where((row & (size // 16)) == 0, 1.0, -1.0).astype(f32)
        else:
            sign = None
        gap = size // 2
        while gap >= 1:
            if gap < 16:
                for v in range(16):
                    if v & gap:
                        continue
                    w = v | gap
                    a, b = data[0][v], data[0][w]
                    if sign is not None:
                        swap_now = a * sign > b * sign
                    elif size < 16 and v & size:
                        swap_now = a < b
                    else:
                        swap_now = a > b
                    for part in data:
                        a, b = part[v], part[w]
                        part[v] = jnp.where(swap_now, b, a)
                        part[w] = jnp.where(swap_now, a, b)
            else:
                e = gap // 16
                low = (row & e) == 0
                way = jnp.where(low, 1.0, -1.0).astype(f32)
                if sign is not None:
                    way = way * sign
                for v in range(16):
                    others = []
                    for part in data:
                        if e == 4:
                            others.append(pltpu.roll(part[v], 4, 0))
                        else:
                            others.append(jnp.where(low, pltpu.roll(part[v], 8 - e, 0), pltpu.roll(part[v], e, 0)))
                    take = data[0][v] * way > others[0] * way
                    for part, other in zip(data, others):
                        part[v] = jnp.where(take, other, part[v])
            gap //= 2
        size *= 2
    return data


def strip_copies(kind_in, div_in, first_ref, second_ref, kx_ref, ky_ref, dy_ref, sem):
    nx, ny, nz = kind_in.shape
    copies = []
    side = lax.axis_index("gx") % 2
    for n, (at, out) in enumerate((((1 - side) * (nx - HALO), first_ref), (side * (nx - HALO), second_ref))):
        planes = pl.ds(at, HALO)
        copies.append(pltpu.make_async_copy(kind_in.at[planes], kx_ref.at[n], sem.at[n]))
        copies.append(pltpu.make_async_copy(div_in.at[planes], out.at[1], sem.at[2 + n]))
    for n, at in enumerate((0, ny - 8)):
        rows = pl.ds(at, 8)
        copies.append(pltpu.make_async_copy(kind_in.at[:, rows, :], ky_ref.at[n], sem.at[4 + n]))
        copies.append(pltpu.make_async_copy(div_in.at[:, rows, :], dy_ref.at[n], sem.at[6 + n]))
    return copies


def cut_strips(first_ref, second_ref, face1_ref, face2_ref, kx_ref, ky_ref, dy_ref):
    first_ref[0] = kind_of(kx_ref[0])
    second_ref[0] = kind_of(kx_ref[1])
    low = slice(0, HALO)
    high = slice(8 - HALO, 8)
    even = lax.axis_index("gy") % 2 == 0
    for turn, out in ((True, face1_ref), (False, face2_ref)):
        up = even if turn else jnp.logical_not(even)
        out[0] = jnp.where(up, kind_of(ky_ref[1, :, high, :]), kind_of(ky_ref[0, :, low, :]))
        out[1] = jnp.where(up, dy_ref[1, :, high, :], dy_ref[0, :, low, :])


def pack_kernel(dest_in, block_in, pos_in, kind_in, div_in, send_ref, first_ref, second_ref, face1_ref, face2_ref,
                dest_ref, block_ref, pos_ref, count_ref, tile_ref, turn_ref, kx_ref, ky_ref, dy_ref, sem, strip_sem):
    tiles = block_ref.shape[0]
    copies = [
        pltpu.make_async_copy(a, b, sem.at[n])
        for n, (a, b) in enumerate(((pos_in, pos_ref), (dest_in, dest_ref), (block_in, block_ref)))
    ]
    strips = strip_copies(kind_in, div_in, first_ref, second_ref, kx_ref, ky_ref, dy_ref, strip_sem)
    for copy in copies + strips:
        copy.start()
    lane = lax.broadcasted_iota(jnp.int32, (4, TILE), 1)
    note = (lax.broadcasted_iota(jnp.int32, (4, TILE), 0) == 3) & (lane == 0)

    def clear(i, carry):
        count_ref[i] = 0
        return carry

    lax.fori_loop(0, count_ref.shape[0], clear, 0, unroll=16)
    empty = jnp.where(lane == 0, -1.0, 0.0).astype(f32)
    send_ref[...] = jnp.broadcast_to(empty[None], send_ref.shape)

    copies[0].wait()
    for t in range(tiles):
        tile_ref[0:3, t, :] = pos_ref[:, t * TILE : t * TILE + TILE]
    parts = []
    for c in range(3):
        turned = jnp.transpose(tile_ref[c], (1, 0))
        parts.append([turned[v * 8 : v * 8 + 8, :] for v in range(16)])
    parts = ordered(*parts)
    turn_ref[3] = jnp.zeros((TILE + 16, TILE), f32)
    for k in range(PAIRS):
        below = jnp.zeros((8, TILE), f32)
        upto = jnp.zeros((8, TILE), f32)
        for v in range(16):
            below = below + jnp.where(parts[0][v] < 2 * k + 0.5 - REACH, 1.0, 0.0)
            upto = upto + jnp.where(parts[0][v] < 2 * k + 1.5 + REACH, 1.0, 0.0)
        turn_ref[3, 1 + k : 2 + k, :] = jnp.sum(below, axis=0, keepdims=True) - TILE
        turn_ref[3, 1 + PAIRS + k : 2 + PAIRS + k, :] = -jnp.sum(upto, axis=0, keepdims=True)
    for c in range(3):
        for v in range(16):
            turn_ref[c, pl.ds(v, 8, stride=16), :] = parts[c][v]
    for c in range(4):
        tile_ref[c] = jnp.transpose(turn_ref[c, 0:TILE, :], (1, 0))

    for copy in copies[1:] + strips:
        copy.wait()
    cut_strips(first_ref, second_ref, face1_ref, face2_ref, kx_ref, ky_ref, dy_ref)

    def place(t, carry):
        owner = dest_ref[t]
        slot = count_ref[owner]
        count_ref[owner] = slot + 1
        send_ref[owner * 2 + slot] = jnp.where(note, block_ref[t].astype(f32), tile_ref[:, t, :])
        return carry

    lax.fori_loop(0, tiles, place, 0, unroll=16)


def ones_where(condition):
    return jnp.where(condition, 1.0, 0.0).astype(jnp.bfloat16)


def row_to_column(row):
    return jnp.concatenate(
        [
            jnp.transpose(jnp.broadcast_to(row[:, h : h + 128], (128, 128)), (1, 0))
            for h in range(0, row.shape[1], 128)
        ],
        axis=0,
    )


def arrange(notes, note_ref, slot_ref):
    records = notes.shape[0]
    halves = records // 128
    turned = [jnp.transpose(notes[h * 128 : h * 128 + 128, :], (1, 0)) for h in range(halves)]
    labels = jnp.concatenate([v[0:1, :] for v in turned], axis=1)
    shift = [v[1 : 1 + PAIRS] - v[1 + PAIRS : 1 + 2 * PAIRS] for v in turned]
    keys = jnp.concatenate([jnp.sum(v, axis=0, keepdims=True) for v in shift], axis=1)
    valid = labels >= 0.0
    spot = (labels.astype(jnp.int32) & 7).astype(f32)
    column = lax.broadcasted_iota(jnp.int32, (8, records), 0).astype(f32)
    member = jnp.where(valid & (column == spot), 1.0, 0.0)
    from_index = lax.broadcasted_iota(jnp.int32, (records, records), 0)
    to_index = lax.broadcasted_iota(jnp.int32, (records, records), 1)
    earlier = ones_where(from_index < to_index)
    own = row_to_column(keys)
    own = jnp.concatenate([own] * halves, axis=1)
    smaller = (own < keys) | ((own == keys) & (from_index < to_index))
    before = jnp.dot(member.astype(jnp.bfloat16), ones_where(smaller), preferred_element_type=f32)
    rank = jnp.sum(member * before, axis=0, keepdims=True)
    counts = jnp.sum(member, axis=1, keepdims=True)
    total = jnp.sum(counts, axis=0, keepdims=True)
    room = 8.0 * jnp.floor((total + 63.0) * (1.0 / 64.0))
    late = jnp.where(valid & (rank >= room), 1.0, 0.0)
    turn = jnp.dot(jnp.broadcast_to(late, (8, records)).astype(jnp.bfloat16), earlier, preferred_element_type=f32)[0:1]
    used = jnp.minimum(counts, room)
    free = room - used
    offsets = [jnp.zeros((1, 1), f32)]
    for t in range(7):
        offsets.append(offsets[-1] + free[t : t + 1])
    offset = jnp.concatenate(offsets, axis=0)
    chosen = (turn >= offset) & (turn < offset + free)
    moved = jnp.sum(jnp.where(chosen, (used + turn - offset) * 8.0 + column, 0.0), axis=0, keepdims=True)
    slots = jnp.where(valid, jnp.where(late > 0.0, moved, rank * 8.0 + spot), -1.0)
    slot_ref[...] = slots
    lane = lax.broadcasted_iota(jnp.int32, (records, 128), 1).astype(f32)
    raised = jnp.broadcast_to(jnp.where(valid, labels + 1.0, 0.0), (8, records)).astype(jnp.bfloat16)
    late_slots = jnp.broadcast_to(jnp.where(late > 0.0, slots + 1.0, 0.0), (8, records)).astype(jnp.bfloat16)
    to_slot = row_to_column(slots)
    to_turn = row_to_column(jnp.where(late > 0.0, turn, -1.0))
    for h in range(halves):
        here = jnp.dot(raised, ones_where(to_slot == lane + 128.0 * h), preferred_element_type=f32)
        note_ref[h : h + 1, :] = (here[0:1] - 1.0).astype(jnp.int32)
        here = jnp.dot(late_slots, ones_where(to_turn == lane + 128.0 * h), preferred_element_type=f32)
        note_ref[halves + h : halves + h + 1, :] = here[0:1].astype(jnp.int32)
    sums = jnp.where(lane[0:1] == 0.0, total, jnp.sum(late, axis=1, keepdims=True))
    for b in range(records // 64):
        here = jnp.where((slots >= 64.0 * b) & (slots < 64.0 * b + 64.0), late, 0.0)
        sums = jnp.where(lane[0:1] == 2.0 + b, jnp.sum(here, axis=1, keepdims=True), sums)
    note_ref[2 * halves : 2 * halves + 1, :] = sums.astype(jnp.int32)


def kind_of(flag):
    return 5.0 - 4.0 * flag.astype(f32)


def splat_kernel(spread_ref, rec_ref, near_ref, first_ref, second_ref, left_ref, right_ref, meta_ref, sem,
                 note_ref, slot_ref, piece_ref, turn_ref, px_ref, py_ref, pz_ref, dyz_ref, acc_ref):
    records = rec_ref.shape[0]
    halves = records // 128
    nx, ny = left_ref.shape[0], first_ref.shape[1]

    notes = rec_ref[:, 3, :]
    arrange(notes, note_ref, slot_ref)
    index = lax.broadcasted_iota(jnp.int32, (records, records), 0).astype(f32)
    to_slot = ones_where(index == slot_ref[...])
    pieces = [[], [], []]
    for c in range(3):
        whole = rec_ref[:, c, :]
        high = whole.astype(jnp.bfloat16)
        rest = whole - high.astype(f32)
        middle = rest.astype(jnp.bfloat16)
        pieces[0].append(high)
        pieces[1].append(middle)
        pieces[2].append((rest - middle.astype(f32)).astype(jnp.bfloat16))
    for n in range(3):
        for c in range(3):
            piece_ref[n * 3 + c] = jnp.dot(to_slot, pieces[n][c], preferred_element_type=f32)
    placed = jnp.dot(to_slot, notes.astype(jnp.bfloat16), preferred_element_type=f32)
    for b in range(records // 64):
        least = jnp.min(placed[b * 64 : b * 64 + 64, :], axis=0, keepdims=True)
        note_ref[2 * halves + 1 + b : 2 * halves + 2 + b, :] = least.astype(jnp.int32)
    copy = pltpu.make_async_copy(note_ref, meta_ref, sem)
    copy.start()
    near_ref[...] = jnp.full(near_ref.shape, FAR, f32)
    turn_ref[...] = jnp.zeros(turn_ref.shape, f32)
    copy.wait()
    batches = (meta_ref[2 * halves, 0] + 63) // 64
    late = meta_ref[2 * halves, 1]

    lane = lax.broadcasted_iota(jnp.int32, (8, 128), 1)
    depth = (lane & 15).astype(f32) + 0.5
    spots = lax.broadcasted_iota(jnp.int32, (1, 128), 1) >> 4

    def batch(g, carry):
        turns = []
        for s in range(8):
            for n in range(9):
                turn_ref[s, n * 8 : n * 8 + 8, :] = piece_ref[n, pl.ds(pl.multiple_of(g * 64 + s * 8, 8), 8), :]
            turns.append(jnp.transpose(turn_ref[s], (1, 0)).astype(jnp.bfloat16))
        place = jnp.dot(jnp.concatenate(turns, axis=0), spread_ref[...], preferred_element_type=f32)
        for s in range(8):
            at = slice(s * TILE, s * TILE + TILE)
            px_ref[pl.ds(s, TILE, stride=8), :] = place[at, 0:128]
            py_ref[pl.ds(s, TILE, stride=8), :] = place[at, 128:256]
            pz_ref[pl.ds(s, TILE, stride=8), :] = place[at, 256:384]

        def prepare(k, inner):
            for u in range(16):
                p = k * 16 + u
                rows = pl.ds(pl.multiple_of(p * 8, 8), 8)
                py = py_ref[rows, :]
                dz = depth - pz_ref[rows, :]
                dz = dz * dz
                for y in range(16):
                    dy = (y + 0.5) - py
                    dyz_ref[p * 16 + y] = dy * dy + dz
            return inner

        lax.fori_loop(0, TILE // 16, prepare, 0)

        for k in range(PAIRS):
            stop = -meta_ref[2 * halves + 1 + g, 1 + PAIRS + k]
            steps = (stop - (meta_ref[2 * halves + 1 + g, 1 + k] + TILE) + 7) // 8
            first = jnp.maximum(stop - steps * 8, 0)

            def step(i, accs):
                accs = list(accs)
                for u in range(4):
                    p = first + i * 8 + u * 2
                    away = []
                    for v in range(2):
                        px = px_ref[pl.ds(pl.multiple_of((p + v) * 8, 8), 8), :]
                        d0 = (2 * k + 0.5) - px
                        d1 = (2 * k + 1.5) - px
                        away.append((d0 * d0, d1 * d1))
                    for y in range(16):
                        one = dyz_ref[p * 16 + y]
                        two = dyz_ref[p * 16 + 16 + y]
                        for x in range(2):
                            both = jnp.minimum(one + away[0][x], two + away[1][x])
                            accs[x * 16 + y] = jnp.minimum(accs[x * 16 + y], both)
                return tuple(accs)

            accs = lax.fori_loop(0, steps, step, tuple(jnp.full((8, 128), FAR, f32) for _ in range(32)))
            for i in range(32):
                acc_ref[(k * 32 + i) * 8 : (k * 32 + i) * 8 + 8, :] = accs[i]

        def put_down(s, t, label, mask, move):
            bx = label // 64
            base = (label // 8 % 2) * ny + bx * (32 * ny) + label // 16 % 4 * 16
            for x in range(16):
                tile = acc_ref[pl.ds(x * 128 + s, 16, stride=8), :]
                tile = pltpu.roll(tile, move, 1)
                rows = pl.ds(pl.multiple_of(base + x * (2 * ny), 16), 16)
                near_ref[rows, :] = jnp.minimum(near_ref[rows, :], jnp.where(mask, tile, FAR))

        def merge(s, inner):
            labels = [meta_ref[g // 2, g % 2 * 64 + s * 8 + t] for t in range(8)]
            wanted = [(label >= 0) & ((label & 7) == t) for t, label in enumerate(labels)]
            masks = [spots == jnp.where(want, t, -1) for t, want in enumerate(wanted)]
            labels = [jnp.maximum(label, 0) for label in labels]
            bases = [v // 8 % 2 * ny + v // 64 * (32 * ny) + v // 16 % 4 * 16 for v in labels]
            for start in range(0, 16, 8):
                tiles = [acc_ref[pl.ds(x * 128 + s, 16, stride=8), :] for x in range(start, start + 8)]
                for mask, base in zip(masks, bases):
                    for x, tile in enumerate(tiles):
                        rows = pl.ds(pl.multiple_of(base + (start + x) * (2 * ny), 16), 16)
                        near_ref[rows, :] = jnp.minimum(near_ref[rows, :], jnp.where(mask, tile, FAR))
            return inner

        lax.fori_loop(0, 8, merge, 0)

        def merge_late(i, inner):
            j = meta_ref[halves + i // 128, i % 128] - 1
            here = j // 64 == g
            j = jnp.maximum(j, 0)
            t = j % 8
            label = jnp.maximum(meta_ref[j // 128, j % 128], 0)
            spot = label & 7
            put_down(j // 8 % 8, t, label, spots == jnp.where(here, spot, -1), ((spot - t) & 7) * 16)
            return inner

        steps = jnp.where(meta_ref[2 * halves, 2 + g] > 0, (late + 3) // 4, 0)

        def merge_late_four(i, inner):
            for n in range(4):
                merge_late(i * 4 + n, inner)
            return inner

        lax.fori_loop(0, steps, merge_late_four, 0)
        return carry

    lax.fori_loop(0, batches, batch, 0)

    def size_at(row, rows):
        return jnp.abs(level_of(near_ref[pl.ds(row, rows), :]))

    side = lax.axis_index("gx") % 2
    for at, out in (((1 - side) * (nx - HALO), first_ref), (side * (nx - HALO), second_ref)):
        for i in range(HALO):
            for half in range(2):
                row = pl.multiple_of((at + i) * (2 * ny) + half * ny, ny)
                out[i, :, half * 128 : half * 128 + 128] = size_at(row, ny)
    for x in range(nx):
        for half in range(2):
            lanes = slice(half * 128, half * 128 + 128)
            row = (x * 2 + half) * ny
            left_ref[x, :, lanes] = size_at(row, HALO)
            right_ref[x, :, lanes] = size_at(row + ny - HALO, HALO)


def level_of(near):
    return jnp.minimum(jnp.sqrt(near) - RADIUS, BAND)


def along(pair):
    rows = pair[0].shape[0]
    lane = lax.broadcasted_iota(jnp.int32, (rows, 128), 1)
    first = lane == 0
    last = lane == 127
    up = [pltpu.roll(v, 1, 1) for v in pair]
    down = [pltpu.roll(v, 127, 1) for v in pair]
    return (
        (jnp.where(first, 0.0, up[0]), jnp.where(last, down[1], down[0])),
        (jnp.where(first, up[0], up[1]), jnp.where(last, 0.0, down[1])),
    )


def coefficients(a_ref, u_ref, x, r0, rows):
    at = slice(r0, r0 + rows)
    mags = [a_ref[x, h, at, :] for h in range(2)]
    kinds = [u_ref[x, h, at, :] for h in range(2)]
    za, zu = along(mags), along(kinds)
    result = []
    for h in range(2):
        a, u = mags[h], kinds[h]
        r = 1.0 / jnp.maximum(a, 1e-30)
        diagonal = None
        near = [(za[h][0], zu[h][0]), (za[h][1], zu[h][1])]
        for dx, dy in ((-1, 0), (1, 0), (0, -1), (0, 1)):
            beside = slice(r0 + dy, r0 + dy + rows)
            near.append((a_ref[x + dx, h, beside, :], u_ref[x + dx, h, beside, :]))
        for b, w in near:
            term = jnp.minimum(jnp.maximum(a + b, 1.0) * r, w)
            diagonal = term if diagonal is None else diagonal + term
        result.append(jnp.where(u == 1.0, WEIGHT / jnp.maximum(diagonal, 1.0), 0.0))
    return result


def interior_kernel(near_ref, flag_in, div_in, out_ref, size_ref, kind_ref, c_ref, p_ref, a_ref, u_ref, d_ref, f_ref, sem):
    nx, _, ny, _ = near_ref.shape
    R = ROWS
    copies = []
    for half in range(2):
        lanes = pl.ds(half * 128, 128)
        copies.append(pltpu.make_async_copy(flag_in.at[:, :, lanes], f_ref.at[:, half], sem.at[0, half]))
        copies.append(pltpu.make_async_copy(div_in.at[:, :, lanes], d_ref.at[:, half], sem.at[1, half]))
    for copy in copies:
        copy.start()

    def levels(x, carry):
        for half in range(2):
            level = level_of(near_ref[x, half])
            out_ref[x, :, half * 128 : half * 128 + 128] = level
            size = jnp.abs(level)
            size_ref[x, half] = size
            a_ref[x, half, R : R + ny, :] = size
        return carry

    lax.fori_loop(0, nx, levels, 0, unroll=2)
    for copy in copies:
        copy.wait()

    def convert(x, carry):
        for half in range(2):
            kind = kind_of(f_ref[x, half])
            kind_ref[x, half] = kind
            u_ref[x, half, R : R + ny, :] = kind
        return carry

    lax.fori_loop(0, nx, convert, 0, unroll=2)

    def weigh(x, carry):
        for half, c in enumerate(coefficients(a_ref, u_ref, x, R, ny)):
            c_ref[x, half] = c
            p_ref[x, half, R : R + ny, :] = c * d_ref[x, half]
        return carry

    lax.fori_loop(1, nx - 1, weigh, 0, unroll=2)


def interior(near, flag, divergence):
    vmem, hbm, _ = specs()
    nx, ny, nz = divergence.shape
    whole = jax.ShapeDtypeStruct((nx, 2, ny, 128), f32)
    padded = (nx, 2, ny + 2 * ROWS, 128)
    return pl.pallas_call(
        interior_kernel,
        out_shape=(jax.ShapeDtypeStruct((nx, ny, nz), f32),) + (whole,) * 3 + (jax.ShapeDtypeStruct(padded, f32),),
        in_specs=[vmem, hbm, hbm],
        out_specs=(vmem,) * 5,
        scratch_shapes=[
            pltpu.VMEM(padded, f32),
            pltpu.VMEM(padded, f32),
            pltpu.VMEM(whole.shape, f32),
            pltpu.VMEM(whole.shape, jnp.int32),
            pltpu.SemaphoreType.DMA((2, 2)),
        ],
        compiler_params=pltpu.CompilerParams(vmem_limit_bytes=36 << 20),
        name="interior",
    )(near.reshape(whole.shape), flag, divergence)


def specs():
    return tuple(pl.BlockSpec(memory_space=space) for space in (pltpu.VMEM, pl.ANY, pltpu.HBM))


def pack(dest, block, pos, flag, divergence, bricks):
    vmem, _, hbm = specs()
    nx, ny, nz = divergence.shape
    strip = jax.ShapeDtypeStruct((2, HALO, ny, nz), f32)
    edge = jax.ShapeDtypeStruct((2, nx, HALO, nz), f32)
    return pl.pallas_call(
        pack_kernel,
        out_shape=(jax.ShapeDtypeStruct((bricks * 2, 4, TILE), f32), strip, strip, edge, edge),
        in_specs=[hbm] * 5,
        out_specs=(vmem,) * 5,
        scratch_shapes=[
            pltpu.SMEM(dest.shape, jnp.int32),
            pltpu.SMEM(block.shape, jnp.int32),
            pltpu.VMEM(pos.shape, f32),
            pltpu.SMEM((bricks,), jnp.int32),
            pltpu.VMEM((4, TILE, TILE), f32),
            pltpu.VMEM((4, TILE + 16, TILE), f32),
            pltpu.VMEM((2, HALO, ny, nz), jnp.int32),
            pltpu.VMEM((2, nx, 8, nz), jnp.int32),
            pltpu.VMEM((2, nx, 8, nz), f32),
            pltpu.SemaphoreType.DMA((3,)),
            pltpu.SemaphoreType.DMA((8,)),
        ],
        compiler_params=pltpu.CompilerParams(vmem_limit_bytes=60 << 20),
        name="pack",
    )(dest, block, pos, flag, divergence)


def splat(arrived, nx, ny, nz):
    vmem, _, _ = specs()
    records = arrived.shape[0]
    strip = jax.ShapeDtypeStruct((HALO, ny, nz), f32)
    edge = jax.ShapeDtypeStruct((nx, HALO, nz), f32)
    return pl.pallas_call(
        splat_kernel,
        out_shape=(
            jax.ShapeDtypeStruct((nx * 2 * ny, 128), f32),
            strip,
            strip,
            edge,
            edge,
        ),
        in_specs=[vmem, vmem],
        out_specs=(vmem,) * 5,
        scratch_shapes=[
            pltpu.SMEM((16, 128), jnp.int32),
            pltpu.SemaphoreType.DMA,
            pltpu.VMEM((16, 128), jnp.int32),
            pltpu.VMEM((1, records), f32),
            pltpu.VMEM((9, records, TILE), f32),
            pltpu.VMEM((8, 128, TILE), f32),
            pltpu.VMEM((TILE * 8 + 8, 128), f32),
            pltpu.VMEM((TILE * 8 + 8, 128), f32),
            pltpu.VMEM((TILE * 8 + 8, 128), f32),
            pltpu.VMEM((TILE * BLOCK, 8, 128), f32),
            pltpu.VMEM((BLOCK * BLOCK * 8 + 8, 128), f32),
        ],
        compiler_params=pltpu.CompilerParams(vmem_limit_bytes=28 << 20),
        name="splat",
    )(spread_matrix(), arrived)


def edges_kernel(left_ref, right_ref, lx1_ref, lx2_ref, ix1_ref, ix2_ref, out1_ref, out2_ref):
    nx, H = left_ref.shape[0:2]
    ny = lx1_ref.shape[1]
    side = lax.axis_index("gx") % 2
    even = lax.axis_index("gy") % 2 == 0
    ext = nx + 2 * H
    low = slice(0, H)
    high = slice(ny - H, ny)
    for turn, out in ((True, out1_ref), (False, out2_ref)):
        up = even if turn else jnp.logical_not(even)
        out[H : nx + H] = jnp.where(up, right_ref[...], left_ref[...])
        for at, step, one, two in (
            (0, nx + H, lx1_ref, lx2_ref),
            (ext, H, ix1_ref.at[0], ix2_ref.at[0]),
            (ext + 2 * H, H, ix1_ref.at[1], ix2_ref.at[1]),
        ):
            out[pl.ds(at + (1 - side) * step, H)] = jnp.where(up, one[:, high, :], one[:, low, :])
            out[pl.ds(at + side * step, H)] = jnp.where(up, two[:, high, :], two[:, low, :])


def edges(left, right, lx1, lx2, ix1, ix2):
    vmem, _, _ = specs()
    nx, H, nz = left.shape
    out = jax.ShapeDtypeStruct((nx + 6 * H, H, nz), f32)
    return pl.pallas_call(
        edges_kernel,
        out_shape=(out, out),
        in_specs=[vmem] * 6,
        out_specs=(vmem, vmem),
        compiler_params=pltpu.CompilerParams(vmem_limit_bytes=16 << 20),
        name="edges",
    )(left, right, lx1, lx2, ix1, ix2)


def around(ref, x, r0, rows):
    at = slice(r0, r0 + rows)
    pair = [ref[x, h, at, :] for h in range(2)]
    z = along(pair)
    totals = []
    for h in range(2):
        total = z[h][0] + z[h][1]
        total = total + (ref[x - 1, h, at, :] + ref[x + 1, h, at, :])
        total = total + (ref[x, h, r0 - 1 : r0 - 1 + rows, :] + ref[x, h, r0 + 1 : r0 + 1 + rows, :])
        totals.append(total)
    return pair, totals


def second_sweep(p_ref, c, x, r0, rows):
    own, total = around(p_ref, x, r0, rows)
    return [own[h] * (4.0 / 3.0) + c[h] * total[h] for h in range(2)]


def later_sweep(ref, p, c, x, r0, rows):
    own, total = around(ref, x, r0, rows)
    return [own[h] * (1.0 / 3.0) + p[h] + c[h] * total[h] for h in range(2)]


def middle_kernel(c_ref, p_ref, out_ref, q_ref, r_ref):
    nx, _, ny, _ = c_ref.shape
    R = ROWS
    at = slice(R, R + ny)

    def both(ref, x, rows=slice(None)):
        return [ref[x, h, rows, :] for h in range(2)]

    def second(x, carry):
        for h, v in enumerate(second_sweep(p_ref, both(c_ref, x), x, R, ny)):
            q_ref[x, h, at, :] = v
        return carry

    lax.fori_loop(2, nx - 2, second, 0, unroll=7)

    def third(x, carry):
        for h, v in enumerate(later_sweep(q_ref, both(p_ref, x, at), both(c_ref, x), x, R, ny)):
            r_ref[x, h, at, :] = v
        return carry

    lax.fori_loop(3, nx - 3, third, 0, unroll=13)

    def fourth(x, carry):
        for h, v in enumerate(later_sweep(r_ref, both(p_ref, x, at), both(c_ref, x), x, R, ny)):
            out_ref[x, :, h * 128 : h * 128 + 128] = v
        return carry

    lax.fori_loop(4, nx - 4, fourth, 0, unroll=8)


def middle(c, p):
    vmem, _, _ = specs()
    nx, _, ny, lanes = c.shape
    padded = jax.ShapeDtypeStruct(p.shape, f32)
    return pl.pallas_call(
        middle_kernel,
        out_shape=(jax.ShapeDtypeStruct((nx, ny, 2 * lanes), f32), padded, padded),
        in_specs=[vmem, vmem],
        out_specs=(vmem,) * 3,
        compiler_params=pltpu.CompilerParams(vmem_limit_bytes=24 << 20),
        name="middle",
    )(c, p)


def jacobi_kernel(result_in, size_ref, kind_ref, div_ref, c_in, p_in, q_in, r_in, lx1_ref, lx2_ref, ix1_ref, ix2_ref,
                  ly1_ref, ly2_ref, iy1_ref, iy2_ref, out_ref,
                  a_ref, u_ref, d_ref, c_ref, p_ref, q_ref, r_ref, slab_ref, tile_ref, sem, out_sem):
    nx, _, ny, _ = size_ref.shape
    H = HALO
    R = ROWS
    S = H + 1
    side = lax.axis_index("gx") % 2
    inner = pl.ds(R, ny)
    first_x, second_x = pl.ds((1 - side) * (nx + H), H), pl.ds(side * (nx + H), H)
    copies = []

    def copy(source, target, n, half):
        copies.append(pltpu.make_async_copy(source, target, sem.at[n, half]))
        copies[-1].start()

    shell = ((0, S, 0, ny), (nx - S, S, 0, ny), (S, nx - 2 * S, 0, 8), (S, nx - 2 * S, ny - 8, 8))
    for n, (x, planes, y, rows) in enumerate(shell):
        xs, ys, padded = pl.ds(x, planes), pl.ds(y, rows), pl.ds(y + R, rows)
        at = pl.ds(x + H, planes)
        copy(size_ref.at[xs, :, ys], a_ref.at[at, :, padded], n, 0)
        copy(kind_ref.at[xs, :, ys], u_ref.at[at, :, padded], n, 1)
        for half in range(2):
            copy(div_ref.at[xs, ys, pl.ds(half * 128, 128)], d_ref.at[at, half, padded], 4 + n, half)
        copy(c_in.at[xs, :, ys], c_ref.at[at, :, padded], 8 + n, 0)
        copy(p_in.at[xs, :, padded], p_ref.at[at, :, padded], 8 + n, 1)
    for half in range(2):
        lanes = pl.ds(half * 128, 128)
        for n, (source, target) in enumerate(
            (
                (ix1_ref.at[0], u_ref.at[first_x, half, inner]),
                (ix2_ref.at[0], u_ref.at[second_x, half, inner]),
                (ix1_ref.at[1], d_ref.at[first_x, half, inner]),
                (ix2_ref.at[1], d_ref.at[second_x, half, inner]),
                (lx1_ref, a_ref.at[first_x, half, inner]),
                (lx2_ref, a_ref.at[second_x, half, inner]),
            )
        ):
            copy(source.at[:, :, lanes], target, 16 + n, half)
    ready = len(copies)
    for m, (source, target) in enumerate(((q_in, q_ref), (r_in, r_ref))):
        for n, (x, planes, y, rows) in enumerate(shell):
            xs, padded, at = pl.ds(x, planes), pl.ds(y + R, rows), pl.ds(x + H, planes)
            copy(source.at[xs, :, padded], target.at[at, :, padded], 12 + n, m)
    mid = pl.ds(H, nx - 2 * H)
    copy(result_in.at[mid, pl.ds(0, 8)], tile_ref.at[0], 22, 0)
    copy(result_in.at[mid, pl.ds(ny - 8, 8)], tile_ref.at[1], 22, 1)
    for half in range(2):
        lanes = slice(half * 128, half * 128 + 128)
        for turn, rows in ((1, slice(R - H, R)), (0, slice(R + ny, R + ny + H))):
            first = lax.axis_index("gy") % 2 == turn
            a_ref[:, half, rows, :] = jnp.where(first, ly1_ref[0 : nx + 2 * H, :, lanes], ly2_ref[0 : nx + 2 * H, :, lanes])
            for n, ext in enumerate((u_ref, d_ref)):
                at = nx + 2 * H + n * 2 * H
                corner = jnp.where(first, ly1_ref[at : at + 2 * H, :, lanes], ly2_ref[at : at + 2 * H, :, lanes])
                ext[0:H, half, rows, :] = corner[0:H]
                ext[nx + H : nx + 2 * H, half, rows, :] = corner[H : 2 * H]
                ext[H : nx + H, half, rows, :] = jnp.where(first, iy1_ref[n, :, :, lanes], iy2_ref[n, :, :, lanes])
    for one in copies[:ready]:
        one.wait()

    def over_shell(first, body):
        last = nx + 2 * H - first - H

        def planes(i, carry):
            body(first + i, R - H, ny + 2 * H)
            body(last + i, R - H, ny + 2 * H)
            return carry

        def sides(x, carry):
            body(x, R - H, 8)
            body(x, R + ny - H, 8)
            return carry

        lax.fori_loop(0, H, planes, 0, unroll=4)
        lax.fori_loop(first + H, last, sides, 0, unroll=8)

    def both(ref, x, r0, rows):
        return [ref[x, h, r0 : r0 + rows, :] for h in range(2)]

    def weigh(x, r0, rows):
        at = slice(r0, r0 + rows)
        for half, c in enumerate(coefficients(a_ref, u_ref, x, r0, rows)):
            c_ref[x, half, at, :] = c
            p_ref[x, half, at, :] = c * d_ref[x, half, at, :]

    def second(x, r0, rows):
        for h, v in enumerate(second_sweep(p_ref, both(c_ref, x, r0, rows), x, r0, rows)):
            q_ref[x, h, r0 : r0 + rows, :] = v

    def third(x, r0, rows):
        for h, v in enumerate(later_sweep(q_ref, both(p_ref, x, r0, rows), both(c_ref, x, r0, rows), x, r0, rows)):
            r_ref[x, h, r0 : r0 + rows, :] = v

    over_shell(1, weigh)
    for one in copies[ready:]:
        one.wait()
    over_shell(2, second)
    over_shell(3, third)

    def last(x, r0, rows):
        return later_sweep(r_ref, both(p_ref, x, r0, rows), both(c_ref, x, r0, rows), x, r0, rows)

    def planes(i, carry):
        for n, x in enumerate((H + i, nx + i)):
            for h, v in enumerate(last(x, R, ny)):
                slab_ref[n, i, :, h * 128 : h * 128 + 128] = v
        return carry

    lax.fori_loop(0, H, planes, 0, unroll=4)
    outs = [
        pltpu.make_async_copy(slab_ref.at[n], out_ref.at[pl.ds(x, H)], out_sem.at[n]) for n, x in enumerate((0, nx - H))
    ]
    for one in outs:
        one.start()

    def sides(x, carry):
        for h, v in enumerate(last(x, R - H, 8)):
            tile_ref[0, x - 2 * H, 0:H, h * 128 : h * 128 + 128] = v[H:8]
        for h, v in enumerate(last(x, R + ny - H, 8)):
            tile_ref[1, x - 2 * H, 8 - H : 8, h * 128 : h * 128 + 128] = v[0:H]
        return carry

    lax.fori_loop(2 * H, nx, sides, 0, unroll=8)
    for n, y in enumerate((0, ny - 8)):
        outs.append(pltpu.make_async_copy(tile_ref.at[n], out_ref.at[mid, pl.ds(y, 8)], out_sem.at[2 + n]))
        outs[-1].start()
    for one in outs:
        one.wait()


def jacobi(result, parts, halo):
    vmem, hbm, _ = specs()
    nx, ny, nz = result.shape
    ext = (nx + 2 * HALO, 2, ny + 2 * ROWS, 128)
    return pl.pallas_call(
        jacobi_kernel,
        out_shape=jax.ShapeDtypeStruct((nx, ny, nz), f32),
        in_specs=[hbm] * 12 + [vmem] * 4,
        out_specs=hbm,
        input_output_aliases={0: 0},
        scratch_shapes=[pltpu.VMEM(ext, f32)] * 7
        + [
            pltpu.VMEM((2, HALO, ny, nz), f32),
            pltpu.VMEM((2, nx - 2 * HALO, 8, nz), f32),
            pltpu.SemaphoreType.DMA((23, 2)),
            pltpu.SemaphoreType.DMA((4,)),
        ],
        compiler_params=pltpu.CompilerParams(vmem_limit_bytes=32 << 20),
        name="jacobi",
    )(result, *parts, *halo)


def spread_matrix():
    row = jnp.arange(128)
    coord, tile = row // 8 % 3, row % 8
    column = jnp.arange(384)
    hit = (row[:, None] < 72) & (coord[:, None] == column[None, :] // 128)
    hit = hit & (tile[:, None] == column[None, :] % 128 // 16)
    return hit.astype(jnp.bfloat16)


def swap(axis, first, second):
    count = lax.axis_size(axis)
    arrived = []
    for part, start in ((first, 0), (second, 1)):
        pairs = []
        for i in range(start, count - 1, 2):
            pairs += [(i, i + 1), (i + 1, i)]
        arrived.append(lax.ppermute(part, axis, pairs))
    return arrived


def per_device(particle_pos, tile_dest, tile_block, fluid_flag, divergence):
    nx, ny, nz = divergence.shape
    bricks = lax.axis_size("gx") * lax.axis_size("gy")
    flag, div = fluid_flag, divergence
    send, first, second, face1, face2 = pack(tile_dest[:, 0], tile_block, particle_pos, flag, div, bricks)
    arrived = lax.all_to_all(send, ("gx", "gy"), split_axis=0, concat_axis=0, tiled=True)
    ix1, ix2 = swap("gx", first, second)
    iy1, iy2 = swap("gy", face1, face2)
    arrived, iy1, iy2 = lax.optimization_barrier((arrived, iy1, iy2))
    near, first, second, left, right = splat(arrived, nx, ny, nz)
    lx1, lx2 = swap("gx", first, second)
    level, sizes, kinds, c, p = interior(near, flag, div)
    lx1, lx2, c = lax.optimization_barrier((lx1, lx2, c))
    ly1, ly2 = swap("gy", *edges(left, right, lx1, lx2, ix1, ix2))
    result, q, r = middle(c, p)
    pressure = jacobi(result, (sizes, kinds, div, c, p, q, r), (lx1, lx2, ix1, ix2, ly1, ly2, iy1, iy2))
    return (level, pressure)


def solution(mesh):
    placed = (
        P(None, ("gx", "gy")),
        P(("gx", "gy"), None),
        P(("gx", "gy")),
        P("gx", "gy", None),
        P("gx", "gy", None),
    )
    return jax.shard_map(
        per_device,
        mesh=mesh,
        in_specs=placed,
        out_specs=(P("gx", "gy", None), P("gx", "gy", None)),
        check_vma=False,
    )
```

```python
import functools

import jax
import jax.numpy as jnp
from jax import lax
from jax.experimental import pallas as pl
from jax.experimental.pallas import tpu as pltpu
from jax.sharding import PartitionSpec as P

BLOCK = 16
TILE = 128
RADIUS = 1.2
BAND = 3.0
WEIGHT = 2.0 / 3.0
FAR = 1.0e9
HALO = 4
ROWS = 8
REACH = RADIUS + BAND + 1.0e-3
PAIRS = 8

f32 = jnp.float32


def ordered(keys, first, second):
    row = lax.broadcasted_iota(jnp.int32, (8, TILE), 0)
    data = [list(keys), list(first), list(second)]
    size = 2
    while size <= TILE:
        if size >= 16 and size < TILE:
            sign = jnp.where((row & (size // 16)) == 0, 1.0, -1.0).astype(f32)
        else:
            sign = None
        gap = size // 2
        while gap >= 1:
            if gap < 16:
                for v in range(16):
                    if v & gap:
                        continue
                    w = v | gap
                    a, b = data[0][v], data[0][w]
                    if sign is not None:
                        swap_now = a * sign > b * sign
                    elif size < 16 and v & size:
                        swap_now = a < b
                    else:
                        swap_now = a > b
                    for part in data:
                        a, b = part[v], part[w]
                        part[v] = jnp.where(swap_now, b, a)
                        part[w] = jnp.where(swap_now, a, b)
            else:
                e = gap // 16
                low = (row & e) == 0
                way = jnp.where(low, 1.0, -1.0).astype(f32)
                if sign is not None:
                    way = way * sign
                for v in range(16):
                    others = []
                    for part in data:
                        if e == 4:
                            others.append(pltpu.roll(part[v], 4, 0))
                        else:
                            others.append(jnp.where(low, pltpu.roll(part[v], 8 - e, 0), pltpu.roll(part[v], e, 0)))
                    take = data[0][v] * way > others[0] * way
                    for part, other in zip(data, others):
                        part[v] = jnp.where(take, other, part[v])
            gap //= 2
        size *= 2
    return data


def strip_copies(kind_in, div_in, first_ref, second_ref, kx_ref, ky_ref, dy_ref, sem):
    nx, ny, nz = kind_in.shape
    copies = []
    side = lax.axis_index("gx") % 2
    for n, (at, out) in enumerate((((1 - side) * (nx - HALO), first_ref), (side * (nx - HALO), second_ref))):
        planes = pl.ds(at, HALO)
        copies.append(pltpu.make_async_copy(kind_in.at[planes], kx_ref.at[n], sem.at[n]))
        copies.append(pltpu.make_async_copy(div_in.at[planes], out.at[1], sem.at[2 + n]))
    for n, at in enumerate((0, ny - 8)):
        rows = pl.ds(at, 8)
        copies.append(pltpu.make_async_copy(kind_in.at[:, rows, :], ky_ref.at[n], sem.at[4 + n]))
        copies.append(pltpu.make_async_copy(div_in.at[:, rows, :], dy_ref.at[n], sem.at[6 + n]))
    return copies


def cut_strips(first_ref, second_ref, face1_ref, face2_ref, kx_ref, ky_ref, dy_ref):
    first_ref[0] = kind_of(kx_ref[0])
    second_ref[0] = kind_of(kx_ref[1])
    low = slice(0, HALO)
    high = slice(8 - HALO, 8)
    even = lax.axis_index("gy") % 2 == 0
    for turn, out in ((True, face1_ref), (False, face2_ref)):
        up = even if turn else jnp.logical_not(even)
        out[0] = jnp.where(up, kind_of(ky_ref[1, :, high, :]), kind_of(ky_ref[0, :, low, :]))
        out[1] = jnp.where(up, dy_ref[1, :, high, :], dy_ref[0, :, low, :])


def pack_kernel(dest_in, block_in, pos_in, kind_in, div_in, send_ref, first_ref, second_ref, face1_ref, face2_ref,
                dest_ref, block_ref, pos_ref, count_ref, tile_ref, turn_ref, kx_ref, ky_ref, dy_ref, sem, strip_sem):
    tiles = block_ref.shape[0]
    copies = [
        pltpu.make_async_copy(a, b, sem.at[n])
        for n, (a, b) in enumerate(((pos_in, pos_ref), (dest_in, dest_ref), (block_in, block_ref)))
    ]
    strips = strip_copies(kind_in, div_in, first_ref, second_ref, kx_ref, ky_ref, dy_ref, strip_sem)
    for copy in copies + strips:
        copy.start()
    lane = lax.broadcasted_iota(jnp.int32, (4, TILE), 1)
    note = (lax.broadcasted_iota(jnp.int32, (4, TILE), 0) == 3) & (lane == 0)

    def clear(i, carry):
        count_ref[i] = 0
        return carry

    lax.fori_loop(0, count_ref.shape[0], clear, 0, unroll=16)
    empty = jnp.where(lane == 0, -1.0, 0.0).astype(f32)
    send_ref[...] = jnp.broadcast_to(empty[None], send_ref.shape)

    copies[0].wait()
    for t in range(tiles):
        tile_ref[0:3, t, :] = pos_ref[:, t * TILE : t * TILE + TILE]
    parts = []
    for c in range(3):
        turned = jnp.transpose(tile_ref[c], (1, 0))
        parts.append([turned[v * 8 : v * 8 + 8, :] for v in range(16)])
    parts = ordered(*parts)
    turn_ref[3] = jnp.zeros((TILE + 16, TILE), f32)
    for k in range(PAIRS):
        below = jnp.zeros((8, TILE), f32)
        upto = jnp.zeros((8, TILE), f32)
        for v in range(16):
            below = below + jnp.where(parts[0][v] < 2 * k + 0.5 - REACH, 1.0, 0.0)
            upto = upto + jnp.where(parts[0][v] < 2 * k + 1.5 + REACH, 1.0, 0.0)
        turn_ref[3, 1 + k : 2 + k, :] = jnp.sum(below, axis=0, keepdims=True) - TILE
        turn_ref[3, 1 + PAIRS + k : 2 + PAIRS + k, :] = -jnp.sum(upto, axis=0, keepdims=True)
    for c in range(3):
        for v in range(16):
            turn_ref[c, pl.ds(v, 8, stride=16), :] = parts[c][v]
    for c in range(4):
        tile_ref[c] = jnp.transpose(turn_ref[c, 0:TILE, :], (1, 0))

    for copy in copies[1:] + strips:
        copy.wait()
    cut_strips(first_ref, second_ref, face1_ref, face2_ref, kx_ref, ky_ref, dy_ref)

    def place(t, carry):
        owner = dest_ref[t]
        slot = count_ref[owner]
        count_ref[owner] = slot + 1
        send_ref[owner * 2 + slot] = jnp.where(note, block_ref[t].astype(f32), tile_ref[:, t, :])
        return carry

    lax.fori_loop(0, tiles, place, 0, unroll=16)


def ones_where(condition):
    return jnp.where(condition, 1.0, 0.0).astype(jnp.bfloat16)


def row_to_column(row):
    return jnp.concatenate(
        [
            jnp.transpose(jnp.broadcast_to(row[:, h : h + 128], (128, 128)), (1, 0))
            for h in range(0, row.shape[1], 128)
        ],
        axis=0,
    )


def arrange(notes, note_ref, slot_ref):
    records = notes.shape[0]
    halves = records // 128
    turned = [jnp.transpose(notes[h * 128 : h * 128 + 128, :], (1, 0)) for h in range(halves)]
    labels = jnp.concatenate([v[0:1, :] for v in turned], axis=1)
    shift = [v[1 : 1 + PAIRS] - v[1 + PAIRS : 1 + 2 * PAIRS] for v in turned]
    keys = jnp.concatenate([jnp.sum(v, axis=0, keepdims=True) for v in shift], axis=1)
    valid = labels >= 0.0
    spot = (labels.astype(jnp.int32) & 7).astype(f32)
    column = lax.broadcasted_iota(jnp.int32, (8, records), 0).astype(f32)
    member = jnp.where(valid & (column == spot), 1.0, 0.0)
    from_index = lax.broadcasted_iota(jnp.int32, (records, records), 0)
    to_index = lax.broadcasted_iota(jnp.int32, (records, records), 1)
    earlier = ones_where(from_index < to_index)
    own = row_to_column(keys)
    own = jnp.concatenate([own] * halves, axis=1)
    smaller = (own < keys) | ((own == keys) & (from_index < to_index))
    before = jnp.dot(member.astype(jnp.bfloat16), ones_where(smaller), preferred_element_type=f32)
    rank = jnp.sum(member * before, axis=0, keepdims=True)
    counts = jnp.sum(member, axis=1, keepdims=True)
    total = jnp.sum(counts, axis=0, keepdims=True)
    room = 8.0 * jnp.floor((total + 63.0) * (1.0 / 64.0))
    late = jnp.where(valid & (rank >= room), 1.0, 0.0)
    turn = jnp.dot(jnp.broadcast_to(late, (8, records)).astype(jnp.bfloat16), earlier, preferred_element_type=f32)[0:1]
    used = jnp.minimum(counts, room)
    free = room - used
    offsets = [jnp.zeros((1, 1), f32)]
    for t in range(7):
        offsets.append(offsets[-1] + free[t : t + 1])
    offset = jnp.concatenate(offsets, axis=0)
    chosen = (turn >= offset) & (turn < offset + free)
    moved = jnp.sum(jnp.where(chosen, (used + turn - offset) * 8.0 + column, 0.0), axis=0, keepdims=True)
    slots = jnp.where(valid, jnp.where(late > 0.0, moved, rank * 8.0 + spot), -1.0)
    slot_ref[...] = slots
    lane = lax.broadcasted_iota(jnp.int32, (records, 128), 1).astype(f32)
    raised = jnp.broadcast_to(jnp.where(valid, labels + 1.0, 0.0), (8, records)).astype(jnp.bfloat16)
    late_slots = jnp.broadcast_to(jnp.where(late > 0.0, slots + 1.0, 0.0), (8, records)).astype(jnp.bfloat16)
    to_slot = row_to_column(slots)
    to_turn = row_to_column(jnp.where(late > 0.0, turn, -1.0))
    for h in range(halves):
        here = jnp.dot(raised, ones_where(to_slot == lane + 128.0 * h), preferred_element_type=f32)
        note_ref[h : h + 1, :] = (here[0:1] - 1.0).astype(jnp.int32)
        here = jnp.dot(late_slots, ones_where(to_turn == lane + 128.0 * h), preferred_element_type=f32)
        note_ref[halves + h : halves + h + 1, :] = here[0:1].astype(jnp.int32)
    sums = jnp.where(lane[0:1] == 0.0, total, jnp.sum(late, axis=1, keepdims=True))
    for b in range(records // 64):
        here = jnp.where((slots >= 64.0 * b) & (slots < 64.0 * b + 64.0), late, 0.0)
        sums = jnp.where(lane[0:1] == 2.0 + b, jnp.sum(here, axis=1, keepdims=True), sums)
    note_ref[2 * halves : 2 * halves + 1, :] = sums.astype(jnp.int32)


def kind_of(flag):
    return 5.0 - 4.0 * flag.astype(f32)


def splat_kernel(spread_ref, rec_ref, near_ref, first_ref, second_ref, left_ref, right_ref, meta_ref, sem,
                 note_ref, slot_ref, piece_ref, turn_ref, px_ref, py_ref, pz_ref, dyz_ref, acc_ref):
    records = rec_ref.shape[0]
    halves = records // 128
    nx, ny = left_ref.shape[0], first_ref.shape[1]

    notes = rec_ref[:, 3, :]
    arrange(notes, note_ref, slot_ref)
    index = lax.broadcasted_iota(jnp.int32, (records, records), 0).astype(f32)
    to_slot = ones_where(index == slot_ref[...])
    pieces = [[], [], []]
    for c in range(3):
        whole = rec_ref[:, c, :]
        high = whole.astype(jnp.bfloat16)
        rest = whole - high.astype(f32)
        middle = rest.astype(jnp.bfloat16)
        pieces[0].append(high)
        pieces[1].append(middle)
        pieces[2].append((rest - middle.astype(f32)).astype(jnp.bfloat16))
    for n in range(3):
        for c in range(3):
            piece_ref[n * 3 + c] = jnp.dot(to_slot, pieces[n][c], preferred_element_type=f32)
    placed = jnp.dot(to_slot, notes.astype(jnp.bfloat16), preferred_element_type=f32)
    for b in range(records // 64):
        least = jnp.min(placed[b * 64 : b * 64 + 64, :], axis=0, keepdims=True)
        note_ref[2 * halves + 1 + b : 2 * halves + 2 + b, :] = least.astype(jnp.int32)
    copy = pltpu.make_async_copy(note_ref, meta_ref, sem)
    copy.start()
    near_ref[...] = jnp.full(near_ref.shape, FAR, f32)
    turn_ref[...] = jnp.zeros(turn_ref.shape, f32)
    copy.wait()
    batches = (meta_ref[2 * halves, 0] + 63) // 64
    late = meta_ref[2 * halves, 1]

    lane = lax.broadcasted_iota(jnp.int32, (8, 128), 1)
    depth = (lane & 15).astype(f32) + 0.5
    spots = lax.broadcasted_iota(jnp.int32, (1, 128), 1) >> 4

    def batch(g, carry):
        turns = []
        for s in range(8):
            for n in range(9):
                turn_ref[s, n * 8 : n * 8 + 8, :] = piece_ref[n, pl.ds(pl.multiple_of(g * 64 + s * 8, 8), 8), :]
            turns.append(jnp.transpose(turn_ref[s], (1, 0)).astype(jnp.bfloat16))
        place = jnp.dot(jnp.concatenate(turns, axis=0), spread_ref[...], preferred_element_type=f32)
        for s in range(8):
            at = slice(s * TILE, s * TILE + TILE)
            px_ref[pl.ds(s, TILE, stride=8), :] = place[at, 0:128]
            py_ref[pl.ds(s, TILE, stride=8), :] = place[at, 128:256]
            pz_ref[pl.ds(s, TILE, stride=8), :] = place[at, 256:384]

        def prepare(k, inner):
            for u in range(16):
                p = k * 16 + u
                rows = pl.ds(pl.multiple_of(p * 8, 8), 8)
                py = py_ref[rows, :]
                dz = depth - pz_ref[rows, :]
                dz = dz * dz
                for y in range(16):
                    dy = (y + 0.5) - py
                    dyz_ref[p * 16 + y] = dy * dy + dz
            return inner

        lax.fori_loop(0, TILE // 16, prepare, 0)

        for k in range(PAIRS):
            stop = -meta_ref[2 * halves + 1 + g, 1 + PAIRS + k]
            steps = (stop - (meta_ref[2 * halves + 1 + g, 1 + k] + TILE) + 7) // 8
            first = jnp.maximum(stop - steps * 8, 0)

            def step(i, accs):
                accs = list(accs)
                for u in range(4):
                    p = first + i * 8 + u * 2
                    away = []
                    for v in range(2):
                        px = px_ref[pl.ds(pl.multiple_of((p + v) * 8, 8), 8), :]
                        d0 = (2 * k + 0.5) - px
                        d1 = (2 * k + 1.5) - px
                        away.append((d0 * d0, d1 * d1))
                    for y in range(16):
                        one = dyz_ref[p * 16 + y]
                        two = dyz_ref[p * 16 + 16 + y]
                        for x in range(2):
                            both = jnp.minimum(one + away[0][x], two + away[1][x])
                            accs[x * 16 + y] = jnp.minimum(accs[x * 16 + y], both)
                return tuple(accs)

            accs = lax.fori_loop(0, steps, step, tuple(jnp.full((8, 128), FAR, f32) for _ in range(32)))
            for i in range(32):
                acc_ref[(k * 32 + i) * 8 : (k * 32 + i) * 8 + 8, :] = accs[i]

        def put_down(s, t, label, mask, move):
            bx = label // 64
            base = (label // 8 % 2) * ny + bx * (32 * ny) + label // 16 % 4 * 16
            for x in range(16):
                tile = acc_ref[pl.ds(x * 128 + s, 16, stride=8), :]
                tile = pltpu.roll(tile, move, 1)
                rows = pl.ds(pl.multiple_of(base + x * (2 * ny), 16), 16)
                near_ref[rows, :] = jnp.minimum(near_ref[rows, :], jnp.where(mask, tile, FAR))

        def merge(s, inner):
            labels = [meta_ref[g // 2, g % 2 * 64 + s * 8 + t] for t in range(8)]
            wanted = [(label >= 0) & ((label & 7) == t) for t, label in enumerate(labels)]
            masks = [spots == jnp.where(want, t, -1) for t, want in enumerate(wanted)]
            labels = [jnp.maximum(label, 0) for label in labels]
            bases = [v // 8 % 2 * ny + v // 64 * (32 * ny) + v // 16 % 4 * 16 for v in labels]
            for start in range(0, 16, 8):
                tiles = [acc_ref[pl.ds(x * 128 + s, 16, stride=8), :] for x in range(start, start + 8)]
                for mask, base in zip(masks, bases):
                    for x, tile in enumerate(tiles):
                        rows = pl.ds(pl.multiple_of(base + (start + x) * (2 * ny), 16), 16)
                        near_ref[rows, :] = jnp.minimum(near_ref[rows, :], jnp.where(mask, tile, FAR))
            return inner

        lax.fori_loop(0, 8, merge, 0, unroll=2)

        def merge_late(i, inner):
            j = meta_ref[halves + i // 128, i % 128] - 1
            here = j // 64 == g
            j = jnp.maximum(j, 0)
            t = j % 8
            label = jnp.maximum(meta_ref[j // 128, j % 128], 0)
            spot = label & 7
            put_down(j // 8 % 8, t, label, spots == jnp.where(here, spot, -1), ((spot - t) & 7) * 16)
            return inner

        steps = jnp.where(meta_ref[2 * halves, 2 + g] > 0, (late + 3) // 4, 0)

        def merge_late_four(i, inner):
            for n in range(4):
                merge_late(i * 4 + n, inner)
            return inner

        lax.fori_loop(0, steps, merge_late_four, 0)
        return carry

    lax.fori_loop(0, batches, batch, 0)

    def size_at(row, rows):
        return jnp.abs(level_of(near_ref[pl.ds(row, rows), :]))

    side = lax.axis_index("gx") % 2
    for at, out in (((1 - side) * (nx - HALO), first_ref), (side * (nx - HALO), second_ref)):
        for i in range(HALO):
            for half in range(2):
                row = pl.multiple_of((at + i) * (2 * ny) + half * ny, ny)
                out[i, :, half * 128 : half * 128 + 128] = size_at(row, ny)
    for x in range(nx):
        for half in range(2):
            lanes = slice(half * 128, half * 128 + 128)
            row = (x * 2 + half) * ny
            left_ref[x, :, lanes] = size_at(row, HALO)
            right_ref[x, :, lanes] = size_at(row + ny - HALO, HALO)


def level_of(near):
    return jnp.minimum(jnp.sqrt(near) - RADIUS, BAND)


def along(pair):
    rows = pair[0].shape[0]
    lane = lax.broadcasted_iota(jnp.int32, (rows, 128), 1)
    first = lane == 0
    last = lane == 127
    up = [pltpu.roll(v, 1, 1) for v in pair]
    down = [pltpu.roll(v, 127, 1) for v in pair]
    return (
        (jnp.where(first, 0.0, up[0]), jnp.where(last, down[1], down[0])),
        (jnp.where(first, up[0], up[1]), jnp.where(last, 0.0, down[1])),
    )


def coefficients(a_ref, u_ref, x, r0, rows):
    at = slice(r0, r0 + rows)
    mags = [a_ref[x, h, at, :] for h in range(2)]
    kinds = [u_ref[x, h, at, :] for h in range(2)]
    za, zu = along(mags), along(kinds)
    result = []
    for h in range(2):
        a, u = mags[h], kinds[h]
        r = 1.0 / jnp.maximum(a, 1e-30)
        diagonal = None
        near = [(za[h][0], zu[h][0]), (za[h][1], zu[h][1])]
        for dx, dy in ((-1, 0), (1, 0), (0, -1), (0, 1)):
            beside = slice(r0 + dy, r0 + dy + rows)
            near.append((a_ref[x + dx, h, beside, :], u_ref[x + dx, h, beside, :]))
        for b, w in near:
            term = jnp.minimum(jnp.maximum(a + b, 1.0) * r, w)
            diagonal = term if diagonal is None else diagonal + term
        result.append(jnp.where(u == 1.0, WEIGHT / jnp.maximum(diagonal, 1.0), 0.0))
    return result


def interior_kernel(near_ref, flag_in, div_in, out_ref, size_ref, kind_ref, c_ref, p_ref, a_ref, u_ref, d_ref, f_ref, sem):
    nx, _, ny, _ = near_ref.shape
    R = ROWS
    copies = []
    for half in range(2):
        lanes = pl.ds(half * 128, 128)
        copies.append(pltpu.make_async_copy(flag_in.at[:, :, lanes], f_ref.at[:, half], sem.at[0, half]))
        copies.append(pltpu.make_async_copy(div_in.at[:, :, lanes], d_ref.at[:, half], sem.at[1, half]))
    for copy in copies:
        copy.start()

    def levels(x, carry):
        for half in range(2):
            level = level_of(near_ref[x, half])
            out_ref[x, :, half * 128 : half * 128 + 128] = level
            size = jnp.abs(level)
            size_ref[x, half] = size
            a_ref[x, half, R : R + ny, :] = size
        return carry

    lax.fori_loop(0, nx, levels, 0, unroll=2)
    for copy in copies:
        copy.wait()

    def convert(x, carry):
        for half in range(2):
            kind = kind_of(f_ref[x, half])
            kind_ref[x, half] = kind
            u_ref[x, half, R : R + ny, :] = kind
        return carry

    lax.fori_loop(0, nx, convert, 0, unroll=2)

    def weigh(x, carry):
        for half, c in enumerate(coefficients(a_ref, u_ref, x, R, ny)):
            c_ref[x, half] = c
            p_ref[x, half, R : R + ny, :] = c * d_ref[x, half]
        return carry

    lax.fori_loop(1, nx - 1, weigh, 0, unroll=2)


def interior(near, flag, divergence):
    vmem, hbm, _ = specs()
    nx, ny, nz = divergence.shape
    whole = jax.ShapeDtypeStruct((nx, 2, ny, 128), f32)
    padded = (nx, 2, ny + 2 * ROWS, 128)
    return pl.pallas_call(
        interior_kernel,
        out_shape=(jax.ShapeDtypeStruct((nx, ny, nz), f32),) + (whole,) * 3 + (jax.ShapeDtypeStruct(padded, f32),),
        in_specs=[vmem, hbm, hbm],
        out_specs=(vmem,) * 5,
        scratch_shapes=[
            pltpu.VMEM(padded, f32),
            pltpu.VMEM(padded, f32),
            pltpu.VMEM(whole.shape, f32),
            pltpu.VMEM(whole.shape, jnp.int32),
            pltpu.SemaphoreType.DMA((2, 2)),
        ],
        compiler_params=pltpu.CompilerParams(vmem_limit_bytes=36 << 20),
        name="interior",
    )(near.reshape(whole.shape), flag, divergence)


def specs():
    return tuple(pl.BlockSpec(memory_space=space) for space in (pltpu.VMEM, pl.ANY, pltpu.HBM))


def pack(dest, block, pos, flag, divergence, bricks):
    vmem, _, hbm = specs()
    nx, ny, nz = divergence.shape
    strip = jax.ShapeDtypeStruct((2, HALO, ny, nz), f32)
    edge = jax.ShapeDtypeStruct((2, nx, HALO, nz), f32)
    return pl.pallas_call(
        pack_kernel,
        out_shape=(jax.ShapeDtypeStruct((bricks * 2, 4, TILE), f32), strip, strip, edge, edge),
        in_specs=[hbm] * 5,
        out_specs=(vmem,) * 5,
        scratch_shapes=[
            pltpu.SMEM(dest.shape, jnp.int32),
            pltpu.SMEM(block.shape, jnp.int32),
            pltpu.VMEM(pos.shape, f32),
            pltpu.SMEM((bricks,), jnp.int32),
            pltpu.VMEM((4, TILE, TILE), f32),
            pltpu.VMEM((4, TILE + 16, TILE), f32),
            pltpu.VMEM((2, HALO, ny, nz), jnp.int32),
            pltpu.VMEM((2, nx, 8, nz), jnp.int32),
            pltpu.VMEM((2, nx, 8, nz), f32),
            pltpu.SemaphoreType.DMA((3,)),
            pltpu.SemaphoreType.DMA((8,)),
        ],
        compiler_params=pltpu.CompilerParams(vmem_limit_bytes=60 << 20),
        name="pack",
    )(dest, block, pos, flag, divergence)


def splat(arrived, nx, ny, nz):
    vmem, _, _ = specs()
    records = arrived.shape[0]
    strip = jax.ShapeDtypeStruct((HALO, ny, nz), f32)
    edge = jax.ShapeDtypeStruct((nx, HALO, nz), f32)
    return pl.pallas_call(
        splat_kernel,
        out_shape=(
            jax.ShapeDtypeStruct((nx * 2 * ny, 128), f32),
            strip,
            strip,
            edge,
            edge,
        ),
        in_specs=[vmem, vmem],
        out_specs=(vmem,) * 5,
        scratch_shapes=[
            pltpu.SMEM((16, 128), jnp.int32),
            pltpu.SemaphoreType.DMA,
            pltpu.VMEM((16, 128), jnp.int32),
            pltpu.VMEM((1, records), f32),
            pltpu.VMEM((9, records, TILE), f32),
            pltpu.VMEM((8, 128, TILE), f32),
            pltpu.VMEM((TILE * 8 + 8, 128), f32),
            pltpu.VMEM((TILE * 8 + 8, 128), f32),
            pltpu.VMEM((TILE * 8 + 8, 128), f32),
            pltpu.VMEM((TILE * BLOCK, 8, 128), f32),
            pltpu.VMEM((BLOCK * BLOCK * 8 + 8, 128), f32),
        ],
        compiler_params=pltpu.CompilerParams(vmem_limit_bytes=28 << 20),
        name="splat",
    )(spread_matrix(), arrived)


def edges_kernel(left_ref, right_ref, lx1_ref, lx2_ref, ix1_ref, ix2_ref, out1_ref, out2_ref):
    nx, H = left_ref.shape[0:2]
    ny = lx1_ref.shape[1]
    side = lax.axis_index("gx") % 2
    even = lax.axis_index("gy") % 2 == 0
    ext = nx + 2 * H
    low = slice(0, H)
    high = slice(ny - H, ny)
    for turn, out in ((True, out1_ref), (False, out2_ref)):
        up = even if turn else jnp.logical_not(even)
        out[H : nx + H] = jnp.where(up, right_ref[...], left_ref[...])
        for at, step, one, two in (
            (0, nx + H, lx1_ref, lx2_ref),
            (ext, H, ix1_ref.at[0], ix2_ref.at[0]),
            (ext + 2 * H, H, ix1_ref.at[1], ix2_ref.at[1]),
        ):
            out[pl.ds(at + (1 - side) * step, H)] = jnp.where(up, one[:, high, :], one[:, low, :])
            out[pl.ds(at + side * step, H)] = jnp.where(up, two[:, high, :], two[:, low, :])


def edges(left, right, lx1, lx2, ix1, ix2):
    vmem, _, _ = specs()
    nx, H, nz = left.shape
    out = jax.ShapeDtypeStruct((nx + 6 * H, H, nz), f32)
    return pl.pallas_call(
        edges_kernel,
        out_shape=(out, out),
        in_specs=[vmem] * 6,
        out_specs=(vmem, vmem),
        compiler_params=pltpu.CompilerParams(vmem_limit_bytes=16 << 20),
        name="edges",
    )(left, right, lx1, lx2, ix1, ix2)


def around(ref, x, r0, rows):
    at = slice(r0, r0 + rows)
    pair = [ref[x, h, at, :] for h in range(2)]
    z = along(pair)
    totals = []
    for h in range(2):
        total = z[h][0] + z[h][1]
        total = total + (ref[x - 1, h, at, :] + ref[x + 1, h, at, :])
        total = total + (ref[x, h, r0 - 1 : r0 - 1 + rows, :] + ref[x, h, r0 + 1 : r0 + 1 + rows, :])
        totals.append(total)
    return pair, totals


def second_sweep(p_ref, c, x, r0, rows):
    own, total = around(p_ref, x, r0, rows)
    return [own[h] * (4.0 / 3.0) + c[h] * total[h] for h in range(2)]


def later_sweep(ref, p, c, x, r0, rows):
    own, total = around(ref, x, r0, rows)
    return [own[h] * (1.0 / 3.0) + p[h] + c[h] * total[h] for h in range(2)]


def middle_kernel(c_ref, p_ref, out_ref, q_ref, r_ref):
    nx, _, ny, _ = c_ref.shape
    R = ROWS
    at = slice(R, R + ny)

    def both(ref, x, rows=slice(None)):
        return [ref[x, h, rows, :] for h in range(2)]

    def second(x, carry):
        for h, v in enumerate(second_sweep(p_ref, both(c_ref, x), x, R, ny)):
            q_ref[x, h, at, :] = v
        return carry

    lax.fori_loop(2, nx - 2, second, 0, unroll=7)

    def third(x, carry):
        for h, v in enumerate(later_sweep(q_ref, both(p_ref, x, at), both(c_ref, x), x, R, ny)):
            r_ref[x, h, at, :] = v
        return carry

    lax.fori_loop(3, nx - 3, third, 0, unroll=13)

    def fourth(x, carry):
        for h, v in enumerate(later_sweep(r_ref, both(p_ref, x, at), both(c_ref, x), x, R, ny)):
            out_ref[x, :, h * 128 : h * 128 + 128] = v
        return carry

    lax.fori_loop(4, nx - 4, fourth, 0, unroll=8)


def middle(c, p):
    vmem, _, _ = specs()
    nx, _, ny, lanes = c.shape
    padded = jax.ShapeDtypeStruct(p.shape, f32)
    return pl.pallas_call(
        middle_kernel,
        out_shape=(jax.ShapeDtypeStruct((nx, ny, 2 * lanes), f32), padded, padded),
        in_specs=[vmem, vmem],
        out_specs=(vmem,) * 3,
        compiler_params=pltpu.CompilerParams(vmem_limit_bytes=24 << 20),
        name="middle",
    )(c, p)


def jacobi_kernel(result_in, size_ref, kind_ref, div_ref, c_in, p_in, q_in, r_in, lx1_ref, lx2_ref, ix1_ref, ix2_ref,
                  ly1_ref, ly2_ref, iy1_ref, iy2_ref, out_ref,
                  a_ref, u_ref, d_ref, c_ref, p_ref, q_ref, r_ref, slab_ref, tile_ref, sem, out_sem):
    nx, _, ny, _ = size_ref.shape
    H = HALO
    R = ROWS
    S = H + 1
    side = lax.axis_index("gx") % 2
    inner = pl.ds(R, ny)
    first_x, second_x = pl.ds((1 - side) * (nx + H), H), pl.ds(side * (nx + H), H)
    copies = []

    def copy(source, target, n, half):
        copies.append(pltpu.make_async_copy(source, target, sem.at[n, half]))
        copies[-1].start()

    shell = ((0, S, 0, ny), (nx - S, S, 0, ny), (S, nx - 2 * S, 0, 8), (S, nx - 2 * S, ny - 8, 8))
    for n, (x, planes, y, rows) in enumerate(shell):
        xs, ys, padded = pl.ds(x, planes), pl.ds(y, rows), pl.ds(y + R, rows)
        at = pl.ds(x + H, planes)
        copy(size_ref.at[xs, :, ys], a_ref.at[at, :, padded], n, 0)
        copy(kind_ref.at[xs, :, ys], u_ref.at[at, :, padded], n, 1)
        for half in range(2):
            copy(div_ref.at[xs, ys, pl.ds(half * 128, 128)], d_ref.at[at, half, padded], 4 + n, half)
        copy(c_in.at[xs, :, ys], c_ref.at[at, :, padded], 8 + n, 0)
        copy(p_in.at[xs, :, padded], p_ref.at[at, :, padded], 8 + n, 1)
    for half in range(2):
        lanes = pl.ds(half * 128, 128)
        for n, (source, target) in enumerate(
            (
                (ix1_ref.at[0], u_ref.at[first_x, half, inner]),
                (ix2_ref.at[0], u_ref.at[second_x, half, inner]),
                (ix1_ref.at[1], d_ref.at[first_x, half, inner]),
                (ix2_ref.at[1], d_ref.at[second_x, half, inner]),
                (lx1_ref, a_ref.at[first_x, half, inner]),
                (lx2_ref, a_ref.at[second_x, half, inner]),
            )
        ):
            copy(source.at[:, :, lanes], target, 16 + n, half)
    ready = len(copies)
    for m, (source, target) in enumerate(((q_in, q_ref), (r_in, r_ref))):
        for n, (x, planes, y, rows) in enumerate(shell):
            xs, padded, at = pl.ds(x, planes), pl.ds(y + R, rows), pl.ds(x + H, planes)
            copy(source.at[xs, :, padded], target.at[at, :, padded], 12 + n, m)
    mid = pl.ds(H, nx - 2 * H)
    copy(result_in.at[mid, pl.ds(0, 8)], tile_ref.at[0], 22, 0)
    copy(result_in.at[mid, pl.ds(ny - 8, 8)], tile_ref.at[1], 22, 1)
    for half in range(2):
        lanes = slice(half * 128, half * 128 + 128)
        for turn, rows in ((1, slice(R - H, R)), (0, slice(R + ny, R + ny + H))):
            first = lax.axis_index("gy") % 2 == turn
            a_ref[:, half, rows, :] = jnp.where(first, ly1_ref[0 : nx + 2 * H, :, lanes], ly2_ref[0 : nx + 2 * H, :, lanes])
            for n, ext in enumerate((u_ref, d_ref)):
                at = nx + 2 * H + n * 2 * H
                corner = jnp.where(first, ly1_ref[at : at + 2 * H, :, lanes], ly2_ref[at : at + 2 * H, :, lanes])
                ext[0:H, half, rows, :] = corner[0:H]
                ext[nx + H : nx + 2 * H, half, rows, :] = corner[H : 2 * H]
                ext[H : nx + H, half, rows, :] = jnp.where(first, iy1_ref[n, :, :, lanes], iy2_ref[n, :, :, lanes])
    for one in copies[:ready]:
        one.wait()

    def over_shell(first, body):
        last = nx + 2 * H - first - H

        def planes(i, carry):
            body(first + i, R - H, ny + 2 * H)
            body(last + i, R - H, ny + 2 * H)
            return carry

        def sides(x, carry):
            body(x, R - H, 8)
            body(x, R + ny - H, 8)
            return carry

        lax.fori_loop(0, H, planes, 0, unroll=4)
        lax.fori_loop(first + H, last, sides, 0, unroll=8)

    def both(ref, x, r0, rows):
        return [ref[x, h, r0 : r0 + rows, :] for h in range(2)]

    def weigh(x, r0, rows):
        at = slice(r0, r0 + rows)
        for half, c in enumerate(coefficients(a_ref, u_ref, x, r0, rows)):
            c_ref[x, half, at, :] = c
            p_ref[x, half, at, :] = c * d_ref[x, half, at, :]

    def second(x, r0, rows):
        for h, v in enumerate(second_sweep(p_ref, both(c_ref, x, r0, rows), x, r0, rows)):
            q_ref[x, h, r0 : r0 + rows, :] = v

    def third(x, r0, rows):
        for h, v in enumerate(later_sweep(q_ref, both(p_ref, x, r0, rows), both(c_ref, x, r0, rows), x, r0, rows)):
            r_ref[x, h, r0 : r0 + rows, :] = v

    over_shell(1, weigh)
    for one in copies[ready:]:
        one.wait()
    over_shell(2, second)
    over_shell(3, third)

    def last(x, r0, rows):
        return later_sweep(r_ref, both(p_ref, x, r0, rows), both(c_ref, x, r0, rows), x, r0, rows)

    def planes(i, carry):
        for n, x in enumerate((H + i, nx + i)):
            for h, v in enumerate(last(x, R, ny)):
                slab_ref[n, i, :, h * 128 : h * 128 + 128] = v
        return carry

    lax.fori_loop(0, H, planes, 0, unroll=4)
    outs = [
        pltpu.make_async_copy(slab_ref.at[n], out_ref.at[pl.ds(x, H)], out_sem.at[n]) for n, x in enumerate((0, nx - H))
    ]
    for one in outs:
        one.start()

    def sides(x, carry):
        for h, v in enumerate(last(x, R - H, 8)):
            tile_ref[0, x - 2 * H, 0:H, h * 128 : h * 128 + 128] = v[H:8]
        for h, v in enumerate(last(x, R + ny - H, 8)):
            tile_ref[1, x - 2 * H, 8 - H : 8, h * 128 : h * 128 + 128] = v[0:H]
        return carry

    lax.fori_loop(2 * H, nx, sides, 0, unroll=8)
    for n, y in enumerate((0, ny - 8)):
        outs.append(pltpu.make_async_copy(tile_ref.at[n], out_ref.at[mid, pl.ds(y, 8)], out_sem.at[2 + n]))
        outs[-1].start()
    for one in outs:
        one.wait()


def jacobi(result, parts, halo):
    vmem, hbm, _ = specs()
    nx, ny, nz = result.shape
    ext = (nx + 2 * HALO, 2, ny + 2 * ROWS, 128)
    return pl.pallas_call(
        jacobi_kernel,
        out_shape=jax.ShapeDtypeStruct((nx, ny, nz), f32),
        in_specs=[hbm] * 12 + [vmem] * 4,
        out_specs=hbm,
        input_output_aliases={0: 0},
        scratch_shapes=[pltpu.VMEM(ext, f32)] * 7
        + [
            pltpu.VMEM((2, HALO, ny, nz), f32),
            pltpu.VMEM((2, nx - 2 * HALO, 8, nz), f32),
            pltpu.SemaphoreType.DMA((23, 2)),
            pltpu.SemaphoreType.DMA((4,)),
        ],
        compiler_params=pltpu.CompilerParams(vmem_limit_bytes=32 << 20),
        name="jacobi",
    )(result, *parts, *halo)


def spread_matrix():
    row = jnp.arange(128)
    coord, tile = row // 8 % 3, row % 8
    column = jnp.arange(384)
    hit = (row[:, None] < 72) & (coord[:, None] == column[None, :] // 128)
    hit = hit & (tile[:, None] == column[None, :] % 128 // 16)
    return hit.astype(jnp.bfloat16)


def swap(axis, first, second):
    count = lax.axis_size(axis)
    arrived = []
    for part, start in ((first, 0), (second, 1)):
        pairs = []
        for i in range(start, count - 1, 2):
            pairs += [(i, i + 1), (i + 1, i)]
        arrived.append(lax.ppermute(part, axis, pairs))
    return arrived


def per_device(particle_pos, tile_dest, tile_block, fluid_flag, divergence):
    nx, ny, nz = divergence.shape
    bricks = lax.axis_size("gx") * lax.axis_size("gy")
    flag, div = fluid_flag, divergence
    send, first, second, face1, face2 = pack(tile_dest[:, 0], tile_block, particle_pos, flag, div, bricks)
    arrived = lax.all_to_all(send, ("gx", "gy"), split_axis=0, concat_axis=0, tiled=True)
    ix1, ix2 = swap("gx", first, second)
    iy1, iy2 = swap("gy", face1, face2)
    arrived, iy1, iy2 = lax.optimization_barrier((arrived, iy1, iy2))
    near, first, second, left, right = splat(arrived, nx, ny, nz)
    lx1, lx2 = swap("gx", first, second)
    level, sizes, kinds, c, p = interior(near, flag, div)
    lx1, lx2, c = lax.optimization_barrier((lx1, lx2, c))
    ly1, ly2 = swap("gy", *edges(left, right, lx1, lx2, ix1, ix2))
    result, q, r = middle(c, p)
    pressure = jacobi(result, (sizes, kinds, div, c, p, q, r), (lx1, lx2, ix1, ix2, ly1, ly2, iy1, iy2))
    return (level, pressure)


def solution(mesh):
    placed = (
        P(None, ("gx", "gy")),
        P(("gx", "gy"), None),
        P(("gx", "gy")),
        P("gx", "gy", None),
        P("gx", "gy", None),
    )
    return jax.shard_map(
        per_device,
        mesh=mesh,
        in_specs=placed,
        out_specs=(P("gx", "gy", None), P("gx", "gy", None)),
        check_vma=False,
    )
```

```python
import functools

import jax
import jax.numpy as jnp
from jax import lax
from jax.experimental import pallas as pl
from jax.experimental.pallas import tpu as pltpu
from jax.sharding import PartitionSpec as P

BLOCK = 16
TILE = 128
RADIUS = 1.2
BAND = 3.0
WEIGHT = 2.0 / 3.0
FAR = 1.0e9
HALO = 4
ROWS = 8
REACH = RADIUS + BAND + 1.0e-3
PAIRS = 8

f32 = jnp.float32


def ordered(keys, first, second):
    row = lax.broadcasted_iota(jnp.int32, (8, TILE), 0)
    data = [list(keys), list(first), list(second)]
    size = 2
    while size <= TILE:
        if size >= 16 and size < TILE:
            sign = jnp.where((row & (size // 16)) == 0, 1.0, -1.0).astype(f32)
        else:
            sign = None
        gap = size // 2
        while gap >= 1:
            if gap < 16:
                for v in range(16):
                    if v & gap:
                        continue
                    w = v | gap
                    a, b = data[0][v], data[0][w]
                    if sign is not None:
                        swap_now = a * sign > b * sign
                    elif size < 16 and v & size:
                        swap_now = a < b
                    else:
                        swap_now = a > b
                    for part in data:
                        a, b = part[v], part[w]
                        part[v] = jnp.where(swap_now, b, a)
                        part[w] = jnp.where(swap_now, a, b)
            else:
                e = gap // 16
                low = (row & e) == 0
                way = jnp.where(low, 1.0, -1.0).astype(f32)
                if sign is not None:
                    way = way * sign
                for v in range(16):
                    others = []
                    for part in data:
                        if e == 4:
                            others.append(pltpu.roll(part[v], 4, 0))
                        else:
                            others.append(jnp.where(low, pltpu.roll(part[v], 8 - e, 0), pltpu.roll(part[v], e, 0)))
                    take = data[0][v] * way > others[0] * way
                    for part, other in zip(data, others):
                        part[v] = jnp.where(take, other, part[v])
            gap //= 2
        size *= 2
    return data


def strip_copies(kind_in, div_in, first_ref, second_ref, kx_ref, ky_ref, dy_ref, sem):
    nx, ny, nz = kind_in.shape
    copies = []
    side = lax.axis_index("gx") % 2
    for n, (at, out) in enumerate((((1 - side) * (nx - HALO), first_ref), (side * (nx - HALO), second_ref))):
        planes = pl.ds(at, HALO)
        copies.append(pltpu.make_async_copy(kind_in.at[planes], kx_ref.at[n], sem.at[n]))
        copies.append(pltpu.make_async_copy(div_in.at[planes], out.at[1], sem.at[2 + n]))
    for n, at in enumerate((0, ny - 8)):
        rows = pl.ds(at, 8)
        copies.append(pltpu.make_async_copy(kind_in.at[:, rows, :], ky_ref.at[n], sem.at[4 + n]))
        copies.append(pltpu.make_async_copy(div_in.at[:, rows, :], dy_ref.at[n], sem.at[6 + n]))
    return copies


def cut_strips(first_ref, second_ref, face1_ref, face2_ref, kx_ref, ky_ref, dy_ref):
    first_ref[0] = kind_of(kx_ref[0])
    second_ref[0] = kind_of(kx_ref[1])
    low = slice(0, HALO)
    high = slice(8 - HALO, 8)
    even = lax.axis_index("gy") % 2 == 0
    for turn, out in ((True, face1_ref), (False, face2_ref)):
        up = even if turn else jnp.logical_not(even)
        out[0] = jnp.where(up, kind_of(ky_ref[1, :, high, :]), kind_of(ky_ref[0, :, low, :]))
        out[1] = jnp.where(up, dy_ref[1, :, high, :], dy_ref[0, :, low, :])


def pack_kernel(dest_in, block_in, pos_in, kind_in, div_in, send_ref, first_ref, second_ref, face1_ref, face2_ref,
                dest_ref, block_ref, pos_ref, count_ref, tile_ref, turn_ref, kx_ref, ky_ref, dy_ref, sem, strip_sem):
    tiles = block_ref.shape[0]
    copies = [
        pltpu.make_async_copy(a, b, sem.at[n])
        for n, (a, b) in enumerate(((pos_in, pos_ref), (dest_in, dest_ref), (block_in, block_ref)))
    ]
    strips = strip_copies(kind_in, div_in, first_ref, second_ref, kx_ref, ky_ref, dy_ref, strip_sem)
    for copy in copies + strips:
        copy.start()
    lane = lax.broadcasted_iota(jnp.int32, (4, TILE), 1)
    note = (lax.broadcasted_iota(jnp.int32, (4, TILE), 0) == 3) & (lane == 0)

    def clear(i, carry):
        count_ref[i] = 0
        return carry

    lax.fori_loop(0, count_ref.shape[0], clear, 0, unroll=16)
    empty = jnp.where(lane == 0, -1.0, 0.0).astype(f32)
    send_ref[...] = jnp.broadcast_to(empty[None], send_ref.shape)

    copies[0].wait()
    for t in range(tiles):
        tile_ref[0:3, t, :] = pos_ref[:, t * TILE : t * TILE + TILE]
    parts = []
    for c in range(3):
        turned = jnp.transpose(tile_ref[c], (1, 0))
        parts.append([turned[v * 8 : v * 8 + 8, :] for v in range(16)])
    parts = ordered(*parts)
    turn_ref[3] = jnp.zeros((TILE + 16, TILE), f32)
    for k in range(PAIRS):
        below = jnp.zeros((8, TILE), f32)
        upto = jnp.zeros((8, TILE), f32)
        for v in range(16):
            below = below + jnp.where(parts[0][v] < 2 * k + 0.5 - REACH, 1.0, 0.0)
            upto = upto + jnp.where(parts[0][v] < 2 * k + 1.5 + REACH, 1.0, 0.0)
        turn_ref[3, 1 + k : 2 + k, :] = jnp.sum(below, axis=0, keepdims=True) - TILE
        turn_ref[3, 1 + PAIRS + k : 2 + PAIRS + k, :] = -jnp.sum(upto, axis=0, keepdims=True)
    for c in range(3):
        for v in range(16):
            turn_ref[c, pl.ds(v, 8, stride=16), :] = parts[c][v]
    for c in range(4):
        tile_ref[c] = jnp.transpose(turn_ref[c, 0:TILE, :], (1, 0))

    for copy in copies[1:] + strips:
        copy.wait()
    cut_strips(first_ref, second_ref, face1_ref, face2_ref, kx_ref, ky_ref, dy_ref)

    def place(t, carry):
        owner = dest_ref[t]
        slot = count_ref[owner]
        count_ref[owner] = slot + 1
        send_ref[owner * 2 + slot] = jnp.where(note, block_ref[t].astype(f32), tile_ref[:, t, :])
        return carry

    lax.fori_loop(0, tiles, place, 0, unroll=16)


def ones_where(condition):
    return jnp.where(condition, 1.0, 0.0).astype(jnp.bfloat16)


def row_to_column(row):
    return jnp.concatenate(
        [
            jnp.transpose(jnp.broadcast_to(row[:, h : h + 128], (128, 128)), (1, 0))
            for h in range(0, row.shape[1], 128)
        ],
        axis=0,
    )


def arrange(notes, note_ref, slot_ref):
    records = notes.shape[0]
    halves = records // 128
    turned = [jnp.transpose(notes[h * 128 : h * 128 + 128, :], (1, 0)) for h in range(halves)]
    labels = jnp.concatenate([v[0:1, :] for v in turned], axis=1)
    shift = [v[1 : 1 + PAIRS] - v[1 + PAIRS : 1 + 2 * PAIRS] for v in turned]
    keys = jnp.concatenate([jnp.sum(v, axis=0, keepdims=True) for v in shift], axis=1)
    valid = labels >= 0.0
    spot = (labels.astype(jnp.int32) & 7).astype(f32)
    column = lax.broadcasted_iota(jnp.int32, (8, records), 0).astype(f32)
    member = jnp.where(valid & (column == spot), 1.0, 0.0)
    from_index = lax.broadcasted_iota(jnp.int32, (records, records), 0)
    to_index = lax.broadcasted_iota(jnp.int32, (records, records), 1)
    earlier = ones_where(from_index < to_index)
    own = row_to_column(keys)
    own = jnp.concatenate([own] * halves, axis=1)
    smaller = (own < keys) | ((own == keys) & (from_index < to_index))
    before = jnp.dot(member.astype(jnp.bfloat16), ones_where(smaller), preferred_element_type=f32)
    rank = jnp.sum(member * before, axis=0, keepdims=True)
    counts = jnp.sum(member, axis=1, keepdims=True)
    total = jnp.sum(counts, axis=0, keepdims=True)
    room = 8.0 * jnp.floor((total + 63.0) * (1.0 / 64.0))
    late = jnp.where(valid & (rank >= room), 1.0, 0.0)
    turn = jnp.dot(jnp.broadcast_to(late, (8, records)).astype(jnp.bfloat16), earlier, preferred_element_type=f32)[0:1]
    used = jnp.minimum(counts, room)
    free = room - used
    offsets = [jnp.zeros((1, 1), f32)]
    for t in range(7):
        offsets.append(offsets[-1] + free[t : t + 1])
    offset = jnp.concatenate(offsets, axis=0)
    chosen = (turn >= offset) & (turn < offset + free)
    moved = jnp.sum(jnp.where(chosen, (used + turn - offset) * 8.0 + column, 0.0), axis=0, keepdims=True)
    slots = jnp.where(valid, jnp.where(late > 0.0, moved, rank * 8.0 + spot), -1.0)
    slot_ref[...] = slots
    lane = lax.broadcasted_iota(jnp.int32, (records, 128), 1).astype(f32)
    raised = jnp.broadcast_to(jnp.where(valid, labels + 1.0, 0.0), (8, records)).astype(jnp.bfloat16)
    late_slots = jnp.broadcast_to(jnp.where(late > 0.0, slots + 1.0, 0.0), (8, records)).astype(jnp.bfloat16)
    to_slot = row_to_column(slots)
    to_turn = row_to_column(jnp.where(late > 0.0, turn, -1.0))
    for h in range(halves):
        here = jnp.dot(raised, ones_where(to_slot == lane + 128.0 * h), preferred_element_type=f32)
        note_ref[h : h + 1, :] = (here[0:1] - 1.0).astype(jnp.int32)
        here = jnp.dot(late_slots, ones_where(to_turn == lane + 128.0 * h), preferred_element_type=f32)
        note_ref[halves + h : halves + h + 1, :] = here[0:1].astype(jnp.int32)
    sums = jnp.where(lane[0:1] == 0.0, total, jnp.sum(late, axis=1, keepdims=True))
    for b in range(records // 64):
        here = jnp.where((slots >= 64.0 * b) & (slots < 64.0 * b + 64.0), late, 0.0)
        sums = jnp.where(lane[0:1] == 2.0 + b, jnp.sum(here, axis=1, keepdims=True), sums)
    note_ref[2 * halves : 2 * halves + 1, :] = sums.astype(jnp.int32)


def kind_of(flag):
    return 5.0 - 4.0 * flag.astype(f32)


def splat_kernel(spread_ref, rec_ref, near_ref, first_ref, second_ref, left_ref, right_ref, meta_ref, sem,
                 note_ref, slot_ref, piece_ref, turn_ref, px_ref, py_ref, pz_ref, dyz_ref, acc_ref):
    records = rec_ref.shape[0]
    halves = records // 128
    nx, ny = left_ref.shape[0], first_ref.shape[1]

    notes = rec_ref[:, 3, :]
    arrange(notes, note_ref, slot_ref)
    index = lax.broadcasted_iota(jnp.int32, (records, records), 0).astype(f32)
    to_slot = ones_where(index == slot_ref[...])
    pieces = [[], [], []]
    for c in range(3):
        whole = rec_ref[:, c, :]
        high = whole.astype(jnp.bfloat16)
        rest = whole - high.astype(f32)
        middle = rest.astype(jnp.bfloat16)
        pieces[0].append(high)
        pieces[1].append(middle)
        pieces[2].append((rest - middle.astype(f32)).astype(jnp.bfloat16))
    for n in range(3):
        for c in range(3):
            piece_ref[n * 3 + c] = jnp.dot(to_slot, pieces[n][c], preferred_element_type=f32)
    placed = jnp.dot(to_slot, notes.astype(jnp.bfloat16), preferred_element_type=f32)
    for b in range(records // 64):
        least = jnp.min(placed[b * 64 : b * 64 + 64, :], axis=0, keepdims=True)
        note_ref[2 * halves + 1 + b : 2 * halves + 2 + b, :] = least.astype(jnp.int32)
    copy = pltpu.make_async_copy(note_ref, meta_ref, sem)
    copy.start()
    near_ref[...] = jnp.full(near_ref.shape, FAR, f32)
    turn_ref[...] = jnp.zeros(turn_ref.shape, f32)
    copy.wait()
    batches = (meta_ref[2 * halves, 0] + 63) // 64
    late = meta_ref[2 * halves, 1]

    lane = lax.broadcasted_iota(jnp.int32, (8, 128), 1)
    depth = (lane & 15).astype(f32) + 0.5
    spots = lax.broadcasted_iota(jnp.int32, (1, 128), 1) >> 4

    def batch(g, carry):
        turns = []
        for s in range(8):
            for n in range(9):
                turn_ref[s, n * 8 : n * 8 + 8, :] = piece_ref[n, pl.ds(pl.multiple_of(g * 64 + s * 8, 8), 8), :]
            turns.append(jnp.transpose(turn_ref[s], (1, 0)).astype(jnp.bfloat16))
        place = jnp.dot(jnp.concatenate(turns, axis=0), spread_ref[...], preferred_element_type=f32)
        for s in range(8):
            at = slice(s * TILE, s * TILE + TILE)
            px_ref[pl.ds(s, TILE, stride=8), :] = place[at, 0:128]
            py_ref[pl.ds(s, TILE, stride=8), :] = place[at, 128:256]
            pz_ref[pl.ds(s, TILE, stride=8), :] = place[at, 256:384]

        def prepare(k, inner):
            for u in range(16):
                p = k * 16 + u
                rows = pl.ds(pl.multiple_of(p * 8, 8), 8)
                py = py_ref[rows, :]
                dz = depth - pz_ref[rows, :]
                dz = dz * dz
                for y in range(16):
                    dy = (y + 0.5) - py
                    dyz_ref[p * 16 + y] = dy * dy + dz
            return inner

        lax.fori_loop(0, TILE // 16, prepare, 0)

        for k in range(PAIRS):
            stop = -meta_ref[2 * halves + 1 + g, 1 + PAIRS + k]
            steps = (stop - (meta_ref[2 * halves + 1 + g, 1 + k] + TILE) + 7) // 8
            first = jnp.maximum(stop - steps * 8, 0)

            def step(i, accs):
                accs = list(accs)
                for u in range(4):
                    p = first + i * 8 + u * 2
                    away = []
                    for v in range(2):
                        px = px_ref[pl.ds(pl.multiple_of((p + v) * 8, 8), 8), :]
                        d0 = (2 * k + 0.5) - px
                        d1 = (2 * k + 1.5) - px
                        away.append((d0 * d0, d1 * d1))
                    for y in range(16):
                        one = dyz_ref[p * 16 + y]
                        two = dyz_ref[p * 16 + 16 + y]
                        for x in range(2):
                            both = jnp.minimum(one + away[0][x], two + away[1][x])
                            accs[x * 16 + y] = jnp.minimum(accs[x * 16 + y], both)
                return tuple(accs)

            accs = lax.fori_loop(0, steps, step, tuple(jnp.full((8, 128), FAR, f32) for _ in range(32)))
            for i in range(32):
                acc_ref[(k * 32 + i) * 8 : (k * 32 + i) * 8 + 8, :] = accs[i]

        def put_down(s, t, label, mask, move):
            bx = label // 64
            base = (label // 8 % 2) * ny + bx * (32 * ny) + label // 16 % 4 * 16
            for x in range(16):
                tile = acc_ref[pl.ds(x * 128 + s, 16, stride=8), :]
                tile = pltpu.roll(tile, move, 1)
                rows = pl.ds(pl.multiple_of(base + x * (2 * ny), 16), 16)
                near_ref[rows, :] = jnp.minimum(near_ref[rows, :], jnp.where(mask, tile, FAR))

        def merge(s, inner):
            labels = [meta_ref[g // 2, g % 2 * 64 + s * 8 + t] for t in range(8)]
            wanted = [(label >= 0) & ((label & 7) == t) for t, label in enumerate(labels)]
            masks = [spots == jnp.where(want, t, -1) for t, want in enumerate(wanted)]
            labels = [jnp.maximum(label, 0) for label in labels]
            bases = [v // 8 % 2 * ny + v // 64 * (32 * ny) + v // 16 % 4 * 16 for v in labels]
            for start in range(0, 16, 8):
                tiles = [acc_ref[pl.ds(x * 128 + s, 16, stride=8), :] for x in range(start, start + 8)]
                for mask, base in zip(masks, bases):
                    for x, tile in enumerate(tiles):
                        rows = pl.ds(pl.multiple_of(base + (start + x) * (2 * ny), 16), 16)
                        near_ref[rows, :] = jnp.minimum(near_ref[rows, :], jnp.where(mask, tile, FAR))
            return inner

        lax.fori_loop(0, 8, merge, 0, unroll=4)

        def merge_late(i, inner):
            j = meta_ref[halves + i // 128, i % 128] - 1
            here = j // 64 == g
            j = jnp.maximum(j, 0)
            t = j % 8
            label = jnp.maximum(meta_ref[j // 128, j % 128], 0)
            spot = label & 7
            put_down(j // 8 % 8, t, label, spots == jnp.where(here, spot, -1), ((spot - t) & 7) * 16)
            return inner

        steps = jnp.where(meta_ref[2 * halves, 2 + g] > 0, (late + 3) // 4, 0)

        def merge_late_four(i, inner):
            for n in range(4):
                merge_late(i * 4 + n, inner)
            return inner

        lax.fori_loop(0, steps, merge_late_four, 0)
        return carry

    lax.fori_loop(0, batches, batch, 0)

    def size_at(row, rows):
        return jnp.abs(level_of(near_ref[pl.ds(row, rows), :]))

    side = lax.axis_index("gx") % 2
    for at, out in (((1 - side) * (nx - HALO), first_ref), (side * (nx - HALO), second_ref)):
        for i in range(HALO):
            for half in range(2):
                row = pl.multiple_of((at + i) * (2 * ny) + half * ny, ny)
                out[i, :, half * 128 : half * 128 + 128] = size_at(row, ny)
    for x in range(nx):
        for half in range(2):
            lanes = slice(half * 128, half * 128 + 128)
            row = (x * 2 + half) * ny
            left_ref[x, :, lanes] = size_at(row, HALO)
            right_ref[x, :, lanes] = size_at(row + ny - HALO, HALO)


def level_of(near):
    return jnp.minimum(jnp.sqrt(near) - RADIUS, BAND)


def along(pair):
    rows = pair[0].shape[0]
    lane = lax.broadcasted_iota(jnp.int32, (rows, 128), 1)
    first = lane == 0
    last = lane == 127
    up = [pltpu.roll(v, 1, 1) for v in pair]
    down = [pltpu.roll(v, 127, 1) for v in pair]
    return (
        (jnp.where(first, 0.0, up[0]), jnp.where(last, down[1], down[0])),
        (jnp.where(first, up[0], up[1]), jnp.where(last, 0.0, down[1])),
    )


def coefficients(a_ref, u_ref, x, r0, rows):
    at = slice(r0, r0 + rows)
    mags = [a_ref[x, h, at, :] for h in range(2)]
    kinds = [u_ref[x, h, at, :] for h in range(2)]
    za, zu = along(mags), along(kinds)
    result = []
    for h in range(2):
        a, u = mags[h], kinds[h]
        r = 1.0 / jnp.maximum(a, 1e-30)
        diagonal = None
        near = [(za[h][0], zu[h][0]), (za[h][1], zu[h][1])]
        for dx, dy in ((-1, 0), (1, 0), (0, -1), (0, 1)):
            beside = slice(r0 + dy, r0 + dy + rows)
            near.append((a_ref[x + dx, h, beside, :], u_ref[x + dx, h, beside, :]))
        for b, w in near:
            term = jnp.minimum(jnp.maximum(a + b, 1.0) * r, w)
            diagonal = term if diagonal is None else diagonal + term
        result.append(jnp.where(u == 1.0, WEIGHT / jnp.maximum(diagonal, 1.0), 0.0))
    return result


def interior_kernel(near_ref, flag_in, div_in, out_ref, size_ref, kind_ref, c_ref, p_ref, a_ref, u_ref, d_ref, f_ref, sem):
    nx, _, ny, _ = near_ref.shape
    R = ROWS
    copies = []
    for half in range(2):
        lanes = pl.ds(half * 128, 128)
        copies.append(pltpu.make_async_copy(flag_in.at[:, :, lanes], f_ref.at[:, half], sem.at[0, half]))
        copies.append(pltpu.make_async_copy(div_in.at[:, :, lanes], d_ref.at[:, half], sem.at[1, half]))
    for copy in copies:
        copy.start()

    def levels(x, carry):
        for half in range(2):
            level = level_of(near_ref[x, half])
            out_ref[x, :, half * 128 : half * 128 + 128] = level
            size = jnp.abs(level)
            size_ref[x, half] = size
            a_ref[x, half, R : R + ny, :] = size
        return carry

    lax.fori_loop(0, nx, levels, 0, unroll=2)
    for copy in copies:
        copy.wait()

    def convert(x, carry):
        for half in range(2):
            kind = kind_of(f_ref[x, half])
            kind_ref[x, half] = kind
            u_ref[x, half, R : R + ny, :] = kind
        return carry

    lax.fori_loop(0, nx, convert, 0, unroll=2)

    def weigh(x, carry):
        for half, c in enumerate(coefficients(a_ref, u_ref, x, R, ny)):
            c_ref[x, half] = c
            p_ref[x, half, R : R + ny, :] = c * d_ref[x, half]
        return carry

    lax.fori_loop(1, nx - 1, weigh, 0, unroll=2)


def interior(near, flag, divergence):
    vmem, hbm, _ = specs()
    nx, ny, nz = divergence.shape
    whole = jax.ShapeDtypeStruct((nx, 2, ny, 128), f32)
    padded = (nx, 2, ny + 2 * ROWS, 128)
    return pl.pallas_call(
        interior_kernel,
        out_shape=(jax.ShapeDtypeStruct((nx, ny, nz), f32),) + (whole,) * 3 + (jax.ShapeDtypeStruct(padded, f32),),
        in_specs=[vmem, hbm, hbm],
        out_specs=(vmem,) * 5,
        scratch_shapes=[
            pltpu.VMEM(padded, f32),
            pltpu.VMEM(padded, f32),
            pltpu.VMEM(whole.shape, f32),
            pltpu.VMEM(whole.shape, jnp.int32),
            pltpu.SemaphoreType.DMA((2, 2)),
        ],
        compiler_params=pltpu.CompilerParams(vmem_limit_bytes=36 << 20),
        name="interior",
    )(near.reshape(whole.shape), flag, divergence)


def specs():
    return tuple(pl.BlockSpec(memory_space=space) for space in (pltpu.VMEM, pl.ANY, pltpu.HBM))


def pack(dest, block, pos, flag, divergence, bricks):
    vmem, _, hbm = specs()
    nx, ny, nz = divergence.shape
    strip = jax.ShapeDtypeStruct((2, HALO, ny, nz), f32)
    edge = jax.ShapeDtypeStruct((2, nx, HALO, nz), f32)
    return pl.pallas_call(
        pack_kernel,
        out_shape=(jax.ShapeDtypeStruct((bricks * 2, 4, TILE), f32), strip, strip, edge, edge),
        in_specs=[hbm] * 5,
        out_specs=(vmem,) * 5,
        scratch_shapes=[
            pltpu.SMEM(dest.shape, jnp.int32),
            pltpu.SMEM(block.shape, jnp.int32),
            pltpu.VMEM(pos.shape, f32),
            pltpu.SMEM((bricks,), jnp.int32),
            pltpu.VMEM((4, TILE, TILE), f32),
            pltpu.VMEM((4, TILE + 16, TILE), f32),
            pltpu.VMEM((2, HALO, ny, nz), jnp.int32),
            pltpu.VMEM((2, nx, 8, nz), jnp.int32),
            pltpu.VMEM((2, nx, 8, nz), f32),
            pltpu.SemaphoreType.DMA((3,)),
            pltpu.SemaphoreType.DMA((8,)),
        ],
        compiler_params=pltpu.CompilerParams(vmem_limit_bytes=60 << 20),
        name="pack",
    )(dest, block, pos, flag, divergence)


def splat(arrived, nx, ny, nz):
    vmem, _, _ = specs()
    records = arrived.shape[0]
    strip = jax.ShapeDtypeStruct((HALO, ny, nz), f32)
    edge = jax.ShapeDtypeStruct((nx, HALO, nz), f32)
    return pl.pallas_call(
        splat_kernel,
        out_shape=(
            jax.ShapeDtypeStruct((nx * 2 * ny, 128), f32),
            strip,
            strip,
            edge,
            edge,
        ),
        in_specs=[vmem, vmem],
        out_specs=(vmem,) * 5,
        scratch_shapes=[
            pltpu.SMEM((16, 128), jnp.int32),
            pltpu.SemaphoreType.DMA,
            pltpu.VMEM((16, 128), jnp.int32),
            pltpu.VMEM((1, records), f32),
            pltpu.VMEM((9, records, TILE), f32),
            pltpu.VMEM((8, 128, TILE), f32),
            pltpu.VMEM((TILE * 8 + 8, 128), f32),
            pltpu.VMEM((TILE * 8 + 8, 128), f32),
            pltpu.VMEM((TILE * 8 + 8, 128), f32),
            pltpu.VMEM((TILE * BLOCK, 8, 128), f32),
            pltpu.VMEM((BLOCK * BLOCK * 8 + 8, 128), f32),
        ],
        compiler_params=pltpu.CompilerParams(vmem_limit_bytes=28 << 20),
        name="splat",
    )(spread_matrix(), arrived)


def edges_kernel(left_ref, right_ref, lx1_ref, lx2_ref, ix1_ref, ix2_ref, out1_ref, out2_ref):
    nx, H = left_ref.shape[0:2]
    ny = lx1_ref.shape[1]
    side = lax.axis_index("gx") % 2
    even = lax.axis_index("gy") % 2 == 0
    ext = nx + 2 * H
    low = slice(0, H)
    high = slice(ny - H, ny)
    for turn, out in ((True, out1_ref), (False, out2_ref)):
        up = even if turn else jnp.logical_not(even)
        out[H : nx + H] = jnp.where(up, right_ref[...], left_ref[...])
        for at, step, one, two in (
            (0, nx + H, lx1_ref, lx2_ref),
            (ext, H, ix1_ref.at[0], ix2_ref.at[0]),
            (ext + 2 * H, H, ix1_ref.at[1], ix2_ref.at[1]),
        ):
            out[pl.ds(at + (1 - side) * step, H)] = jnp.where(up, one[:, high, :], one[:, low, :])
            out[pl.ds(at + side * step, H)] = jnp.where(up, two[:, high, :], two[:, low, :])


def edges(left, right, lx1, lx2, ix1, ix2):
    vmem, _, _ = specs()
    nx, H, nz = left.shape
    out = jax.ShapeDtypeStruct((nx + 6 * H, H, nz), f32)
    return pl.pallas_call(
        edges_kernel,
        out_shape=(out, out),
        in_specs=[vmem] * 6,
        out_specs=(vmem, vmem),
        compiler_params=pltpu.CompilerParams(vmem_limit_bytes=16 << 20),
        name="edges",
    )(left, right, lx1, lx2, ix1, ix2)


def around(ref, x, r0, rows):
    at = slice(r0, r0 + rows)
    pair = [ref[x, h, at, :] for h in range(2)]
    z = along(pair)
    totals = []
    for h in range(2):
        total = z[h][0] + z[h][1]
        total = total + (ref[x - 1, h, at, :] + ref[x + 1, h, at, :])
        total = total + (ref[x, h, r0 - 1 : r0 - 1 + rows, :] + ref[x, h, r0 + 1 : r0 + 1 + rows, :])
        totals.append(total)
    return pair, totals


def second_sweep(p_ref, c, x, r0, rows):
    own, total = around(p_ref, x, r0, rows)
    return [own[h] * (4.0 / 3.0) + c[h] * total[h] for h in range(2)]


def later_sweep(ref, p, c, x, r0, rows):
    own, total = around(ref, x, r0, rows)
    return [own[h] * (1.0 / 3.0) + p[h] + c[h] * total[h] for h in range(2)]


def middle_kernel(c_ref, p_ref, out_ref, q_ref, r_ref):
    nx, _, ny, _ = c_ref.shape
    R = ROWS
    at = slice(R, R + ny)

    def both(ref, x, rows=slice(None)):
        return [ref[x, h, rows, :] for h in range(2)]

    def second(x, carry):
        for h, v in enumerate(second_sweep(p_ref, both(c_ref, x), x, R, ny)):
            q_ref[x, h, at, :] = v
        return carry

    lax.fori_loop(2, nx - 2, second, 0, unroll=7)

    def third(x, carry):
        for h, v in enumerate(later_sweep(q_ref, both(p_ref, x, at), both(c_ref, x), x, R, ny)):
            r_ref[x, h, at, :] = v
        return carry

    lax.fori_loop(3, nx - 3, third, 0, unroll=13)

    def fourth(x, carry):
        for h, v in enumerate(later_sweep(r_ref, both(p_ref, x, at), both(c_ref, x), x, R, ny)):
            out_ref[x, :, h * 128 : h * 128 + 128] = v
        return carry

    lax.fori_loop(4, nx - 4, fourth, 0, unroll=8)


def middle(c, p):
    vmem, _, _ = specs()
    nx, _, ny, lanes = c.shape
    padded = jax.ShapeDtypeStruct(p.shape, f32)
    return pl.pallas_call(
        middle_kernel,
        out_shape=(jax.ShapeDtypeStruct((nx, ny, 2 * lanes), f32), padded, padded),
        in_specs=[vmem, vmem],
        out_specs=(vmem,) * 3,
        compiler_params=pltpu.CompilerParams(vmem_limit_bytes=24 << 20),
        name="middle",
    )(c, p)


def jacobi_kernel(result_in, size_ref, kind_ref, div_ref, c_in, p_in, q_in, r_in, lx1_ref, lx2_ref, ix1_ref, ix2_ref,
                  ly1_ref, ly2_ref, iy1_ref, iy2_ref, out_ref,
                  a_ref, u_ref, d_ref, c_ref, p_ref, q_ref, r_ref, slab_ref, tile_ref, sem, out_sem):
    nx, _, ny, _ = size_ref.shape
    H = HALO
    R = ROWS
    S = H + 1
    side = lax.axis_index("gx") % 2
    inner = pl.ds(R, ny)
    first_x, second_x = pl.ds((1 - side) * (nx + H), H), pl.ds(side * (nx + H), H)
    copies = []

    def copy(source, target, n, half):
        copies.append(pltpu.make_async_copy(source, target, sem.at[n, half]))
        copies[-1].start()

    shell = ((0, S, 0, ny), (nx - S, S, 0, ny), (S, nx - 2 * S, 0, 8), (S, nx - 2 * S, ny - 8, 8))
    for n, (x, planes, y, rows) in enumerate(shell):
        xs, ys, padded = pl.ds(x, planes), pl.ds(y, rows), pl.ds(y + R, rows)
        at = pl.ds(x + H, planes)
        copy(size_ref.at[xs, :, ys], a_ref.at[at, :, padded], n, 0)
        copy(kind_ref.at[xs, :, ys], u_ref.at[at, :, padded], n, 1)
        for half in range(2):
            copy(div_ref.at[xs, ys, pl.ds(half * 128, 128)], d_ref.at[at, half, padded], 4 + n, half)
        copy(c_in.at[xs, :, ys], c_ref.at[at, :, padded], 8 + n, 0)
        copy(p_in.at[xs, :, padded], p_ref.at[at, :, padded], 8 + n, 1)
    for half in range(2):
        lanes = pl.ds(half * 128, 128)
        for n, (source, target) in enumerate(
            (
                (ix1_ref.at[0], u_ref.at[first_x, half, inner]),
                (ix2_ref.at[0], u_ref.at[second_x, half, inner]),
                (ix1_ref.at[1], d_ref.at[first_x, half, inner]),
                (ix2_ref.at[1], d_ref.at[second_x, half, inner]),
                (lx1_ref, a_ref.at[first_x, half, inner]),
                (lx2_ref, a_ref.at[second_x, half, inner]),
            )
        ):
            copy(source.at[:, :, lanes], target, 16 + n, half)
    ready = len(copies)
    for m, (source, target) in enumerate(((q_in, q_ref), (r_in, r_ref))):
        for n, (x, planes, y, rows) in enumerate(shell):
            xs, padded, at = pl.ds(x, planes), pl.ds(y + R, rows), pl.ds(x + H, planes)
            copy(source.at[xs, :, padded], target.at[at, :, padded], 12 + n, m)
    mid = pl.ds(H, nx - 2 * H)
    copy(result_in.at[mid, pl.ds(0, 8)], tile_ref.at[0], 22, 0)
    copy(result_in.at[mid, pl.ds(ny - 8, 8)], tile_ref.at[1], 22, 1)
    for half in range(2):
        lanes = slice(half * 128, half * 128 + 128)
        for turn, rows in ((1, slice(R - H, R)), (0, slice(R + ny, R + ny + H))):
            first = lax.axis_index("gy") % 2 == turn
            a_ref[:, half, rows, :] = jnp.where(first, ly1_ref[0 : nx + 2 * H, :, lanes], ly2_ref[0 : nx + 2 * H, :, lanes])
            for n, ext in enumerate((u_ref, d_ref)):
                at = nx + 2 * H + n * 2 * H
                corner = jnp.where(first, ly1_ref[at : at + 2 * H, :, lanes], ly2_ref[at : at + 2 * H, :, lanes])
                ext[0:H, half, rows, :] = corner[0:H]
                ext[nx + H : nx + 2 * H, half, rows, :] = corner[H : 2 * H]
                ext[H : nx + H, half, rows, :] = jnp.where(first, iy1_ref[n, :, :, lanes], iy2_ref[n, :, :, lanes])
    for one in copies[:ready]:
        one.wait()

    def over_shell(first, body):
        last = nx + 2 * H - first - H

        def planes(i, carry):
            body(first + i, R - H, ny + 2 * H)
            body(last + i, R - H, ny + 2 * H)
            return carry

        def sides(x, carry):
            body(x, R - H, 8)
            body(x, R + ny - H, 8)
            return carry

        lax.fori_loop(0, H, planes, 0, unroll=4)
        lax.fori_loop(first + H, last, sides, 0, unroll=8)

    def both(ref, x, r0, rows):
        return [ref[x, h, r0 : r0 + rows, :] for h in range(2)]

    def weigh(x, r0, rows):
        at = slice(r0, r0 + rows)
        for half, c in enumerate(coefficients(a_ref, u_ref, x, r0, rows)):
            c_ref[x, half, at, :] = c
            p_ref[x, half, at, :] = c * d_ref[x, half, at, :]

    def second(x, r0, rows):
        for h, v in enumerate(second_sweep(p_ref, both(c_ref, x, r0, rows), x, r0, rows)):
            q_ref[x, h, r0 : r0 + rows, :] = v

    def third(x, r0, rows):
        for h, v in enumerate(later_sweep(q_ref, both(p_ref, x, r0, rows), both(c_ref, x, r0, rows), x, r0, rows)):
            r_ref[x, h, r0 : r0 + rows, :] = v

    over_shell(1, weigh)
    for one in copies[ready:]:
        one.wait()
    over_shell(2, second)
    over_shell(3, third)

    def last(x, r0, rows):
        return later_sweep(r_ref, both(p_ref, x, r0, rows), both(c_ref, x, r0, rows), x, r0, rows)

    def planes(i, carry):
        for n, x in enumerate((H + i, nx + i)):
            for h, v in enumerate(last(x, R, ny)):
                slab_ref[n, i, :, h * 128 : h * 128 + 128] = v
        return carry

    lax.fori_loop(0, H, planes, 0, unroll=4)
    outs = [
        pltpu.make_async_copy(slab_ref.at[n], out_ref.at[pl.ds(x, H)], out_sem.at[n]) for n, x in enumerate((0, nx - H))
    ]
    for one in outs:
        one.start()

    def sides(x, carry):
        for h, v in enumerate(last(x, R - H, 8)):
            tile_ref[0, x - 2 * H, 0:H, h * 128 : h * 128 + 128] = v[H:8]
        for h, v in enumerate(last(x, R + ny - H, 8)):
            tile_ref[1, x - 2 * H, 8 - H : 8, h * 128 : h * 128 + 128] = v[0:H]
        return carry

    lax.fori_loop(2 * H, nx, sides, 0, unroll=8)
    for n, y in enumerate((0, ny - 8)):
        outs.append(pltpu.make_async_copy(tile_ref.at[n], out_ref.at[mid, pl.ds(y, 8)], out_sem.at[2 + n]))
        outs[-1].start()
    for one in outs:
        one.wait()


def jacobi(result, parts, halo):
    vmem, hbm, _ = specs()
    nx, ny, nz = result.shape
    ext = (nx + 2 * HALO, 2, ny + 2 * ROWS, 128)
    return pl.pallas_call(
        jacobi_kernel,
        out_shape=jax.ShapeDtypeStruct((nx, ny, nz), f32),
        in_specs=[hbm] * 12 + [vmem] * 4,
        out_specs=hbm,
        input_output_aliases={0: 0},
        scratch_shapes=[pltpu.VMEM(ext, f32)] * 7
        + [
            pltpu.VMEM((2, HALO, ny, nz), f32),
            pltpu.VMEM((2, nx - 2 * HALO, 8, nz), f32),
            pltpu.SemaphoreType.DMA((23, 2)),
            pltpu.SemaphoreType.DMA((4,)),
        ],
        compiler_params=pltpu.CompilerParams(vmem_limit_bytes=32 << 20),
        name="jacobi",
    )(result, *parts, *halo)


def spread_matrix():
    row = jnp.arange(128)
    coord, tile = row // 8 % 3, row % 8
    column = jnp.arange(384)
    hit = (row[:, None] < 72) & (coord[:, None] == column[None, :] // 128)
    hit = hit & (tile[:, None] == column[None, :] % 128 // 16)
    return hit.astype(jnp.bfloat16)


def swap(axis, first, second):
    count = lax.axis_size(axis)
    arrived = []
    for part, start in ((first, 0), (second, 1)):
        pairs = []
        for i in range(start, count - 1, 2):
            pairs += [(i, i + 1), (i + 1, i)]
        arrived.append(lax.ppermute(part, axis, pairs))
    return arrived


def per_device(particle_pos, tile_dest, tile_block, fluid_flag, divergence):
    nx, ny, nz = divergence.shape
    bricks = lax.axis_size("gx") * lax.axis_size("gy")
    flag, div = fluid_flag, divergence
    send, first, second, face1, face2 = pack(tile_dest[:, 0], tile_block, particle_pos, flag, div, bricks)
    arrived = lax.all_to_all(send, ("gx", "gy"), split_axis=0, concat_axis=0, tiled=True)
    ix1, ix2 = swap("gx", first, second)
    iy1, iy2 = swap("gy", face1, face2)
    arrived, iy1, iy2 = lax.optimization_barrier((arrived, iy1, iy2))
    near, first, second, left, right = splat(arrived, nx, ny, nz)
    lx1, lx2 = swap("gx", first, second)
    level, sizes, kinds, c, p = interior(near, flag, div)
    lx1, lx2, c = lax.optimization_barrier((lx1, lx2, c))
    ly1, ly2 = swap("gy", *edges(left, right, lx1, lx2, ix1, ix2))
    result, q, r = middle(c, p)
    pressure = jacobi(result, (sizes, kinds, div, c, p, q, r), (lx1, lx2, ix1, ix2, ly1, ly2, iy1, iy2))
    return (level, pressure)


def solution(mesh):
    placed = (
        P(None, ("gx", "gy")),
        P(("gx", "gy"), None),
        P(("gx", "gy")),
        P("gx", "gy", None),
        P("gx", "gy", None),
    )
    return jax.shard_map(
        per_device,
        mesh=mesh,
        in_specs=placed,
        out_specs=(P("gx", "gy", None), P("gx", "gy", None)),
        check_vma=False,
    )
```
